128 devices in a mesh: row: 32 (over y, z, core), col: 4 (over x).
Axes of the slice: x: 4, y: 4, z: 4, core: 2. Of those that a mesh axis runs over, the one named last changes fastest.
Arguments:
- adjoint: float32 [32, 32, 8, 8, 4, 256], P(None, 'row', None, None, 'col'), may hold values from -6 to 6
- lower_panels: float32 [2, 8, 4, 32, 8, 256], P(None, None, 'col', 'row'), may hold values from -0.16 to 2, as said below
- diag_inverse: float32 [2, 256, 256], replicated, may hold values from -0.16 to 1.5, as said below
Outputs:
- symmetric_adjoint: float32 [32, 32, 8, 8, 4, 256], P(None, 'row', None, None, 'col')
The draws below stay inside these ranges and needn't reach their ends.
Inputs may be any that keep to these rules, and one draw needn't show every extreme that they name: `lower_panels`: row blocks of panel k before block k are zero; its block k is lower triangular with diagonal entries between 1 and 2. `diag_inverse`: each matrix is lower triangular with diagonal entries between 0.5 and 1.5.
All inputs are finite; a program needn't handle non-finite values.
Results may differ from the reference program's by a relative error of at most 0.00011.
Values sent between devices are 32-bit elements; how exact they have to be, the bound alone decides.
No kernel may reach another device: no remote copies, remote signals or barrier semaphores. Data moves between devices by JAX's collectives and lax.ppermute only.
A program may use at most 192 MiB of HBM per device.

```python
import math
import jax
import jax.numpy as jnp
from jax import lax

BLK = 256
LOC_C = 8
RSUB = 8
NBLK = 32
ORDER = 8192
N_ROW = 32
N_COL = 4


def draw_lower_panels(key, part):
    key = jax.random.fold_in(key, 11)
    spread_key, diagonal_key = jax.random.split(key, 2)
    spread = jax.random.uniform(spread_key, (2, ORDER, BLK), jnp.float32, -1.0, 1.0)
    diagonal = jax.random.uniform(diagonal_key, (2, ORDER, BLK), jnp.float32, 1.0, 2.0)
    within = (jnp.arange(ORDER) % BLK)[:, None]
    column = jnp.arange(BLK)[None, :]
    block_value = jnp.where(within == column, diagonal, jnp.where(within > column, spread * (0.5 * math.sqrt(3.0 / BLK)), 0.0))
    below_value = spread * math.sqrt(3.0 / ORDER)
    block_of_row = (jnp.arange(ORDER) // BLK)[None, :, None]
    panel_index = jnp.arange(2)[:, None, None]
    values = jnp.where(block_of_row > panel_index, below_value, jnp.where(block_of_row == panel_index, block_value, 0.0))
    return values.reshape(2, LOC_C, N_COL, N_ROW, RSUB, BLK)


def draw_diag_inverse(key, part):
    key = jax.random.fold_in(key, 23)
    spread_key, diagonal_key = jax.random.split(key, 2)
    spread = jax.random.uniform(spread_key, (2, BLK, BLK), jnp.float32, -1.0, 1.0)
    diagonal = jax.random.uniform(diagonal_key, (2, BLK, BLK), jnp.float32, 0.5, 1.5)
    within = jnp.arange(BLK)[:, None]
    column = jnp.arange(BLK)[None, :]
    return jnp.where(within == column, diagonal, jnp.where(within > column, spread * (0.5 * math.sqrt(3.0 / BLK)), 0.0))


def shard_levels(stream_key, extent, pieces, smallest, high):
    def one(position, parts):
        steps = jax.random.uniform(jax.random.fold_in(jax.random.fold_in(stream_key, 6), position), (parts,), jnp.float32, smallest / len(pieces), high / len(pieces))
        return jnp.repeat(jnp.exp(steps), extent[position] // parts).reshape((-1,) + (1,) * (len(extent) - position - 1))

    level = one(*pieces[0])
    for cut in pieces[1:]:
        level = level * one(*cut)
    return level


def noise(rng, shape, scale, limit, cuts=(), kind=jnp.bfloat16):
    values = jax.random.normal(rng, shape, jnp.float32) * scale
    if len(cuts) > 0:
        values = shard_levels(rng, shape, cuts, -0.22, 0.18) * values
    return jnp.clip(values, min=-limit, max=limit).astype(kind)


def setup_inputs(seed: int = 0) -> dict:
    seeds = jax.random.split(jax.random.key(seed), 4)
    return {
        "adjoint": noise(seeds[0], (NBLK, N_ROW, RSUB, LOC_C, N_COL, BLK), 1.0, 6.0, ((1, 32), (4, 4)), jnp.float32),
        "lower_panels": draw_lower_panels(jax.random.fold_in(seeds[3], 71), 0),
        "diag_inverse": draw_diag_inverse(jax.random.fold_in(seeds[3], 71), 0),
    }


highest = lax.Precision.HIGHEST


def matmul_high(left_side, right_side):
    return jnp.dot(left_side, right_side, precision=highest, preferred_element_type=jnp.float32)


def halve_lower(square):
    size = square.shape[0]
    return jnp.tril(square) - 0.5 * square * jnp.eye(size, dtype=jnp.float32)


def reference(adjoint, lower_panels, diag_inverse):
    matrix = adjoint.reshape(ORDER, ORDER)
    panels = lower_panels.reshape(2, ORDER, BLK)
    for panel in (1, 0):
        lower_edge = panel * BLK
        upper_edge = lower_edge + BLK
        factor = panels[panel]
        inverse = diag_inverse[panel]
        trailing = factor[upper_edge:]
        window = matrix[upper_edge:, upper_edge:]
        image = matmul_high(window, trailing) + matmul_high(trailing.T, window).T
        scaled = matmul_high(matrix[upper_edge:, lower_edge:upper_edge] - image, inverse)
        square = matrix[lower_edge:upper_edge, lower_edge:upper_edge] - matmul_high(trailing.T, scaled)
        inner = halve_lower(matmul_high(factor[lower_edge:upper_edge].T, jnp.tril(square)))
        corner = matmul_high(matmul_high(inverse.T, inner), inverse)
        matrix = matrix.at[upper_edge:, lower_edge:upper_edge].set(scaled)
        matrix = matrix.at[lower_edge:upper_edge, lower_edge:upper_edge].set(corner)
    result = 0.5 * (matrix + matrix.T)
    return result.reshape(adjoint.shape)
```

```python
import functools

import jax
import jax.numpy as jnp
from jax import lax
from jax.experimental import pallas as pl
from jax.experimental.pallas import tpu as pltpu
from jax.sharding import PartitionSpec as P

BLK = 256
RSUB = 8
LOC_C = 8
N_ROW = 32
N_COL = 4
NBLK = 32
ROWS = NBLK * RSUB
COLS = LOC_C * BLK
LINES = ROWS * COLS // 128
HIGH = lax.Precision.HIGH
VMEM_LIMIT = 48 * 1024 * 1024


def mm(left, right):
    return jnp.dot(left, right, precision=HIGH, preferred_element_type=jnp.float32)


def mmt(left, right):
    return lax.dot_general(
        left, right, (((0,), (0,)), ((), ())), precision=HIGH, preferred_element_type=jnp.float32
    )


def phi(square):
    size = square.shape[0]
    return jnp.tril(square) - 0.5 * square * jnp.eye(size, dtype=jnp.float32)


def pack_kernel(lines_ref, out_ref, matrix_ref, turned_ref):
    def first(index, carry):
        group = index // 2
        half = index % 2
        for high in range(2):
            tiles = []
            for col in range(N_COL):
                for low in range(4):
                    block = 4 * (4 * high + low) + col
                    tile = lines_ref[pl.ds(block * 128 + index, 8, stride=16), :]
                    matrix_ref[pl.ds(block * 8, 8), pl.ds(pl.multiple_of(index * 128, 128), 128)] = tile
                    tiles.append(tile)
            turned = jnp.concatenate(tiles, axis=0).T
            turned_ref[high, group, pl.ds(half * 128, 128), :] = turned
        return carry

    lax.fori_loop(0, 16, first, 0)

    def second(row, carry):
        tiles = [
            turned_ref[high, group, pl.ds(row * 8, 8), :]
            for high in range(2)
            for group in range(LOC_C)
        ]
        out_ref[pl.ds(row * 128, 128), :] = jnp.concatenate(tiles, axis=0).T
        return carry

    lax.fori_loop(0, N_ROW, second, 0)


def pack(lines):
    return pl.pallas_call(
        pack_kernel,
        out_shape=(
            jax.ShapeDtypeStruct((LINES, 128), jnp.float32),
            jax.ShapeDtypeStruct((ROWS, COLS), jnp.float32),
        ),
        in_specs=[pl.BlockSpec(memory_space=pltpu.VMEM)],
        out_specs=(pl.BlockSpec(memory_space=pltpu.VMEM), pl.BlockSpec(memory_space=pltpu.VMEM)),
        scratch_shapes=[pltpu.VMEM((2, LOC_C, BLK, 128), jnp.float32)],
        compiler_params=pltpu.CompilerParams(vmem_limit_bytes=VMEM_LIMIT),
    )(lines)


def unpack_kernel(lines_ref, out_ref):
    def turn(index, carry):
        col = index // 4
        low = index % 4
        for half in range(2):
            tiles = [
                lines_ref[pl.ds(((half * 16 + sub) * 4 + col) * 32 + low * 8, 8), :]
                for sub in range(16)
            ]
            turned = jnp.concatenate(tiles, axis=0).T
            for high in range(2):
                for group in range(LOC_C):
                    place = high * 64 + group * 8
                    out_ref[
                        pl.ds((4 * group + col) * 8, 8),
                        pl.ds(pl.multiple_of((4 * high + low) * BLK + half * 128, 128), 128),
                    ] = turned[place : place + 8]
        return carry

    lax.fori_loop(0, 16, turn, 0)


def unpack(lines):
    return pl.pallas_call(
        unpack_kernel,
        out_shape=jax.ShapeDtypeStruct((ROWS, COLS), jnp.float32),
        in_specs=[pl.BlockSpec(memory_space=pltpu.VMEM)],
        out_specs=pl.BlockSpec(memory_space=pltpu.VMEM),
        compiler_params=pltpu.CompilerParams(vmem_limit_bytes=VMEM_LIMIT),
    )(lines)


def finish_kernel(lines_ref, mirror_ref, columns_ref, top_ref, out_ref):
    def one(index, carry):
        lane = pl.multiple_of(index * 128, 128)
        for block in range(NBLK):
            if block < 2:
                other = top_ref[pl.ds(block * 8, 8), pl.ds(lane, 128)]
            else:
                other = mirror_ref[pl.ds(block * 8, 8), pl.ds(lane, 128)]
            rows = pl.ds(block * 128 + index, 8, stride=16)
            out_ref[rows, :] = 0.5 * (lines_ref[rows, :] + other)
        return carry

    lax.fori_loop(2, 16, one, 0)
    for index in range(2):
        lane = index * 128
        for block in range(NBLK):
            if block < 2:
                other = top_ref[pl.ds(block * 8, 8), pl.ds(lane, 128)]
            else:
                other = mirror_ref[pl.ds(block * 8, 8), pl.ds(lane, 128)]
            rows = pl.ds(block * 128 + index, 8, stride=16)
            out_ref[rows, :] = 0.5 * (columns_ref[pl.ds(block * 8, 8), pl.ds(lane, 128)] + other)


def finish(lines, mirror, columns, top):
    return pl.pallas_call(
        finish_kernel,
        out_shape=jax.ShapeDtypeStruct((LINES, 128), jnp.float32),
        in_specs=[pl.BlockSpec(memory_space=pltpu.VMEM)] * 4,
        out_specs=pl.BlockSpec(memory_space=pltpu.VMEM),
        compiler_params=pltpu.CompilerParams(vmem_limit_bytes=VMEM_LIMIT),
    )(lines, mirror, columns, top)


def on_device(adjoint, lower_panels, diag_inverse):
    row_place = lax.axis_index("row")
    col_place = lax.axis_index("col")
    own_zero = col_place == 0
    own_one = col_place == 1
    lines = adjoint.reshape(LINES, 128)
    pieces = lower_panels.reshape(2, LOC_C, 1, RSUB, BLK)
    by_cols = lax.all_gather(pieces, "row", axis=2, tiled=True).reshape(2, COLS, BLK)
    by_rows = lax.all_gather(pieces, "col", axis=2, tiled=True).reshape(2, ROWS, BLK)

    heads = jnp.concatenate([by_rows[1, 8:16], by_rows[0, 8:16], by_rows[0, 0:8]], axis=0)
    heads = heads.reshape(1, 48, 128)
    heads = lax.all_to_all(
        jnp.broadcast_to(heads, (N_ROW, 48, 128)), "row", split_axis=0, concat_axis=0, tiled=True
    )
    heads = heads.reshape(N_ROW, 3, RSUB, BLK).transpose(1, 0, 2, 3).reshape(3, BLK, BLK)
    factor_one, factor_cross, factor_zero = heads[0], heads[1], heads[2]

    outgoing, matrix = pack(lines)
    arrived = lax.all_to_all(
        outgoing.reshape(N_ROW * N_COL, 32, 128), ("row", "col"), split_axis=0, concat_axis=0, tiled=True
    )
    mirror = unpack(arrived.reshape(LINES, 128))

    inverse_one = diag_inverse[1]
    inverse_zero = diag_inverse[0]
    first = matrix[:, :BLK]
    row_block = jnp.arange(ROWS)[:, None] // RSUB
    tail_rows = row_block > 1
    col_head = jnp.arange(COLS)[None, :] < BLK
    keep_direct = ~(col_head & (own_zero | own_one))
    keep_mirror = tail_rows & ~(col_head & own_zero)
    both = jnp.where(keep_direct, matrix, 0.0) + jnp.where(keep_mirror, mirror, 0.0)
    block_head = jnp.arange(COLS)[:, None] < BLK
    right = jnp.concatenate(
        [jnp.where(block_head & own_one, 0.0, by_cols[1]), by_cols[0]], axis=1
    )
    image = mm(both, right)
    rest_one = jnp.where(own_one, first, 0.0) - image[:, :BLK]
    rest_zero = jnp.where(own_zero, first, 0.0) - image[:, BLK:]

    scaled_one = mm(rest_one, inverse_one)
    scaled_zero = mm(rest_zero - mm(scaled_one, factor_cross), inverse_zero)
    chunk = jnp.concatenate([scaled_one, scaled_zero], axis=1)
    chunk = chunk.reshape(LOC_C, N_COL, RSUB, 2 * BLK).transpose(1, 0, 2, 3)
    chunk = chunk.reshape(N_COL, LOC_C * RSUB, 2 * BLK)
    chunk = lax.all_to_all(chunk, "col", split_axis=0, concat_axis=0, tiled=True)
    strip = jnp.sum(chunk, axis=0)

    def spread_rows(part):
        return lax.dynamic_update_slice_in_dim(
            jnp.zeros((BLK, BLK), jnp.float32), part, row_place * RSUB, 0
        )

    tail_one = jnp.where(tail_rows, scaled_one, 0.0)
    tail_zero = jnp.where(tail_rows, scaled_zero, 0.0)
    square_one = spread_rows(jnp.where(own_one, first[8:16], 0.0)) - mmt(by_rows[1], tail_one)
    corner_one = mm(
        mmt(inverse_one, phi(mmt(factor_one, jnp.tril(square_one)))), inverse_one
    )
    corner_one = corner_one + corner_one.T
    cross = spread_rows(rest_zero[8:16]) - mmt(tail_one, by_rows[0]) - mm(corner_one, factor_cross)
    cross = mm(cross, inverse_zero)
    square_zero = (
        spread_rows(jnp.where(own_zero, first[0:8], 0.0))
        - mmt(by_rows[0], tail_zero)
        - mmt(factor_cross, cross)
    )
    corner_zero = mm(
        mmt(inverse_zero, phi(mmt(factor_zero, jnp.tril(square_zero)))), inverse_zero
    )
    corner_zero = corner_zero + corner_zero.T

    corners = jnp.stack([cross, corner_zero, corner_one, cross.T])
    corners = corners.reshape(4, N_ROW, RSUB, BLK).transpose(1, 0, 2, 3).reshape(N_ROW, 64, 128)
    across = strip.reshape(LOC_C * RSUB, 2, N_ROW, RSUB).transpose(2, 1, 3, 0).reshape(N_ROW, 8, 128)
    shared = lax.all_to_all(
        jnp.concatenate([corners, across], axis=1), "row", split_axis=0, concat_axis=0, tiled=True
    )
    corner_rows = jnp.sum(shared[:, :64], axis=0).reshape(2, 16, BLK)
    top = shared[:, 64:].reshape(N_ROW, 2, RSUB, LOC_C, RSUB)
    top = top.transpose(1, 2, 3, 0, 4).reshape(2, RSUB, COLS)

    final = jnp.stack([strip[:, BLK:], strip[:, :BLK]]).reshape(2, 128, 128)
    final = jnp.concatenate([final, corner_rows.reshape(2, 32, 128)], axis=1)
    final = jnp.concatenate([final, jnp.zeros_like(final)], axis=0)
    final = lax.all_to_all(final, "col", split_axis=0, concat_axis=0, tiled=True)
    new_columns = final[:, :128].reshape(N_COL, LOC_C, RSUB, BLK).transpose(1, 0, 2, 3).reshape(ROWS, BLK)
    corner_rows = jnp.sum(final[:, 128:], axis=0).reshape(2, RSUB, BLK)

    head_zero = jnp.where(own_zero, corner_rows[1], first[0:8])
    head_one = jnp.where(own_zero, corner_rows[0], jnp.where(own_one, corner_rows[0], first[8:16]))
    owner = own_zero | own_one
    columns = jnp.concatenate(
        [head_zero, head_one, jnp.where(owner, new_columns[16:], first[16:])], axis=0
    )
    top_zero = top[1]
    top_one = top[0]
    lead_zero = jnp.where(own_zero, 0.0, jnp.where(own_one, corner_rows[1], top_zero[:, :BLK]))
    lead_one = jnp.where(own_zero, mirror[8:16, :BLK], jnp.where(own_one, 0.0, top_one[:, :BLK]))
    top = jnp.concatenate(
        [
            jnp.concatenate([lead_zero, top_zero[:, BLK:]], axis=1),
            jnp.concatenate([lead_one, top_one[:, BLK:]], axis=1),
        ],
        axis=0,
    )
    result = finish(lines, mirror, columns, top)
    return result.reshape(NBLK, 1, RSUB, LOC_C, 1, BLK)


def solution(mesh):
    return jax.shard_map(
        on_device,
        mesh=mesh,
        in_specs=(
            P(None, "row", None, None, "col", None),
            P(None, None, "col", "row", None, None),
            P(),
        ),
        out_specs=P(None, "row", None, None, "col", None),
        check_vma=False,
    )
```

```python
import jax
import jax.numpy as jnp
from jax import lax
from jax.experimental import pallas as pl
from jax.experimental.pallas import tpu as pltpu
from jax.sharding import PartitionSpec as P

BLK = 256
RSUB = 8
LOC_C = 8
N_ROW = 32
N_COL = 4
NBLK = 32
ROWS = NBLK * RSUB
COLS = LOC_C * BLK
LINES = ROWS * COLS // 128
STRIP = LOC_C * RSUB
PIECE = STRIP + 3 * RSUB
RING = (0, 1, 3, 2)
F32 = jnp.float32
BF16 = jnp.bfloat16
VMEM_LIMIT = 48 * 1024 * 1024
VMEM = pl.BlockSpec(memory_space=pltpu.VMEM)
SMEM = pl.BlockSpec(memory_space=pltpu.SMEM)


def shape(*dims):
    return jax.ShapeDtypeStruct(dims, F32)


def call(kernel, outs, ins, scratch=(), flops=0, size=0):
    return pl.pallas_call(
        kernel,
        out_shape=outs,
        in_specs=ins,
        out_specs=jax.tree.map(lambda _: VMEM, outs),
        scratch_shapes=scratch,
        compiler_params=pltpu.CompilerParams(vmem_limit_bytes=VMEM_LIMIT),
        cost_estimate=pl.CostEstimate(flops=flops, bytes_accessed=size, transcendentals=0),
    )


def split(value):
    high = value.astype(BF16)
    return high, (value - high.astype(F32)).astype(BF16)


def dot3(left, right, dims=((1,), (0,))):
    left_high, left_low = split(left)
    right_high, right_low = split(right)

    def one(a, b):
        return lax.dot_general(a, b, (dims, ((), ())), preferred_element_type=F32)

    return one(left_high, right_high) + (one(left_high, right_low) + one(left_low, right_high))


def dot3t(left, right):
    return dot3(left.T, right)


def swap_groups(tiles):
    tiles = list(tiles)
    group = lax.broadcasted_iota(jnp.int32, (8, 128), 1) // 8
    for bit in (1, 2, 4, 8):
        keep = (group & bit) == 0
        for i in range(16):
            if i & bit:
                continue
            a, b = tiles[i], tiles[i | bit]
            tiles[i] = jnp.where(keep, a, pltpu.roll(b, 8 * bit, 1))
            tiles[i | bit] = jnp.where(keep, pltpu.roll(a, 128 - 8 * bit, 1), b)
    return tiles


def pack_kernel(lines_ref, out_ref):
    def one(index, carry):
        col = index // 2
        half = index % 2
        tiles = [
            lines_ref[high, 0, pl.ds(col * 128 + group * 2 + half, 8, stride=16), :]
            for high in range(2)
            for group in range(LOC_C)
        ]
        for sub, tile in enumerate(swap_groups(tiles)):
            out_ref[half * 16 + sub, col, 0] = tile
        return carry

    lax.fori_loop(0, 2 * N_COL, one, 0)


def pack(lines):
    return pl.pallas_call(
        pack_kernel,
        grid=(4,),
        out_shape=shape(N_ROW, N_COL, 4, RSUB, 128),
        in_specs=[pl.BlockSpec((2, 1, 512, 128), lambda i: (0, i, 0, 0))],
        out_specs=pl.BlockSpec((N_ROW, N_COL, 1, RSUB, 128), lambda i: (0, 0, i, 0, 0)),
        compiler_params=pltpu.CompilerParams(vmem_limit_bytes=VMEM_LIMIT),
        cost_estimate=pl.CostEstimate(flops=0, bytes_accessed=16 * 2**20, transcendentals=0),
    )(lines.reshape(2, 4, 512, 128))


def mirror_tiles(lines_ref, col, low, half):
    tiles = [
        lines_ref[pl.ds(((half * 16 + sub) * 4 + col) * 32 + low * 8, 8), :] for sub in range(16)
    ]
    turned = jnp.concatenate(tiles, axis=0).T
    return {
        (high, group): turned[high * 64 + group * 8 : high * 64 + group * 8 + 8]
        for high in range(2)
        for group in range(LOC_C)
    }


def half_kernel(lines_ref, arrived_ref, out_ref):
    def turn(col, carry):
        for low in range(4):
            for half in range(2):
                for (high, group), tile in mirror_tiles(arrived_ref, col, low, half).items():
                    start = (4 * group + col) * 128 + (4 * high + low) * 2 + half
                    rows = pl.ds(start, 8, stride=16)
                    out_ref[rows, :] = 0.5 * (lines_ref[rows, :] + tile)
        return carry

    lax.fori_loop(0, N_COL, turn, 0)


def image_kernel(
    place_ref, lines_ref, arrived_ref, one_ref, *rest
):
    pieces = rest[:8]
    inverse_ref = rest[8]
    chunk_refs = rest[9:13]
    heads_ref, corner_ref, first_ref, both_ref, zero_ref, strips_ref = rest[13:]
    row_y, row_z, core, col_place = (place_ref[i] for i in range(1, 5))
    is_zero = col_place == 0
    is_one = col_place == 1

    def turn(col, carry):
        for low in range(4):
            for half in range(2):
                for (high, group), tile in mirror_tiles(arrived_ref, col, low, half).items():
                    block = 4 * group + col
                    inner = 4 * high + low
                    start = block * 128 + inner * 2 + half
                    own = lines_ref[pl.ds(start, 8, stride=16), :]
                    if group == 0:
                        tile = jnp.where(col < 2, 0.0, tile)
                    rows = pl.ds(block * 8, 8)
                    if inner == 0:
                        first_ref[rows, half * 128 : half * 128 + 128] = own
                        own = jnp.where(is_zero | is_one, 0.0, own)
                        tile = jnp.where(is_zero, 0.0, tile)
                    both_ref[inner, rows, half * 128 : half * 128 + 128] = own + tile
        return carry

    lax.fori_loop(0, N_COL, turn, 0)

    for j in range(4):
        for i in range(4):
            chip = ((row_y - RING[j]) & 3) * 4 + ((row_z - RING[i]) & 3)
            for side in range(2):
                piece = pieces[4 * side + j]
                owner = chip * 2 + (core if side == 0 else 1 - core)
                rows = pl.ds(pl.multiple_of(owner * 8, 8), 8)
                for s in range(LOC_C):
                    zero_ref[s, rows, :] = piece[i * PIECE + s * 8 : i * PIECE + s * 8 + 8, :]
                for head in range(3):
                    start = i * PIECE + STRIP + head * 8
                    heads_ref[head, rows, :] = piece[start : start + 8, :]

    def product(s, carry):
        both = both_ref[s]
        panel_one = one_ref[:, s].reshape(BLK, BLK)
        panel_one = jnp.where(jnp.logical_and(is_one, s == 0), 0.0, panel_one)
        strips_ref[0] += dot3(both, panel_one)
        strips_ref[1] += dot3(both, zero_ref[s])
        return carry

    strips_ref[...] = jnp.zeros_like(strips_ref)
    lax.fori_loop(0, LOC_C, product, 0)
    first = first_ref[...]
    rest_one = jnp.where(is_one, first, 0.0) - strips_ref[0]
    rest_zero = jnp.where(is_zero, first, 0.0) - strips_ref[1]
    corner_ref[0:8, :] = jnp.where(is_one, first[8:16], 0.0)
    corner_ref[8:16, :] = rest_zero[8:16]
    corner_ref[16:24, :] = jnp.where(is_zero, first[0:8], 0.0)
    scaled_one = dot3(rest_one, inverse_ref[1])
    strips_ref[0] = scaled_one
    strips_ref[1] = dot3(rest_zero - dot3(scaled_one, heads_ref[1]), inverse_ref[0])
    for d in range(4):
        kind = (col_place + d) & 3
        for s in range(LOC_C):
            rows = pl.ds(pl.multiple_of((4 * s + kind) * 8, 8), 8)
            for panel in range(2):
                tile = strips_ref[panel, rows, :]
                if s == 0:
                    tile = jnp.where(kind < 2, 0.0, tile)
                chunk_refs[d][s * 8 : s * 8 + 8, panel * BLK : panel * BLK + BLK] = tile


def chain_kernel(place_ref, corner_ref, heads_ref, inverse_ref, *rest):
    chunks = rest[0:4]
    panels = rest[4:8]
    out_ref, left_ref, right_ref, square_ref = rest[8:]
    mine = pl.ds(pl.multiple_of(place_ref[0] * 8, 8), 8)
    for d in range(4):
        rows = slice(d * STRIP, (d + 1) * STRIP)
        left_ref[0, rows, :] = panels[d][0]
        left_ref[1, rows, :] = panels[d][1]
        right_ref[0, rows, :] = chunks[d][:, BLK:]
        right_ref[1, rows, :] = chunks[d][:, :BLK]
    row = lax.broadcasted_iota(jnp.int32, (BLK, BLK), 0)
    column = lax.broadcasted_iota(jnp.int32, (BLK, BLK), 1)

    def lower(value):
        return jnp.where(row >= column, value, 0.0)

    def phi(value):
        return jnp.where(row > column, value, jnp.where(row == column, 0.5 * value, 0.0))

    def spread(square, start):
        square_ref[...] = square
        square_ref[mine, :] += corner_ref[start : start + 8, :]
        return square_ref[...]

    def corner(square, factor, inverse):
        inner = phi(dot3t(factor, lower(square)))
        whole = dot3(dot3t(inverse, inner), inverse)
        return whole + whole.T

    def put(place, value):
        for half in range(2):
            tile = value[:, half * 128 : half * 128 + 128].reshape(N_ROW, RSUB, 128)
            start = (place * 2 + half) * 8
            out_ref[:, start : start + 8, :] = tile

    panel_zero, panel_one = left_ref[0], left_ref[1]
    scaled_zero, scaled_one = right_ref[0], right_ref[1]
    cross_factor = heads_ref[1]
    corner_one = corner(
        spread(-dot3t(panel_one, scaled_one), 0), heads_ref[0], inverse_ref[1]
    )
    put(2, corner_one)
    cross = spread(-(dot3t(scaled_one, panel_zero) + dot3(corner_one, cross_factor)), 8)
    cross = dot3(cross, inverse_ref[0])
    put(0, cross)
    put(3, cross.T)
    corner_zero = corner(
        spread(-(dot3t(panel_zero, scaled_zero) + dot3t(cross_factor, cross)), 16),
        heads_ref[2],
        inverse_ref[0],
    )
    put(1, corner_zero)


def strip_kernel(place_ref, a_ref, b_ref, c_ref, d_ref, across_ref, *out_refs):
    col_place = place_ref[4]
    strip = (a_ref[...] + b_ref[...]) + (c_ref[...] + d_ref[...])
    for d in range(4):
        target = (col_place + d) & 3
        out_refs[d][...] = jnp.where(target == 0, strip[:, BLK:], strip[:, :BLK])
    for half in range(2):
        tiles = [
            strip[s * 8 : s * 8 + 8, k * BLK + half * 128 : k * BLK + half * 128 + 128]
            for s in range(LOC_C)
            for k in range(2)
        ]
        for sub, tile in enumerate(swap_groups(tiles)):
            across_ref[half * 16 + sub] = tile


def total_kernel(place_ref, parts_ref, *out_refs):
    col_place = place_ref[4]
    total = jnp.sum(parts_ref[...], axis=0)
    for d in range(4):
        target = (col_place + d) & 3
        out_refs[d][...] = jnp.where(target == 0, total[:32], total[32:])


def finish_kernel(place_ref, half_ref, lines_ref, first_ref, across_ref, *rest):
    strips = rest[0:4]
    corners = rest[4:8]
    out_ref, top_ref = rest[8:]
    col_place = place_ref[4]
    is_zero = col_place == 0
    is_one = col_place == 1
    owner = col_place < 2
    for half in range(2):
        turned = across_ref[half * 16 : half * 16 + 16].reshape(128, 128).T
        for s in range(LOC_C):
            for k in range(2):
                start = (s * 2 + k) * 8
                top_ref[k, s, half] = turned[start : start + 8]
    out_ref[...] = half_ref[...]
    for s in range(LOC_C):
        for half in range(2):
            for block in range(2):
                rows = pl.ds(block * 128 + s * 2 + half, 8, stride=16)
                new = lines_ref[rows, :] + top_ref[1 - block, s, half]
                if s == 0:
                    continue
                out_ref[rows, :] = 0.5 * new
    for half in range(2):
        lanes = slice(half * 128, half * 128 + 128)
        rows = slice(half * 8, half * 8 + 8)
        late = slice(16 + half * 8, 24 + half * 8)
        part_a = (corners[0][rows] + corners[1][rows]) + (corners[2][rows] + corners[3][rows])
        part_b = (corners[0][late] + corners[1][late]) + (corners[2][late] + corners[3][late])
        zero_rows = pl.ds(half, 8, stride=16)
        own = lines_ref[zero_rows, :]
        out_ref[zero_rows, :] = 0.5 * jnp.where(
            is_zero, part_b, own + jnp.where(is_one, part_b, top_ref[1, 0, half])
        )
        one_rows = pl.ds(128 + half, 8, stride=16)
        own = lines_ref[one_rows, :]
        out_ref[one_rows, :] = jnp.where(
            is_zero,
            half_ref[one_rows, :] + 0.5 * (part_a - own),
            0.5 * jnp.where(is_one, part_a, own + top_ref[0, 0, half]),
        )
        for d in range(4):
            kind = (col_place - d) & 3
            for s in range(LOC_C):
                block = 4 * s + kind
                rows = pl.ds(block * 128 + half, 8, stride=16)
                use = owner if s > 0 else jnp.logical_and(owner, kind > 1)
                change = strips[d][s * 8 : s * 8 + 8, lanes] - first_ref[pl.ds(block * 8, 8), lanes]
                out_ref[rows, :] += jnp.where(use, 0.5 * change, 0.0)


def ring_z(d):
    return [(i, (i & ~6) | ((((i >> 1) + d) & 3) << 1)) for i in range(N_ROW)]


def ring_y(d):
    return [(i, (i & 7) | ((((i >> 3) + d) & 3) << 3)) for i in range(N_ROW)]


def around(piece, ring):
    return [piece] + [lax.ppermute(piece, "row", ring(d)) for d in RING[1:]]


def to_owners(pieces):
    moved = [
        lax.ppermute(pieces[d], "col", [((t - d) % 4, t) for t in range(2)]) for d in range(1, 4)
    ]
    return [pieces[0]] + moved


def on_device(adjoint, lower_panels, diag_inverse):
    row_place = lax.axis_index("row")
    col_place = lax.axis_index("col")
    place = jnp.stack(
        [row_place, row_place >> 3, (row_place >> 1) & 3, row_place & 1, col_place]
    ).astype(jnp.int32)
    lines = adjoint.reshape(LINES, 128)
    panels = lower_panels.reshape(2, STRIP, BLK)
    gathered = lax.all_gather(panels[1], "row", axis=0, tiled=True).reshape(
        N_ROW, LOC_C, RSUB, BLK
    )
    by_rows = [panels] + [
        lax.ppermute(panels, "col", [(i, (i + d) % 4) for i in range(4)]) for d in range(1, 4)
    ]
    lead = jnp.stack([piece[:, :RSUB] for piece in by_rows])
    lead_one = lax.dynamic_index_in_dim(lead, (col_place - 1) & 3, 0, False)
    lead_zero = lax.dynamic_index_in_dim(lead, col_place, 0, False)
    piece = jnp.concatenate([panels[0], lead_one[1], lead_one[0], lead_zero[0]], axis=0)

    outgoing = pack(lines)
    outgoing, piece = lax.optimization_barrier((outgoing, piece))
    arrived = lax.all_to_all(
        outgoing.reshape(N_ROW * N_COL, 32, 128), ("row", "col"), split_axis=0, concat_axis=0, tiled=True
    ).reshape(LINES, 128)
    plane = around(jnp.concatenate(around(piece, ring_z), axis=0), ring_y)
    plane = plane + [lax.ppermute(part, "row", [(i, i ^ 1) for i in range(N_ROW)]) for part in plane]

    *chunks, heads, corner_in, first = call(
        image_kernel,
        [shape(STRIP, 2 * BLK)] * 4 + [shape(3, BLK, BLK), shape(24, BLK), shape(ROWS, BLK)],
        [SMEM] + [VMEM] * 12,
        scratch=[
            pltpu.VMEM((LOC_C, ROWS, BLK), F32),
            pltpu.VMEM((LOC_C, BLK, BLK), F32),
            pltpu.VMEM((2, ROWS, BLK), F32),
        ],
        flops=2**32,
        size=2**24,
    )(place, lines, arrived, gathered, *plane, diag_inverse)
    strips = [chunks[0]] + [
        lax.ppermute(chunks[d], "col", [(i, (i + d) % 4) for i in range(4)]) for d in range(1, 4)
    ]
    corners = call(
        chain_kernel,
        shape(N_ROW, 64, 128),
        [SMEM] + [VMEM] * 11,
        scratch=[
            pltpu.VMEM((2, ROWS, BLK), F32),
            pltpu.VMEM((2, ROWS, BLK), F32),
            pltpu.VMEM((BLK, BLK), F32),
        ],
        flops=2**32,
        size=2**23,
    )(
        place, corner_in, heads, diag_inverse, *chunks,
        by_rows[0], by_rows[3], by_rows[2], by_rows[1],
    )
    corners = lax.all_to_all(corners, "row", split_axis=0, concat_axis=0, tiled=True)
    across, *strips = call(
        strip_kernel,
        [shape(N_ROW, RSUB, 128)] + [shape(STRIP, BLK)] * 4,
        [SMEM] + [VMEM] * 4,
        size=2**21,
    )(place, *strips)
    across = lax.all_to_all(across, "row", split_axis=0, concat_axis=0, tiled=True)
    strips = to_owners(strips)
    half = call(
        half_kernel, shape(LINES, 128), [VMEM, VMEM], size=2**24
    )(lines, arrived)
    corners = to_owners(
        call(total_kernel, [shape(32, 128)] * 4, [SMEM, VMEM], size=2**21)(place, corners)
    )
    result = call(
        finish_kernel,
        shape(LINES, 128),
        [SMEM] + [VMEM] * 12,
        scratch=[pltpu.VMEM((2, LOC_C, 2, RSUB, 128), F32)],
        size=2**23,
    )(place, half, lines[:BLK], first, across, *strips, *corners)
    return result.reshape(NBLK, 1, RSUB, LOC_C, 1, BLK)


def solution(mesh):
    return jax.shard_map(
        on_device,
        mesh=mesh,
        in_specs=(
            P(None, "row", None, None, "col", None),
            P(None, None, "col", "row", None, None),
            P(),
        ),
        out_specs=P(None, "row", None, None, "col", None),
        check_vma=False,
    )
```

```python
import jax
import jax.numpy as jnp
from jax import lax
from jax.experimental import pallas as pl
from jax.experimental.pallas import tpu as pltpu
from jax.sharding import PartitionSpec as P

BLK = 256
RSUB = 8
LOC_C = 8
N_ROW = 32
N_COL = 4
NBLK = 32
ROWS = NBLK * RSUB
COLS = LOC_C * BLK
LINES = ROWS * COLS // 128
STRIP = LOC_C * RSUB
PIECE = 2 * STRIP + 3 * RSUB
RING = (0, 1, 3, 2)
F32 = jnp.float32
BF16 = jnp.bfloat16
VMEM_LIMIT = 56 * 1024 * 1024
SMEM = pl.BlockSpec(memory_space=pltpu.SMEM)


def shape(*dims):
    return jax.ShapeDtypeStruct(dims, F32)


def call(body, outs, ins, scratch=(), flops=0, size=0):
    count, results = len(ins), len(outs)

    def kernel(*refs):
        place, sources = refs[0], refs[1 : 1 + count]
        targets = refs[1 + count : 1 + count + results]
        staged = refs[1 + count + results : 1 + 2 * count + results]
        made = refs[1 + 2 * count + results : 1 + 2 * count + 2 * results]
        extra = refs[1 + 2 * count + 2 * results : -2]
        in_sem, out_sem = refs[-2:]
        copies = [
            pltpu.make_async_copy(sources[i], staged[i], in_sem.at[i]) for i in range(count)
        ]
        leaving = [
            pltpu.make_async_copy(made[i], targets[i], out_sem.at[i]) for i in range(results)
        ]
        for copy in copies:
            copy.start()
        body(
            place,
            staged,
            lambda *which: [copies[i].wait() for i in which],
            made,
            lambda *which: [leaving[i].start() for i in which],
            *extra,
        )
        for copy in leaving:
            copy.wait()

    anywhere = pl.BlockSpec(memory_space=pl.ANY)
    return pl.pallas_call(
        kernel,
        out_shape=list(outs),
        in_specs=[SMEM] + [anywhere] * count,
        out_specs=[anywhere] * results,
        scratch_shapes=[pltpu.VMEM(x.shape, F32) for x in ins]
        + [pltpu.VMEM(x.shape, F32) for x in outs]
        + list(scratch)
        + [pltpu.SemaphoreType.DMA((count,)), pltpu.SemaphoreType.DMA((results,))],
        compiler_params=pltpu.CompilerParams(vmem_limit_bytes=VMEM_LIMIT),
        cost_estimate=pl.CostEstimate(flops=flops, bytes_accessed=size, transcendentals=0),
    )


def split(value):
    high = value.astype(BF16)
    return high, (value - high.astype(F32)).astype(BF16)


def dot3(left, right, dims=((1,), (0,))):
    left_high, left_low = split(left)
    right_high, right_low = split(right)

    def one(a, b):
        return lax.dot_general(a, b, (dims, ((), ())), preferred_element_type=F32)

    return one(left_high, right_high) + (one(left_high, right_low) + one(left_low, right_high))


def dot3t(left, right):
    return dot3(left.T, right)


def swap_groups(tiles):
    tiles = list(tiles)
    group = lax.broadcasted_iota(jnp.int32, (8, 128), 1) // 8
    for bit in (1, 2, 4, 8):
        keep = (group & bit) == 0
        for i in range(16):
            if i & bit:
                continue
            a, b = tiles[i], tiles[i | bit]
            tiles[i] = jnp.where(keep, a, pltpu.roll(b, 8 * bit, 1))
            tiles[i | bit] = jnp.where(keep, pltpu.roll(a, 128 - 8 * bit, 1), b)
    return tiles


def pack_body(place_ref, staged, wait, made, flush, turned_ref):
    (lines_ref,), (out_ref,) = staged, made
    wait(0)

    def first(index, carry):
        group = index // 2
        half = index % 2
        for high in range(2):
            tiles = [
                lines_ref[pl.ds((4 * (4 * high + low) + col) * 128 + index, 8, stride=16), :]
                for col in range(N_COL)
                for low in range(4)
            ]
            turned_ref[high, group, pl.ds(half * 128, 128), :] = jnp.concatenate(tiles, axis=0).T
        return carry

    lax.fori_loop(0, 16, first, 0)

    def second(row, carry):
        tiles = [
            turned_ref[high, group, pl.ds(row * 8, 8), :]
            for high in range(2)
            for group in range(LOC_C)
        ]
        out_ref[pl.ds(row * 128, 128), :] = jnp.concatenate(tiles, axis=0).T
        return carry

    lax.fori_loop(0, N_ROW, second, 0)
    flush(0)


def mirror_tiles(lines_ref, col, low, half):
    tiles = [
        lines_ref[pl.ds(((half * 16 + sub) * 4 + col) * 32 + low * 8, 8), :] for sub in range(16)
    ]
    turned = jnp.concatenate(tiles, axis=0).T
    return {
        (high, group): turned[high * 64 + group * 8 : high * 64 + group * 8 + 8]
        for high in range(2)
        for group in range(LOC_C)
    }


def half_body(place_ref, staged, wait, made, flush):
    lines_ref, arrived_ref = staged
    (out_ref,) = made
    wait(0, 1)
    def turn(col, carry):
        for low in range(4):
            for half in range(2):
                for (high, group), tile in mirror_tiles(arrived_ref, col, low, half).items():
                    start = (4 * group + col) * 128 + (4 * high + low) * 2 + half
                    rows = pl.ds(start, 8, stride=16)
                    out_ref[rows, :] = 0.5 * (lines_ref[rows, :] + tile)
        return carry

    lax.fori_loop(0, N_COL, turn, 0)
    flush(0)


def image_body(
    place_ref, staged, wait, made, flush, both_ref, one_ref, zero_ref, strips_ref
):
    lines_ref, arrived_ref, *pieces, inverse_ref = staged
    *chunk_refs, heads_ref, corner_ref, first_ref = made
    wait(0, 1)
    row_y, row_z, core, col_place = (place_ref[i] for i in range(1, 5))
    is_zero = col_place == 0
    is_one = col_place == 1

    def turn(col, carry):
        for low in range(4):
            for half in range(2):
                for (high, group), tile in mirror_tiles(arrived_ref, col, low, half).items():
                    block = 4 * group + col
                    inner = 4 * high + low
                    start = block * 128 + inner * 2 + half
                    own = lines_ref[pl.ds(start, 8, stride=16), :]
                    if group == 0:
                        tile = jnp.where(col < 2, 0.0, tile)
                    rows = pl.ds(block * 8, 8)
                    if inner == 0:
                        first_ref[rows, half * 128 : half * 128 + 128] = own
                        own = jnp.where(is_zero | is_one, 0.0, own)
                        tile = jnp.where(is_zero, 0.0, tile)
                    both_ref[inner, rows, half * 128 : half * 128 + 128] = own + tile
        return carry

    lax.fori_loop(0, N_COL, turn, 0)

    flush(6)
    wait(*range(2, 10))
    for side in range(2):
        moved = core if side == 0 else 1 - core
        for j in range(4):
            for i in range(4):
                place_y = (row_y - jnp.where(moved == 0, RING[j], RING[i])) & 3
                place_z = (row_z - jnp.where(moved == 0, RING[i], RING[j])) & 3
                owner = (place_y * 4 + place_z) * 2 + moved
                rows = pl.ds(pl.multiple_of(owner * 8, 8), 8)
                piece = pieces[4 * side + j]
                for s in range(LOC_C):
                    start = i * PIECE + s * 8
                    zero_ref[s, rows, :] = piece[start : start + 8, :]
                    start = start + STRIP
                    one_ref[s, rows, :] = piece[start : start + 8, :]
                for head in range(3):
                    start = i * PIECE + 2 * STRIP + head * 8
                    heads_ref[head, rows, :] = piece[start : start + 8, :]
    flush(4)

    def product(s, carry):
        both = both_ref[s]
        panel_one = one_ref[s]
        panel_one = jnp.where(jnp.logical_and(is_one, s == 0), 0.0, panel_one)
        strips_ref[0] += dot3(both, panel_one)
        strips_ref[1] += dot3(both, zero_ref[s])
        return carry

    strips_ref[...] = jnp.zeros_like(strips_ref)
    lax.fori_loop(0, LOC_C, product, 0)
    wait(10)
    first = first_ref[...]
    rest_one = jnp.where(is_one, first, 0.0) - strips_ref[0]
    rest_zero = jnp.where(is_zero, first, 0.0) - strips_ref[1]
    corner_ref[0:8, :] = jnp.where(is_one, first[8:16], 0.0)
    corner_ref[8:16, :] = rest_zero[8:16]
    corner_ref[16:24, :] = jnp.where(is_zero, first[0:8], 0.0)
    flush(5)
    scaled_one = dot3(rest_one, inverse_ref[1])
    strips_ref[0] = scaled_one
    strips_ref[1] = dot3(rest_zero - dot3(scaled_one, heads_ref[1]), inverse_ref[0])
    for d in range(4):
        kind = (col_place + d) & 3
        for s in range(LOC_C):
            rows = pl.ds(pl.multiple_of((4 * s + kind) * 8, 8), 8)
            for panel in range(2):
                tile = strips_ref[panel, rows, :]
                if s == 0:
                    tile = jnp.where(kind < 2, 0.0, tile)
                chunk_refs[d][s * 8 : s * 8 + 8, panel * BLK : panel * BLK + BLK] = tile
        flush(d)


def chain_body(place_ref, staged, wait, made, flush, left_ref, right_ref, square_ref):
    corner_ref, heads_ref, inverse_ref = staged[:3]
    chunks, panels = staged[3:7], staged[7:11]
    wait(*range(11))
    mine = pl.ds(pl.multiple_of(place_ref[0] * 8, 8), 8)
    for d in range(4):
        rows = slice(d * STRIP, (d + 1) * STRIP)
        left_ref[0, rows, :] = panels[d][0]
        left_ref[1, rows, :] = panels[d][1]
        right_ref[0, rows, :] = chunks[d][:, BLK:]
        right_ref[1, rows, :] = chunks[d][:, :BLK]
    row = lax.broadcasted_iota(jnp.int32, (BLK, BLK), 0)
    column = lax.broadcasted_iota(jnp.int32, (BLK, BLK), 1)

    def lower(value):
        return jnp.where(row >= column, value, 0.0)

    def phi(value):
        return jnp.where(row > column, value, jnp.where(row == column, 0.5 * value, 0.0))

    def spread(square, start):
        square_ref[...] = square
        square_ref[mine, :] += corner_ref[start : start + 8, :]
        return square_ref[...]

    def corner(square, factor, inverse):
        inner = phi(dot3t(factor, lower(square)))
        whole = dot3(dot3t(inverse, inner), inverse)
        return whole + whole.T

    def put(place, value):
        for half in range(2):
            tile = value[:, half * 128 : half * 128 + 128].reshape(N_ROW, RSUB, 128)
            made[0][:, (place * 2 + half) * 8 : (place * 2 + half) * 8 + 8, :] = tile

    panel_zero, panel_one = left_ref[0], left_ref[1]
    scaled_zero, scaled_one = right_ref[0], right_ref[1]
    cross_factor = heads_ref[1]
    corner_one = corner(
        spread(-dot3t(panel_one, scaled_one), 0), heads_ref[0], inverse_ref[1]
    )
    put(2, corner_one)
    cross = spread(-(dot3t(scaled_one, panel_zero) + dot3(corner_one, cross_factor)), 8)
    cross = dot3(cross, inverse_ref[0])
    put(0, cross)
    put(3, cross.T)
    corner_zero = corner(
        spread(-(dot3t(panel_zero, scaled_zero) + dot3t(cross_factor, cross)), 16),
        heads_ref[2],
        inverse_ref[0],
    )
    put(1, corner_zero)
    flush(0)


def strip_body(place_ref, staged, wait, made, flush):
    a_ref, b_ref, c_ref, d_ref = staged
    across_ref, *out_refs = made
    col_place = place_ref[4]
    wait(*range(4))
    strip = (a_ref[...] + b_ref[...]) + (c_ref[...] + d_ref[...])
    for d in range(4):
        target = (col_place + d) & 3
        out_refs[d][...] = jnp.where(target == 0, strip[:, BLK:], strip[:, :BLK])
    for half in range(2):
        tiles = [
            strip[s * 8 : s * 8 + 8, k * BLK + half * 128 : k * BLK + half * 128 + 128]
            for s in range(LOC_C)
            for k in range(2)
        ]
        for sub, tile in enumerate(swap_groups(tiles)):
            across_ref[half * 16 + sub] = tile
    flush(*range(5))


def total_body(place_ref, staged, wait, made, flush):
    col_place = place_ref[4]
    wait(0)
    total = jnp.sum(staged[0][...], axis=0)
    for d in range(4):
        target = (col_place + d) & 3
        made[d][...] = jnp.where(target == 0, total[:32], total[32:])
    flush(*range(4))


def finish_body(place_ref, staged, wait, made, flush, top_ref):
    half_ref, lines_ref, first_ref, across_ref = staged[:4]
    strips, corners = staged[4:8], staged[8:12]
    (out_ref,) = made
    wait(*range(12))
    col_place = place_ref[4]
    is_zero = col_place == 0
    is_one = col_place == 1
    owner = col_place < 2
    for half in range(2):
        turned = across_ref[half * 16 : half * 16 + 16].reshape(128, 128).T
        for s in range(LOC_C):
            for k in range(2):
                start = (s * 2 + k) * 8
                top_ref[k, s, half] = turned[start : start + 8]
    out_ref[...] = half_ref[...]
    for s in range(LOC_C):
        for half in range(2):
            for block in range(2):
                rows = pl.ds(block * 128 + s * 2 + half, 8, stride=16)
                new = lines_ref[rows, :] + top_ref[1 - block, s, half]
                if s == 0:
                    continue
                out_ref[rows, :] = 0.5 * new
    for half in range(2):
        lanes = slice(half * 128, half * 128 + 128)
        rows = slice(half * 8, half * 8 + 8)
        late = slice(16 + half * 8, 24 + half * 8)
        part_a = (corners[0][rows] + corners[1][rows]) + (corners[2][rows] + corners[3][rows])
        part_b = (corners[0][late] + corners[1][late]) + (corners[2][late] + corners[3][late])
        zero_rows = pl.ds(half, 8, stride=16)
        own = lines_ref[zero_rows, :]
        out_ref[zero_rows, :] = 0.5 * jnp.where(
            is_zero, part_b, own + jnp.where(is_one, part_b, top_ref[1, 0, half])
        )
        one_rows = pl.ds(128 + half, 8, stride=16)
        own = lines_ref[one_rows, :]
        out_ref[one_rows, :] = jnp.where(
            is_zero,
            half_ref[one_rows, :] + 0.5 * (part_a - own),
            0.5 * jnp.where(is_one, part_a, own + top_ref[0, 0, half]),
        )
        for d in range(4):
            kind = (col_place - d) & 3
            for s in range(LOC_C):
                block = 4 * s + kind
                rows = pl.ds(block * 128 + half, 8, stride=16)
                use = owner if s > 0 else jnp.logical_and(owner, kind > 1)
                change = strips[d][s * 8 : s * 8 + 8, lanes] - first_ref[pl.ds(block * 8, 8), lanes]
                out_ref[rows, :] += jnp.where(use, 0.5 * change, 0.0)
    flush(0)


def ring(first, d):
    pairs = []
    for i in range(N_ROW):
        y, z, core = i >> 3, (i >> 1) & 3, i & 1
        if (core == 0) == first:
            z = (z + d) & 3
        else:
            y = (y + d) & 3
        pairs.append((i, (y * 4 + z) * 2 + core))
    return pairs


def around(piece, first):
    return [piece] + [lax.ppermute(piece, "row", ring(first, d)) for d in RING[1:]]


def to_owners(pieces):
    moved = [
        lax.ppermute(pieces[d], "col", [((t - d) % 4, t) for t in range(2)]) for d in range(1, 4)
    ]
    return [pieces[0]] + moved


def on_device(adjoint, lower_panels, diag_inverse):
    row_place = lax.axis_index("row")
    col_place = lax.axis_index("col")
    place = jnp.stack(
        [row_place, row_place >> 3, (row_place >> 1) & 3, row_place & 1, col_place]
    ).astype(jnp.int32)
    lines = adjoint.reshape(LINES, 128)
    panels = lower_panels.reshape(2, STRIP, BLK)
    by_rows = [panels] + [
        lax.ppermute(panels, "col", [(i, (i + d) % 4) for i in range(4)]) for d in range(1, 4)
    ]
    lead = jnp.stack([piece[:, :RSUB] for piece in by_rows])
    lead_one = lax.dynamic_index_in_dim(lead, (col_place - 1) & 3, 0, False)
    lead_zero = lax.dynamic_index_in_dim(lead, col_place, 0, False)
    piece = jnp.concatenate(
        [panels.reshape(2 * STRIP, BLK), lead_one[1], lead_one[0], lead_zero[0]], axis=0
    )
    lines_shape = shape(LINES, 128)
    (outgoing,) = call(
        pack_body,
        [lines_shape],
        [lines_shape],
        scratch=[pltpu.VMEM((2, LOC_C, BLK, 128), F32)],
        size=2**24,
    )(place, lines)
    outgoing, piece = lax.optimization_barrier((outgoing, piece))
    plane = around(jnp.concatenate(around(piece, True), axis=0), False)
    arrived = lax.all_to_all(
        outgoing.reshape(N_ROW * N_COL, 32, 128), ("row", "col"), split_axis=0, concat_axis=0, tiled=True
    ).reshape(LINES, 128)
    plane = plane + [lax.ppermute(part, "row", [(i, i ^ 1) for i in range(N_ROW)]) for part in plane]

    image_ins = [lines, arrived, *plane, diag_inverse]
    *chunks, heads, corner_in, first = call(
        image_body,
        [shape(STRIP, 2 * BLK)] * 4 + [shape(3, BLK, BLK), shape(24, BLK), shape(ROWS, BLK)],
        image_ins,
        scratch=[
            pltpu.VMEM((LOC_C, ROWS, BLK), F32),
            pltpu.VMEM((LOC_C, BLK, BLK), F32),
            pltpu.VMEM((LOC_C, BLK, BLK), F32),
            pltpu.VMEM((2, ROWS, BLK), F32),
        ],
        flops=2**32,
        size=2**24,
    )(place, *image_ins)
    strips = [chunks[0]] + [
        lax.ppermute(chunks[d], "col", [(i, (i + d) % 4) for i in range(4)]) for d in range(1, 4)
    ]
    chain_ins = [
        corner_in, heads, diag_inverse, *chunks, by_rows[0], by_rows[3], by_rows[2], by_rows[1]
    ]
    (corners,) = call(
        chain_body,
        [shape(N_ROW, 64, 128)],
        chain_ins,
        scratch=[
            pltpu.VMEM((2, ROWS, BLK), F32),
            pltpu.VMEM((2, ROWS, BLK), F32),
            pltpu.VMEM((BLK, BLK), F32),
        ],
        flops=2**32,
        size=2**23,
    )(place, *chain_ins)
    corners, *strips = lax.optimization_barrier((corners, *strips))
    corners = lax.all_to_all(corners, "row", split_axis=0, concat_axis=0, tiled=True)
    across, *strips = call(
        strip_body, [shape(N_ROW, RSUB, 128)] + [shape(STRIP, BLK)] * 4, strips, size=2**21
    )(place, *strips)
    across = lax.all_to_all(across, "row", split_axis=0, concat_axis=0, tiled=True)
    strips = to_owners(strips)
    (half,) = call(half_body, [lines_shape], [lines_shape] * 2, size=2**24)(place, lines, arrived)
    corners = to_owners(
        call(total_body, [shape(32, 128)] * 4, [corners], size=2**21)(place, corners)
    )
    finish_ins = [half, lines[:BLK], first, across, *strips, *corners]
    (result,) = call(
        finish_body,
        [lines_shape],
        finish_ins,
        scratch=[pltpu.VMEM((2, LOC_C, 2, RSUB, 128), F32)],
        size=2**23,
    )(place, *finish_ins)
    return result.reshape(NBLK, 1, RSUB, LOC_C, 1, BLK)


def solution(mesh):
    return jax.shard_map(
        on_device,
        mesh=mesh,
        in_specs=(
            P(None, "row", None, None, "col", None),
            P(None, None, "col", "row", None, None),
            P(),
        ),
        out_specs=P(None, "row", None, None, "col", None),
        check_vma=False,
    )
```

```python
import jax
import jax.numpy as jnp
from jax import lax
from jax.experimental import pallas as pl
from jax.experimental.pallas import tpu as pltpu
from jax.sharding import PartitionSpec as P

BLK = 256
RSUB = 8
LOC_C = 8
N_ROW = 32
N_COL = 4
NBLK = 32
ROWS = NBLK * RSUB
COLS = LOC_C * BLK
LINES = ROWS * COLS // 128
STRIP = LOC_C * RSUB
PIECE = 2 * STRIP + 3 * RSUB
RING = (0, 1, 3, 2)
F32 = jnp.float32
BF16 = jnp.bfloat16
VMEM_LIMIT = 56 * 1024 * 1024
SMEM = pl.BlockSpec(memory_space=pltpu.SMEM)


def shape(*dims, dtype=F32):
    return jax.ShapeDtypeStruct(dims, dtype)


def call(body, outs, ins, scratch=(), flops=0, size=0):
    count, results = len(ins), len(outs)

    def kernel(*refs):
        place, sources = refs[0], refs[1 : 1 + count]
        targets = refs[1 + count : 1 + count + results]
        staged = refs[1 + count + results : 1 + 2 * count + results]
        made = refs[1 + 2 * count + results : 1 + 2 * count + 2 * results]
        extra = refs[1 + 2 * count + 2 * results : -2]
        in_sem, out_sem = refs[-2:]
        copies = [
            pltpu.make_async_copy(sources[i], staged[i], in_sem.at[i]) for i in range(count)
        ]
        leaving = [
            pltpu.make_async_copy(made[i], targets[i], out_sem.at[i]) for i in range(results)
        ]
        for copy in copies:
            copy.start()
        body(
            place,
            staged,
            lambda *which: [copies[i].wait() for i in which],
            made,
            lambda *which: [leaving[i].start() for i in which],
            *extra,
        )
        for copy in leaving:
            copy.wait()

    anywhere = pl.BlockSpec(memory_space=pl.ANY)
    return pl.pallas_call(
        kernel,
        out_shape=list(outs),
        in_specs=[SMEM] + [anywhere] * count,
        out_specs=[anywhere] * results,
        scratch_shapes=[pltpu.VMEM(x.shape, x.dtype) for x in ins]
        + [pltpu.VMEM(x.shape, x.dtype) for x in outs]
        + list(scratch)
        + [pltpu.SemaphoreType.DMA((count,)), pltpu.SemaphoreType.DMA((results,))],
        compiler_params=pltpu.CompilerParams(vmem_limit_bytes=VMEM_LIMIT),
        cost_estimate=pl.CostEstimate(flops=flops, bytes_accessed=size, transcendentals=0),
    )


def split(value):
    high = value.astype(BF16)
    return high, (value - high.astype(F32)).astype(BF16)


def dot_split(left, right):
    left_high, left_low = left
    right_high, right_low = right

    def one(a, b):
        return jnp.dot(a, b, preferred_element_type=F32)

    return one(left_high, right_high) + (one(left_high, right_low) + one(left_low, right_high))


def dot3(left, right):
    return dot_split(split(left), split(right))


def dot3t(left, right):
    return dot3(left.T, right)


def swap_groups(tiles):
    tiles = list(tiles)
    group = lax.broadcasted_iota(jnp.int32, (8, 128), 1) // 8
    for bit in (1, 2, 4, 8):
        keep = (group & bit) == 0
        for i in range(16):
            if i & bit:
                continue
            a, b = tiles[i], tiles[i | bit]
            tiles[i] = jnp.where(keep, a, pltpu.roll(b, 8 * bit, 1))
            tiles[i | bit] = jnp.where(keep, pltpu.roll(a, 128 - 8 * bit, 1), b)
    return tiles


def turn_body(place_ref, staged, wait, made, flush):
    (lines_ref,), (turned_ref,) = staged, made
    wait(0)

    def one(index, carry):
        group = index // 2
        half = index % 2
        for high in range(2):
            tiles = [
                lines_ref[pl.ds((4 * (4 * high + low) + col) * 128 + index, 8, stride=16), :]
                for col in range(N_COL)
                for low in range(4)
            ]
            turned_ref[high, group, pl.ds(half * 128, 128), :] = jnp.concatenate(tiles, axis=0).T
        return carry

    lax.fori_loop(0, 16, one, 0)
    flush(0)


def pack_body(place_ref, staged, wait, made, flush):
    (turned_ref,), (out_ref,) = staged, made
    wait(0)

    def one(row, carry):
        tiles = [
            turned_ref[high, group, pl.ds(row * 8, 8), :]
            for high in range(2)
            for group in range(LOC_C)
        ]
        out_ref[pl.ds(row * 128, 128), :] = jnp.concatenate(tiles, axis=0).T
        return carry

    lax.fori_loop(0, N_ROW, one, 0)
    flush(0)


def mirror_tiles(lines_ref, col, low, half):
    tiles = [
        lines_ref[pl.ds(((half * 16 + sub) * 4 + col) * 32 + low * 8, 8), :] for sub in range(16)
    ]
    turned = jnp.concatenate(tiles, axis=0).T
    return {
        (high, group): turned[high * 64 + group * 8 : high * 64 + group * 8 + 8]
        for high in range(2)
        for group in range(LOC_C)
    }


def half_body(place_ref, staged, wait, made, flush):
    lines_ref, arrived_ref = staged
    (out_ref,) = made
    wait(0, 1)
    def turn(col, carry):
        for low in range(4):
            for half in range(2):
                for (high, group), tile in mirror_tiles(arrived_ref, col, low, half).items():
                    start = (4 * group + col) * 128 + (4 * high + low) * 2 + half
                    rows = pl.ds(start, 8, stride=16)
                    out_ref[rows, :] = 0.5 * (lines_ref[rows, :] + tile)
        return carry

    lax.fori_loop(0, N_COL, turn, 0)
    flush(0)


def direct_body(
    place_ref, staged, wait, made, flush, both_ref, one_ref, zero_ref, left_ref, image_ref, square_ref
):
    lines_ref, *pieces = staged[:9]
    inverse_ref = staged[9]
    panels = staged[10:14]
    rest_ref, high_ref, low_ref, heads_ref, first_ref, corners_ref = made
    row_y, row_z, core, col_place = (place_ref[i] for i in range(1, 5))
    is_zero = col_place == 0
    is_one = col_place == 1
    mine = pl.ds(pl.multiple_of(place_ref[0] * 8, 8), 8)
    wait(0)

    def gather(block, carry):
        rows = pl.ds(block * 8, 8)
        for inner in range(LOC_C):
            for half in range(2):
                lanes = slice(half * 128, half * 128 + 128)
                own = lines_ref[pl.ds(block * 128 + inner * 2 + half, 8, stride=16), :]
                if inner == 0:
                    first_ref[rows, lanes] = own
                    own = jnp.where(is_zero | is_one, 0.0, own)
                both_ref[inner, rows, lanes] = own
        return carry

    lax.fori_loop(0, NBLK, gather, 0)
    flush(4)
    wait(*range(1, 9))
    for side in range(2):
        moved = core if side == 0 else 1 - core
        for j in range(4):
            for i in range(4):
                place_y = (row_y - jnp.where(moved == 0, RING[j], RING[i])) & 3
                place_z = (row_z - jnp.where(moved == 0, RING[i], RING[j])) & 3
                owner = (place_y * 4 + place_z) * 2 + moved
                rows = pl.ds(pl.multiple_of(owner * 8, 8), 8)
                piece = pieces[4 * side + j]
                for s in range(LOC_C):
                    start = i * PIECE + s * 8
                    zero_ref[s, rows, :] = piece[start : start + 8, :]
                    start = start + STRIP
                    one_ref[s, rows, :] = piece[start : start + 8, :]
                for head in range(3):
                    start = i * PIECE + 2 * STRIP + head * 8
                    heads_ref[head, rows, :] = piece[start : start + 8, :]
    flush(3)

    def product(s, carry):
        both = split(both_ref[s])
        panel_one = jnp.where(jnp.logical_and(is_one, s == 0), 0.0, one_ref[s])
        for place, panel in enumerate((panel_one, zero_ref[s])):
            high, low = split(panel)
            lanes = slice(place * BLK, place * BLK + BLK)
            high_ref[s, :, lanes] = high
            low_ref[s, :, lanes] = low
            image_ref[place] += dot_split(both, (high, low))
        return carry

    image_ref[...] = jnp.zeros_like(image_ref)
    lax.fori_loop(0, LOC_C, product, 0)
    flush(1, 2)
    first = first_ref[...]
    image_one, image_zero = image_ref[0], image_ref[1]
    rest_one = jnp.where(is_one, first, 0.0) - image_one
    rest_zero = jnp.where(is_zero, first, 0.0) - image_zero
    rest_ref[0] = rest_one
    rest_ref[1] = rest_zero
    flush(0)

    wait(*range(9, 14))
    for d in range(4):
        kind = (col_place - d) & 3
        for s in range(LOC_C):
            rows = pl.ds(pl.multiple_of((4 * s + kind) * 8, 8), 8)
            for panel in range(2):
                tile = panels[d][panel, s * 8 : s * 8 + 8, :]
                if s == 0:
                    tile = jnp.where(kind < 2, 0.0, tile)
                left_ref[panel, rows, :] = tile
    row = lax.broadcasted_iota(jnp.int32, (BLK, BLK), 0)
    column = lax.broadcasted_iota(jnp.int32, (BLK, BLK), 1)

    def lower(value):
        return jnp.where(row >= column, value, 0.0)

    def phi(value):
        return jnp.where(row > column, value, jnp.where(row == column, 0.5 * value, 0.0))

    def spread(square, part):
        square_ref[...] = square
        square_ref[mine, :] += part
        return square_ref[...]

    def corner(square, factor, inverse):
        inner = phi(dot3t(factor, lower(square)))
        whole = dot3(dot3t(inverse, inner), inverse)
        return whole + whole.T

    def put(place, value):
        for half in range(2):
            tile = value[:, half * 128 : half * 128 + 128].reshape(N_ROW, RSUB, 128)
            corners_ref[:, (place * 2 + half) * 8 : (place * 2 + half) * 8 + 8, :] = tile

    left_one = split(left_ref[1].T)
    left_zero = split(left_ref[0].T)
    parts_one = split(image_one)
    parts_zero = split(image_zero)
    parts_rest = split(rest_one)
    inverse_one, inverse_zero = inverse_ref[1], inverse_ref[0]
    cross_factor = heads_ref[1]
    sum_one = dot_split(left_one, parts_rest) - dot_split(left_one, parts_one).T
    corner_one = corner(
        spread(-dot3(sum_one, inverse_one), jnp.where(is_one, first[8:16], 0.0)),
        heads_ref[0],
        inverse_one,
    )
    put(2, corner_one)
    sum_cross = dot_split(left_zero, parts_rest).T - dot_split(left_one, parts_zero)
    mixed = spread(dot3t(inverse_one, sum_cross), image_zero[8:16])
    cross = spread(
        -(mixed + dot3(corner_one, cross_factor)), jnp.where(is_zero, first[8:16], 0.0)
    )
    cross = dot3(cross, inverse_zero)
    put(0, cross)
    put(3, cross.T)
    sum_zero = dot_split(left_zero, split(rest_zero)) - dot_split(left_zero, parts_zero).T
    sum_zero = dot3(sum_zero - dot3t(mixed, cross_factor), inverse_zero)
    corner_zero = corner(
        spread(-(sum_zero + dot3t(cross_factor, cross)), jnp.where(is_zero, first[0:8], 0.0)),
        heads_ref[2],
        inverse_zero,
    )
    put(1, corner_zero)
    flush(5)


def image_body(place_ref, staged, wait, made, flush, both_ref, strips_ref):
    arrived_ref, rest_ref, high_ref, low_ref, heads_ref, inverse_ref = staged
    chunk_refs = made
    col_place = place_ref[4]
    wait(0)

    def turn(col, carry):
        for low in range(4):
            for half in range(2):
                for (high, group), tile in mirror_tiles(arrived_ref, col, low, half).items():
                    inner = 4 * high + low
                    if group == 0:
                        tile = jnp.where(col < 2, 0.0, tile)
                    if inner == 0:
                        tile = jnp.where(col_place == 0, 0.0, tile)
                    rows = pl.ds((4 * group + col) * 8, 8)
                    both_ref[inner, rows, half * 128 : half * 128 + 128] = tile
        return carry

    lax.fori_loop(0, N_COL, turn, 0)
    wait(1, 2, 3)
    strips_ref[...] = jnp.zeros_like(strips_ref)

    def product(s, carry):
        strips_ref[...] += dot_split(split(both_ref[s]), (high_ref[s], low_ref[s]))
        return carry

    lax.fori_loop(0, LOC_C, product, 0)
    wait(4, 5)
    scaled_one = dot3(rest_ref[0] - strips_ref[:, :BLK], inverse_ref[1])
    rest_zero = rest_ref[1] - strips_ref[:, BLK:]
    strips_ref[:, :BLK] = scaled_one
    strips_ref[:, BLK:] = dot3(rest_zero - dot3(scaled_one, heads_ref[1]), inverse_ref[0])
    for d in range(4):
        kind = (col_place + d) & 3
        for s in range(LOC_C):
            tile = strips_ref[pl.ds(pl.multiple_of((4 * s + kind) * 8, 8), 8), :]
            if s == 0:
                tile = jnp.where(kind < 2, 0.0, tile)
            chunk_refs[d][s * 8 : s * 8 + 8, :] = tile
        flush(d)


def strip_body(place_ref, staged, wait, made, flush):
    a_ref, b_ref, c_ref, d_ref = staged
    across_ref, *out_refs = made
    col_place = place_ref[4]
    wait(*range(4))
    strip = (a_ref[...] + b_ref[...]) + (c_ref[...] + d_ref[...])
    for d in range(4):
        target = (col_place + d) & 3
        out_refs[d][...] = jnp.where(target == 0, strip[:, BLK:], strip[:, :BLK])
    for half in range(2):
        tiles = [
            strip[s * 8 : s * 8 + 8, k * BLK + half * 128 : k * BLK + half * 128 + 128]
            for s in range(LOC_C)
            for k in range(2)
        ]
        for sub, tile in enumerate(swap_groups(tiles)):
            across_ref[half * 16 + sub] = tile
    flush(*range(5))


def total_body(place_ref, staged, wait, made, flush):
    col_place = place_ref[4]
    wait(0)
    total = jnp.sum(staged[0][...], axis=0)
    for d in range(4):
        target = (col_place + d) & 3
        made[d][...] = jnp.where(target == 0, total[:32], total[32:])
    flush(*range(4))


def finish_body(place_ref, staged, wait, made, flush, top_ref):
    half_ref, lines_ref, first_ref, across_ref = staged[:4]
    strips, corners = staged[4:8], staged[8:12]
    (out_ref,) = made
    wait(*range(12))
    col_place = place_ref[4]
    is_zero = col_place == 0
    is_one = col_place == 1
    owner = col_place < 2
    for half in range(2):
        turned = across_ref[half * 16 : half * 16 + 16].reshape(128, 128).T
        for s in range(LOC_C):
            for k in range(2):
                start = (s * 2 + k) * 8
                top_ref[k, s, half] = turned[start : start + 8]
    out_ref[...] = half_ref[...]
    for s in range(LOC_C):
        for half in range(2):
            for block in range(2):
                rows = pl.ds(block * 128 + s * 2 + half, 8, stride=16)
                new = lines_ref[rows, :] + top_ref[1 - block, s, half]
                if s == 0:
                    continue
                out_ref[rows, :] = 0.5 * new
    for half in range(2):
        lanes = slice(half * 128, half * 128 + 128)
        rows = slice(half * 8, half * 8 + 8)
        late = slice(16 + half * 8, 24 + half * 8)
        part_a = (corners[0][rows] + corners[1][rows]) + (corners[2][rows] + corners[3][rows])
        part_b = (corners[0][late] + corners[1][late]) + (corners[2][late] + corners[3][late])
        zero_rows = pl.ds(half, 8, stride=16)
        own = lines_ref[zero_rows, :]
        out_ref[zero_rows, :] = 0.5 * jnp.where(
            is_zero, part_b, own + jnp.where(is_one, part_b, top_ref[1, 0, half])
        )
        one_rows = pl.ds(128 + half, 8, stride=16)
        own = lines_ref[one_rows, :]
        out_ref[one_rows, :] = jnp.where(
            is_zero,
            half_ref[one_rows, :] + 0.5 * (part_a - own),
            0.5 * jnp.where(is_one, part_a, own + top_ref[0, 0, half]),
        )
        for d in range(4):
            kind = (col_place - d) & 3
            for s in range(LOC_C):
                block = 4 * s + kind
                rows = pl.ds(block * 128 + half, 8, stride=16)
                use = owner if s > 0 else jnp.logical_and(owner, kind > 1)
                change = strips[d][s * 8 : s * 8 + 8, lanes] - first_ref[pl.ds(block * 8, 8), lanes]
                out_ref[rows, :] += jnp.where(use, 0.5 * change, 0.0)
    flush(0)


def ring(first, d):
    pairs = []
    for i in range(N_ROW):
        y, z, core = i >> 3, (i >> 1) & 3, i & 1
        if (core == 0) == first:
            z = (z + d) & 3
        else:
            y = (y + d) & 3
        pairs.append((i, (y * 4 + z) * 2 + core))
    return pairs


def around(piece, first):
    return [piece] + [lax.ppermute(piece, "row", ring(first, d)) for d in RING[1:]]


def to_owners(pieces):
    moved = [
        lax.ppermute(pieces[d], "col", [((t - d) % 4, t) for t in range(2)]) for d in range(1, 4)
    ]
    return [pieces[0]] + moved


def on_device(adjoint, lower_panels, diag_inverse):
    row_place = lax.axis_index("row")
    col_place = lax.axis_index("col")
    place = jnp.stack(
        [row_place, row_place >> 3, (row_place >> 1) & 3, row_place & 1, col_place]
    ).astype(jnp.int32)
    lines = adjoint.reshape(LINES, 128)
    panels = lower_panels.reshape(2, STRIP, BLK)
    by_rows = [panels] + [
        lax.ppermute(panels, "col", [(i, (i + d) % 4) for i in range(4)]) for d in range(1, 4)
    ]
    lead = jnp.stack([piece[:, :RSUB] for piece in by_rows])
    lead_one = lax.dynamic_index_in_dim(lead, (col_place - 1) & 3, 0, False)
    lead_zero = lax.dynamic_index_in_dim(lead, col_place, 0, False)
    piece = jnp.concatenate(
        [panels.reshape(2 * STRIP, BLK), lead_one[1], lead_one[0], lead_zero[0]], axis=0
    )
    lines_shape = shape(LINES, 128)
    turned_shape = shape(2, LOC_C, BLK, 128)
    (turned,) = call(turn_body, [turned_shape], [lines_shape], size=2**23)(place, lines)
    ring_one = jnp.concatenate(around(piece, True), axis=0)
    turned, ring_one = lax.optimization_barrier((turned, ring_one))
    plane = around(ring_one, False)
    (outgoing,) = call(pack_body, [lines_shape], [turned_shape], size=2**23)(place, turned)
    arrived = lax.all_to_all(
        outgoing.reshape(N_ROW * N_COL, 32, 128), ("row", "col"), split_axis=0, concat_axis=0, tiled=True
    ).reshape(LINES, 128)
    plane = plane + [lax.ppermute(part, "row", [(i, i ^ 1) for i in range(N_ROW)]) for part in plane]

    direct_ins = [lines, *plane, diag_inverse, *by_rows]
    split_shape = shape(LOC_C, BLK, 2 * BLK, dtype=BF16)
    square_shape = pltpu.VMEM((BLK, BLK), F32)
    pair_shape = pltpu.VMEM((2, BLK, BLK), F32)
    wide_shape = pltpu.VMEM((LOC_C, BLK, BLK), F32)
    rest, high, low, heads, first, corners = call(
        direct_body,
        [
            shape(2, BLK, BLK), split_shape, split_shape, shape(3, BLK, BLK), shape(BLK, BLK),
            shape(N_ROW, 64, 128),
        ],
        direct_ins,
        scratch=[wide_shape, wide_shape, wide_shape, pair_shape, pair_shape, square_shape],
        flops=2**33,
        size=2**24,
    )(place, *direct_ins)
    corners = lax.all_to_all(corners, "row", split_axis=0, concat_axis=0, tiled=True)
    image_ins = [arrived, rest, high, low, heads, diag_inverse]
    chunks = call(
        image_body,
        [shape(STRIP, 2 * BLK)] * 4,
        image_ins,
        scratch=[wide_shape, pltpu.VMEM((ROWS, 2 * BLK), F32)],
        flops=2**32,
        size=2**24,
    )(place, *image_ins)
    strips = [chunks[0]] + [
        lax.ppermute(chunks[d], "col", [(i, (i + d) % 4) for i in range(4)]) for d in range(1, 4)
    ]
    across, *strips = call(
        strip_body, [shape(N_ROW, RSUB, 128)] + [shape(STRIP, BLK)] * 4, strips, size=2**21
    )(place, *strips)
    across = lax.all_to_all(across, "row", split_axis=0, concat_axis=0, tiled=True)
    strips = to_owners(strips)
    (half,) = call(half_body, [lines_shape], [lines_shape] * 2, size=2**24)(place, lines, arrived)
    half, corners = lax.optimization_barrier((half, corners))
    corners = to_owners(
        call(total_body, [shape(32, 128)] * 4, [corners], size=2**21)(place, corners)
    )
    finish_ins = [half, lines[:BLK], first, across, *strips, *corners]
    (result,) = call(
        finish_body,
        [lines_shape],
        finish_ins,
        scratch=[pltpu.VMEM((2, LOC_C, 2, RSUB, 128), F32)],
        size=2**23,
    )(place, *finish_ins)
    return result.reshape(NBLK, 1, RSUB, LOC_C, 1, BLK)


def solution(mesh):
    return jax.shard_map(
        on_device,
        mesh=mesh,
        in_specs=(
            P(None, "row", None, None, "col", None),
            P(None, None, "col", "row", None, None),
            P(),
        ),
        out_specs=P(None, "row", None, None, "col", None),
        check_vma=False,
    )
```

```python
import jax
import jax.numpy as jnp
from jax import lax
from jax.experimental import pallas as pl
from jax.experimental.pallas import tpu as pltpu
from jax.sharding import PartitionSpec as P

BLK = 256
RSUB = 8
LOC_C = 8
N_ROW = 32
N_COL = 4
NBLK = 32
ROWS = NBLK * RSUB
COLS = LOC_C * BLK
LINES = ROWS * COLS // 128
STRIP = LOC_C * RSUB
PIECE = 2 * STRIP
N_CHIP = 16
RING = (0, 1, 3, 2)
F32 = jnp.float32
BF16 = jnp.bfloat16
VMEM_LIMIT = 56 * 1024 * 1024
SMEM = pl.BlockSpec(memory_space=pltpu.SMEM)


def shape(*dims, dtype=F32):
    return jax.ShapeDtypeStruct(dims, dtype)


def call(body, outs, ins, scratch=(), heads=None, flops=0, size=0):
    count, results = len(ins), len(outs)
    heads = heads or {}

    def kernel(*refs):
        place, sources = refs[0], refs[1 : 1 + count]
        targets = refs[1 + count : 1 + count + results]
        staged = refs[1 + count + results : 1 + 2 * count + results]
        made = refs[1 + 2 * count + results : 1 + 2 * count + 2 * results]
        extra = refs[1 + 2 * count + 2 * results : -2]
        in_sem, out_sem = refs[-2:]
        copies = [
            pltpu.make_async_copy(
                sources[i].at[pl.ds(0, heads[i])] if i in heads else sources[i],
                staged[i],
                in_sem.at[i],
            )
            for i in range(count)
        ]
        leaving = [
            pltpu.make_async_copy(made[i], targets[i], out_sem.at[i]) for i in range(results)
        ]
        for copy in copies:
            copy.start()
        body(
            place,
            staged,
            lambda *which: [copies[i].wait() for i in which],
            made,
            lambda *which: [leaving[i].start() for i in which],
            *extra,
        )
        for copy in leaving:
            copy.wait()

    anywhere = pl.BlockSpec(memory_space=pl.ANY)
    return pl.pallas_call(
        kernel,
        out_shape=list(outs),
        in_specs=[SMEM] + [anywhere] * count,
        out_specs=[anywhere] * results,
        scratch_shapes=[
            pltpu.VMEM((heads.get(i, x.shape[0]), *x.shape[1:]), x.dtype) for i, x in enumerate(ins)
        ]
        + [pltpu.VMEM(x.shape, x.dtype) for x in outs]
        + list(scratch)
        + [pltpu.SemaphoreType.DMA((count,)), pltpu.SemaphoreType.DMA((results,))],
        compiler_params=pltpu.CompilerParams(vmem_limit_bytes=VMEM_LIMIT),
        cost_estimate=pl.CostEstimate(flops=flops, bytes_accessed=size, transcendentals=0),
    )


def split(value):
    high = value.astype(BF16)
    return high, (value - high.astype(F32)).astype(BF16)


def dot_split(left, right):
    left_high, left_low = left
    right_high, right_low = right

    def one(a, b):
        return jnp.dot(a, b, preferred_element_type=F32)

    return one(left_high, right_high) + (one(left_high, right_low) + one(left_low, right_high))


def dot3(left, right):
    return dot_split(split(left), split(right))


def dot3t(left, right):
    return dot3(left.T, right)


def swap_groups(tiles):
    tiles = list(tiles)
    group = lax.broadcasted_iota(jnp.int32, (8, 128), 1) // 8
    for bit in (1, 2, 4, 8):
        keep = (group & bit) == 0
        for i in range(16):
            if i & bit:
                continue
            a, b = tiles[i], tiles[i | bit]
            tiles[i] = jnp.where(keep, a, pltpu.roll(b, 8 * bit, 1))
            tiles[i | bit] = jnp.where(keep, pltpu.roll(a, 128 - 8 * bit, 1), b)
    return tiles


def pack_body(place_ref, staged, wait, made, flush, turned_ref):
    (lines_ref,), (out_ref,) = staged, made
    wait(0)

    def first(index, carry):
        group = index // 2
        half = index % 2
        for high in range(2):
            tiles = [
                lines_ref[pl.ds((4 * (4 * high + low) + col) * 128 + index, 8, stride=16), :]
                for col in range(N_COL)
                for low in range(4)
            ]
            turned_ref[high, group, pl.ds(half * 128, 128), :] = jnp.concatenate(tiles, axis=0).T
        return carry

    lax.fori_loop(0, 16, first, 0)

    def second(row, carry):
        tiles = [
            turned_ref[high, group, pl.ds(row * 8, 8), :]
            for high in range(2)
            for group in range(LOC_C)
        ]
        out_ref[pl.ds(row * 128, 128), :] = jnp.concatenate(tiles, axis=0).T
        return carry

    lax.fori_loop(0, N_ROW, second, 0)
    flush(0)


def mirror_tiles(lines_ref, col, low, half):
    tiles = [
        lines_ref[pl.ds(((half * 16 + sub) * 4 + col) * 32 + low * 8, 8), :] for sub in range(16)
    ]
    turned = jnp.concatenate(tiles, axis=0).T
    return {
        (high, group): turned[high * 64 + group * 8 : high * 64 + group * 8 + 8]
        for high in range(2)
        for group in range(LOC_C)
    }


def direct_body(
    place_ref, staged, wait, made, flush, both_ref, one_ref, zero_ref, left_ref, image_ref, square_ref
):
    lines_ref, *pieces = staged[:9]
    inverse_ref = staged[9]
    panels = staged[10:14]
    leads = staged[14:16]
    rest_ref, high_ref, low_ref, heads_ref, first_ref, keep_ref, give_ref = made
    row_y, row_z, core, col_place = (place_ref[i] for i in range(1, 5))
    is_zero = col_place == 0
    is_one = col_place == 1
    mine = pl.ds(pl.multiple_of(place_ref[0] * 8, 8), 8)
    wait(0)

    def gather(block, carry):
        rows = pl.ds(block * 8, 8)
        for inner in range(LOC_C):
            for half in range(2):
                lanes = slice(half * 128, half * 128 + 128)
                own = lines_ref[pl.ds(block * 128 + inner * 2 + half, 8, stride=16), :]
                if inner == 0:
                    first_ref[rows, lanes] = own
                    own = jnp.where(is_zero | is_one, 0.0, own)
                both_ref[inner, rows, lanes] = own
        return carry

    lax.fori_loop(0, NBLK, gather, 0)
    flush(4)
    wait(*range(1, 9))
    for side in range(2):
        moved = core if side == 0 else 1 - core
        for j in range(4):
            for i in range(4):
                place_y = (row_y - jnp.where(moved == 0, RING[j], RING[i])) & 3
                place_z = (row_z - jnp.where(moved == 0, RING[i], RING[j])) & 3
                owner = (place_y * 4 + place_z) * 2 + moved
                rows = pl.ds(pl.multiple_of(owner * 8, 8), 8)
                piece = pieces[4 * side + j]
                for s in range(LOC_C):
                    start = i * PIECE + s * 8
                    zero_ref[s, rows, :] = piece[start : start + 8, :]
                    start = start + STRIP
                    one_ref[s, rows, :] = piece[start : start + 8, :]

    def product(s, carry):
        both = split(both_ref[s])
        panel_one = jnp.where(jnp.logical_and(is_one, s == 0), 0.0, one_ref[s])
        for place, panel in enumerate((panel_one, zero_ref[s])):
            high, low = split(panel)
            lanes = slice(place * BLK, place * BLK + BLK)
            high_ref[s, :, lanes] = high
            low_ref[s, :, lanes] = low
            image_ref[place] += dot_split(both, (high, low))
        return carry

    image_ref[...] = jnp.zeros_like(image_ref)
    lax.fori_loop(0, LOC_C, product, 0)
    flush(1, 2)
    first = first_ref[...]
    image_one, image_zero = image_ref[0], image_ref[1]
    rest_one = jnp.where(is_one, first, 0.0) - image_one
    rest_zero = jnp.where(is_zero, first, 0.0) - image_zero
    rest_ref[0] = rest_one
    rest_ref[1] = rest_zero
    flush(0)

    wait(*range(9, 16))
    for side in range(2):
        moved = core if side == 0 else 1 - core
        for chip in range(N_CHIP):
            rows = pl.ds(pl.multiple_of((chip * 2 + moved) * 8, 8), 8)
            for head in range(3):
                for half in range(2):
                    start = (head * 2 + half) * 8
                    lanes = slice(half * 128, half * 128 + 128)
                    heads_ref[head, rows, lanes] = leads[side][chip, start : start + 8, :]
    flush(3)
    for d in range(4):
        kind = (col_place - d) & 3
        for s in range(LOC_C):
            rows = pl.ds(pl.multiple_of((4 * s + kind) * 8, 8), 8)
            for panel in range(2):
                tile = panels[d][panel, s * 8 : s * 8 + 8, :]
                if s == 0:
                    tile = jnp.where(kind < 2, 0.0, tile)
                left_ref[panel, rows, :] = tile
    row = lax.broadcasted_iota(jnp.int32, (BLK, BLK), 0)
    column = lax.broadcasted_iota(jnp.int32, (BLK, BLK), 1)

    def lower(value):
        return jnp.where(row >= column, value, 0.0)

    def phi(value):
        return jnp.where(row > column, value, jnp.where(row == column, 0.5 * value, 0.0))

    def spread(square, part):
        square_ref[...] = square
        square_ref[mine, :] += part
        return square_ref[...]

    def corner(square, factor, inverse):
        inner = phi(dot3t(factor, lower(square)))
        whole = dot3(dot3t(inverse, inner), inverse)
        return whole + whole.T

    def put(place, value):
        for half in range(2):
            tile = value[:, half * 128 : half * 128 + 128].reshape(N_CHIP, 2, RSUB, 128)
            rows = slice((place * 2 + half) * 8, (place * 2 + half) * 8 + 8)
            keep_ref[:, rows, :] = jnp.where(core == 0, tile[:, 0], tile[:, 1])
            give_ref[:, rows, :] = jnp.where(core == 0, tile[:, 1], tile[:, 0])

    left_one = split(left_ref[1].T)
    left_zero = split(left_ref[0].T)
    parts_one = split(image_one)
    parts_zero = split(image_zero)
    parts_rest = split(rest_one)
    inverse_one, inverse_zero = inverse_ref[1], inverse_ref[0]
    cross_factor = heads_ref[1]
    sum_one = dot_split(left_one, parts_rest) - dot_split(left_one, parts_one).T
    corner_one = corner(
        spread(-dot3(sum_one, inverse_one), jnp.where(is_one, first[8:16], 0.0)),
        heads_ref[0],
        inverse_one,
    )
    put(2, corner_one)
    sum_cross = dot_split(left_zero, parts_rest).T - dot_split(left_one, parts_zero)
    mixed = spread(dot3t(inverse_one, sum_cross), image_zero[8:16])
    cross = spread(
        -(mixed + dot3(corner_one, cross_factor)), jnp.where(is_zero, first[8:16], 0.0)
    )
    cross = dot3(cross, inverse_zero)
    put(0, cross)
    put(3, cross.T)
    sum_zero = dot_split(left_zero, split(rest_zero)) - dot_split(left_zero, parts_zero).T
    sum_zero = dot3(sum_zero - dot3t(mixed, cross_factor), inverse_zero)
    corner_zero = corner(
        spread(-(sum_zero + dot3t(cross_factor, cross)), jnp.where(is_zero, first[0:8], 0.0)),
        heads_ref[2],
        inverse_zero,
    )
    put(1, corner_zero)
    flush(5, 6)


def image_body(place_ref, staged, wait, made, flush, both_ref, strips_ref):
    arrived_ref, rest_ref, high_ref, low_ref, heads_ref, inverse_ref, lines_ref = staged
    *chunk_refs, half_ref = made
    col_place = place_ref[4]
    wait(0, 6)

    def turn(col, carry):
        for low in range(4):
            for half in range(2):
                for (high, group), tile in mirror_tiles(arrived_ref, col, low, half).items():
                    inner = 4 * high + low
                    start = (4 * group + col) * 128 + inner * 2 + half
                    rows = pl.ds(start, 8, stride=16)
                    half_ref[rows, :] = 0.5 * (lines_ref[rows, :] + tile)
                    if group == 0:
                        tile = jnp.where(col < 2, 0.0, tile)
                    if inner == 0:
                        tile = jnp.where(col_place == 0, 0.0, tile)
                    rows = pl.ds((4 * group + col) * 8, 8)
                    both_ref[inner, rows, half * 128 : half * 128 + 128] = tile
        return carry

    lax.fori_loop(0, N_COL, turn, 0)
    flush(4)
    wait(1, 2, 3)
    strips_ref[...] = jnp.zeros_like(strips_ref)

    def product(s, carry):
        strips_ref[...] += dot_split(split(both_ref[s]), (high_ref[s], low_ref[s]))
        return carry

    lax.fori_loop(0, LOC_C, product, 0)
    wait(4, 5)
    scaled_one = dot3(rest_ref[0] - strips_ref[:, :BLK], inverse_ref[1])
    rest_zero = rest_ref[1] - strips_ref[:, BLK:]
    strips_ref[:, :BLK] = scaled_one
    strips_ref[:, BLK:] = dot3(rest_zero - dot3(scaled_one, heads_ref[1]), inverse_ref[0])
    for d in range(4):
        kind = (col_place + d) & 3
        for s in range(LOC_C):
            tile = strips_ref[pl.ds(pl.multiple_of((4 * s + kind) * 8, 8), 8), :]
            if s == 0:
                tile = jnp.where(kind < 2, 0.0, tile)
            chunk_refs[d][s * 8 : s * 8 + 8, :] = tile
        flush(d)


def strip_body(place_ref, staged, wait, made, flush):
    across_ref, *out_refs = made
    col_place = place_ref[4]
    wait(*range(4))
    strip = (staged[0][...] + staged[1][...]) + (staged[2][...] + staged[3][...])
    for half in range(2):
        tiles = [
            strip[s * 8 : s * 8 + 8, k * BLK + half * 128 : k * BLK + half * 128 + 128]
            for s in range(LOC_C)
            for k in range(2)
        ]
        for sub, tile in enumerate(swap_groups(tiles)):
            across_ref[half * 16 + sub] = tile
    flush(0)
    wait(4)
    total = jnp.sum(staged[4][...], axis=0)
    for d in range(4):
        target = (col_place + d) & 3
        out_refs[d][:STRIP] = jnp.where(target == 0, strip[:, BLK:], strip[:, :BLK])
        for mat in range(2):
            for half in range(2):
                start = mat * 16 + half * 8
                tile = jnp.where(target == 0, total[start : start + 8], total[start + 32 : start + 40])
                rows = slice(STRIP + mat * 8, STRIP + mat * 8 + 8)
                out_refs[d][rows, half * 128 : half * 128 + 128] = tile
        flush(1 + d)


def finish_body(place_ref, staged, wait, made, flush, top_ref):
    half_ref, lines_ref, first_ref, across_ref = staged[:4]
    strips = staged[4:8]
    (out_ref,) = made
    wait(*range(8))
    col_place = place_ref[4]
    is_zero = col_place == 0
    is_one = col_place == 1
    owner = col_place < 2
    for half in range(2):
        turned = across_ref[half * 16 : half * 16 + 16].reshape(128, 128).T
        for s in range(LOC_C):
            for k in range(2):
                start = (s * 2 + k) * 8
                top_ref[k, s, half] = turned[start : start + 8]
    out_ref[...] = half_ref[...]
    for s in range(LOC_C):
        for half in range(2):
            for block in range(2):
                rows = pl.ds(block * 128 + s * 2 + half, 8, stride=16)
                new = lines_ref[rows, :] + top_ref[1 - block, s, half]
                if s == 0:
                    continue
                out_ref[rows, :] = 0.5 * new
    for half in range(2):
        lanes = slice(half * 128, half * 128 + 128)
        part_a, part_b = [
            (strips[0][rows, lanes] + strips[1][rows, lanes])
            + (strips[2][rows, lanes] + strips[3][rows, lanes])
            for rows in (slice(STRIP, STRIP + 8), slice(STRIP + 8, STRIP + 16))
        ]
        zero_rows = pl.ds(half, 8, stride=16)
        own = lines_ref[zero_rows, :]
        out_ref[zero_rows, :] = 0.5 * jnp.where(
            is_zero, part_b, own + jnp.where(is_one, part_b, top_ref[1, 0, half])
        )
        one_rows = pl.ds(128 + half, 8, stride=16)
        own = lines_ref[one_rows, :]
        out_ref[one_rows, :] = jnp.where(
            is_zero,
            half_ref[one_rows, :] + 0.5 * (part_a - own),
            0.5 * jnp.where(is_one, part_a, own + top_ref[0, 0, half]),
        )
        for d in range(4):
            kind = (col_place - d) & 3
            for s in range(LOC_C):
                block = 4 * s + kind
                rows = pl.ds(block * 128 + half, 8, stride=16)
                use = owner if s > 0 else jnp.logical_and(owner, kind > 1)
                change = strips[d][s * 8 : s * 8 + 8, lanes] - first_ref[pl.ds(block * 8, 8), lanes]
                out_ref[rows, :] += jnp.where(use, 0.5 * change, 0.0)
    flush(0)


def ring(first, d):
    pairs = []
    for i in range(N_ROW):
        y, z, core = i >> 3, (i >> 1) & 3, i & 1
        if (core == 0) == first:
            z = (z + d) & 3
        else:
            y = (y + d) & 3
        pairs.append((i, (y * 4 + z) * 2 + core))
    return pairs


def around(piece, first):
    return [piece] + [lax.ppermute(piece, "row", ring(first, d)) for d in RING[1:]]


def to_owners(pieces):
    moved = [
        lax.ppermute(pieces[d], "col", [((t - d) % 4, t) for t in range(2)]) for d in range(1, 4)
    ]
    return [pieces[0]] + moved


def on_device(adjoint, lower_panels, diag_inverse):
    row_place = lax.axis_index("row")
    col_place = lax.axis_index("col")
    place = jnp.stack(
        [row_place, row_place >> 3, (row_place >> 1) & 3, row_place & 1, col_place]
    ).astype(jnp.int32)
    lines = adjoint.reshape(LINES, 128)
    panels = lower_panels.reshape(2, STRIP, BLK)
    by_rows = [panels] + [
        lax.ppermute(panels, "col", [(i, (i + d) % 4) for i in range(4)]) for d in range(1, 4)
    ]
    lead = jnp.stack([piece[:, :RSUB] for piece in by_rows])
    lead_one = lax.dynamic_index_in_dim(lead, (col_place - 1) & 3, 0, False)
    lead_zero = lax.dynamic_index_in_dim(lead, col_place, 0, False)
    lead = jnp.stack([lead_one[1], lead_one[0], lead_zero[0]]).reshape(3, RSUB, 2, 128)
    lead = lead.transpose(0, 2, 1, 3).reshape(1, 6 * RSUB, 128)
    across_core = [(i, i ^ 1) for i in range(N_ROW)]
    same_core = [[2 * chip + core for chip in range(N_CHIP)] for core in range(2)]

    def exchange(value):
        return lax.all_to_all(
            value, "row", split_axis=0, concat_axis=0, tiled=True, axis_index_groups=same_core
        )

    ring_one = jnp.concatenate(around(panels.reshape(PIECE, BLK), True), axis=0)
    plane = around(ring_one, False)
    leads = exchange(jnp.broadcast_to(lead, (N_CHIP, 6 * RSUB, 128)))
    later, ring_one = lax.optimization_barrier((place, ring_one))
    lines_shape = shape(LINES, 128)
    (outgoing,) = call(
        pack_body,
        [lines_shape],
        [lines_shape],
        scratch=[pltpu.VMEM((2, LOC_C, BLK, 128), F32)],
        size=2**24,
    )(later, lines)
    outgoing, *plane = lax.optimization_barrier((outgoing, *plane))
    arrived = lax.all_to_all(
        outgoing.reshape(N_ROW * N_COL, 32, 128), ("row", "col"), split_axis=0, concat_axis=0, tiled=True
    ).reshape(LINES, 128)
    plane = plane + [lax.ppermute(part, "row", across_core) for part in plane]
    leads = [leads, lax.ppermute(leads, "row", across_core)]

    direct_ins = [lines, *plane, diag_inverse, *by_rows, *leads]
    split_shape = shape(LOC_C, BLK, 2 * BLK, dtype=BF16)
    square_shape = pltpu.VMEM((BLK, BLK), F32)
    pair_shape = pltpu.VMEM((2, BLK, BLK), F32)
    wide_shape = pltpu.VMEM((LOC_C, BLK, BLK), F32)
    rest, high, low, heads, first, corners, given = call(
        direct_body,
        [
            shape(2, BLK, BLK), split_shape, split_shape, shape(3, BLK, BLK), shape(BLK, BLK),
            shape(N_CHIP, 64, 128), shape(N_CHIP, 64, 128),
        ],
        direct_ins,
        scratch=[wide_shape, wide_shape, wide_shape, pair_shape, pair_shape, square_shape],
        flops=2**33,
        size=2**24,
    )(place, *direct_ins)
    corners = exchange(corners + lax.ppermute(given, "row", across_core))
    image_ins = [arrived, rest, high, low, heads, diag_inverse, lines]
    *chunks, half = call(
        image_body,
        [shape(STRIP, 2 * BLK)] * 4 + [lines_shape],
        image_ins,
        scratch=[wide_shape, pltpu.VMEM((ROWS, 2 * BLK), F32)],
        flops=2**32,
        size=2**24,
    )(place, *image_ins)
    strips = [chunks[0]] + [
        lax.ppermute(chunks[d], "col", [(i, (i + d) % 4) for i in range(4)]) for d in range(1, 4)
    ]
    strip_ins = [*strips, corners]
    across, *strips = call(
        strip_body,
        [shape(N_ROW, RSUB, 128)] + [shape(STRIP + 2 * RSUB, BLK)] * 4,
        strip_ins,
        size=2**21,
    )(place, *strip_ins)
    across = lax.all_to_all(across, "row", split_axis=0, concat_axis=0, tiled=True)
    strips = to_owners(strips)
    finish_ins = [half, lines, first, across, *strips]
    (result,) = call(
        finish_body,
        [lines_shape],
        finish_ins,
        scratch=[pltpu.VMEM((2, LOC_C, 2, RSUB, 128), F32)],
        heads={1: 2 * 128},
        size=2**23,
    )(place, *finish_ins)
    return result.reshape(NBLK, 1, RSUB, LOC_C, 1, BLK)


def solution(mesh):
    return jax.shard_map(
        on_device,
        mesh=mesh,
        in_specs=(
            P(None, "row", None, None, "col", None),
            P(None, None, "col", "row", None, None),
            P(),
        ),
        out_specs=P(None, "row", None, None, "col", None),
        check_vma=False,
    )
```

```python
import jax
import jax.numpy as jnp
from jax import lax
from jax.experimental import pallas as pl
from jax.experimental.pallas import tpu as pltpu
from jax.sharding import PartitionSpec as P

BLK = 256
RSUB = 8
LOC_C = 8
N_ROW = 32
N_COL = 4
NBLK = 32
ROWS = NBLK * RSUB
COLS = LOC_C * BLK
LINES = ROWS * COLS // 128
STRIP = LOC_C * RSUB
PIECE = 2 * STRIP
N_CHIP = 16
RING = (0, 1, 3, 2)
F32 = jnp.float32
BF16 = jnp.bfloat16
VMEM_LIMIT = 56 * 1024 * 1024
SMEM = pl.BlockSpec(memory_space=pltpu.SMEM)


def shape(*dims, dtype=F32):
    return jax.ShapeDtypeStruct(dims, dtype)


def call(
    body, outs, ins, scratch=(), heads=None, raw_in=(), raw_out=(), aliases=None, eager=True, flops=0, size=0
):
    count, results = len(ins), len(outs)
    heads = heads or {}
    staged_in = [i for i in range(count) if i not in raw_in]
    staged_out = [i for i in range(results) if i not in raw_out]

    def kernel(*refs):
        refs = list(refs)
        place = refs.pop(0)
        sources, refs = refs[:count], refs[count:]
        targets, refs = refs[:results], refs[results:]
        staged, made = list(sources), list(targets)
        for i in staged_in:
            staged[i] = refs.pop(0)
        for i in staged_out:
            made[i] = refs.pop(0)
        in_sem, out_sem = refs[-2:]
        copies = {
            i: pltpu.make_async_copy(
                sources[i].at[pl.ds(0, heads[i])] if i in heads else sources[i],
                staged[i],
                in_sem.at[i],
            )
            for i in staged_in
        }
        leaving = {
            i: pltpu.make_async_copy(made[i], targets[i], out_sem.at[i]) for i in staged_out
        }

        def begin():
            for copy in copies.values():
                copy.start()

        if eager:
            begin()
        body(
            place,
            staged,
            lambda *which: begin() if which == (None,) else [copies[i].wait() for i in which],
            made,
            lambda *which: [leaving[i].start() for i in which],
            *refs[:-2],
        )
        for copy in leaving.values():
            copy.wait()

    anywhere = pl.BlockSpec(memory_space=pl.ANY)
    return pl.pallas_call(
        kernel,
        out_shape=list(outs),
        in_specs=[SMEM] + [anywhere] * count,
        out_specs=[anywhere] * results,
        scratch_shapes=[
            pltpu.VMEM((heads.get(i, ins[i].shape[0]), *ins[i].shape[1:]), ins[i].dtype)
            for i in staged_in
        ]
        + [pltpu.VMEM(outs[i].shape, outs[i].dtype) for i in staged_out]
        + list(scratch)
        + [pltpu.SemaphoreType.DMA((count,)), pltpu.SemaphoreType.DMA((results,))],
        input_output_aliases=aliases or {},
        compiler_params=pltpu.CompilerParams(vmem_limit_bytes=VMEM_LIMIT),
        cost_estimate=pl.CostEstimate(flops=flops, bytes_accessed=size, transcendentals=0),
    )


def split(value):
    high = value.astype(BF16)
    return high, (value - high.astype(F32)).astype(BF16)


def dot_split(left, right):
    left_high, left_low = left
    right_high, right_low = right

    def one(a, b):
        return jnp.dot(a, b, preferred_element_type=F32)

    return one(left_high, right_high) + (one(left_high, right_low) + one(left_low, right_high))


def dot3(left, right):
    return dot_split(split(left), split(right))


def dot3t(left, right):
    return dot3(left.T, right)


def swap_groups(tiles):
    tiles = list(tiles)
    group = lax.broadcasted_iota(jnp.int32, (8, 128), 1) // 8
    for bit in (1, 2, 4, 8):
        keep = (group & bit) == 0
        for i in range(16):
            if i & bit:
                continue
            a, b = tiles[i], tiles[i | bit]
            tiles[i] = jnp.where(keep, a, pltpu.roll(b, 8 * bit, 1))
            tiles[i | bit] = jnp.where(keep, pltpu.roll(a, 128 - 8 * bit, 1), b)
    return tiles


def pack_body(place_ref, staged, wait, made, flush, lines_ref, turned_ref, packed_ref, in_sem, out_sem):
    (source_ref,), (out_ref,) = staged, made
    arriving = [
        pltpu.make_async_copy(source_ref.at[high], lines_ref.at[high], in_sem.at[high])
        for high in range(2)
    ]
    for copy in arriving:
        copy.start()
    for high in range(2):
        arriving[high].wait()

        def first(group, carry):
            for half in range(2):
                tiles = [
                    lines_ref[high, pl.ds((4 * low + col) * 128 + group * 2 + half, 8, stride=16), :]
                    for col in range(N_COL)
                    for low in range(4)
                ]
                turned = jnp.concatenate(tiles, axis=0).T
                turned_ref[high, group, half * 128 : half * 128 + 128, :] = turned
            return carry

        lax.fori_loop(0, LOC_C, first, 0, unroll=2)
    leaving = []
    for part in range(4):

        def second(index, carry):
            row = part * 8 + index
            tiles = [
                turned_ref[high, group, pl.ds(row * 8, 8), :]
                for high in range(2)
                for group in range(LOC_C)
            ]
            packed_ref[part, pl.ds(index * 128, 128), :] = jnp.concatenate(tiles, axis=0).T
            return carry

        lax.fori_loop(0, 8, second, 0, unroll=4)
        leaving.append(
            pltpu.make_async_copy(packed_ref.at[part], out_ref.at[part], out_sem.at[part])
        )
        leaving[part].start()
    for copy in leaving:
        copy.wait()


def mirror_tiles(piece_ref, low, half):
    tiles = [piece_ref[half * 16 + sub, pl.ds(low * 8, 8), :] for sub in range(16)]
    turned = jnp.concatenate(tiles, axis=0).T
    return {
        (high, group): turned[high * 64 + group * 8 : high * 64 + group * 8 + 8]
        for high in range(2)
        for group in range(LOC_C)
    }


def half_kernel(lines_ref, arrived_ref, out_ref):
    def turn(low, carry):
        for half in range(2):
            for (high, group), tile in mirror_tiles(arrived_ref.at[:, 0], low, half).items():
                rows = pl.ds((4 * high + low) * 2 + half, 8, stride=16)
                out_ref[group, 0, rows, :] = 0.5 * (lines_ref[group, 0, rows, :] + tile)
        return carry

    lax.fori_loop(0, 4, turn, 0, unroll=2)


def half_sum(lines, arrived):
    split_lines = (LOC_C, N_COL, 128, 128)
    block = pl.BlockSpec((LOC_C, 1, 128, 128), lambda i: (0, i, 0, 0))
    return pl.pallas_call(
        half_kernel,
        grid=(N_COL,),
        out_shape=shape(*split_lines),
        in_specs=[block, pl.BlockSpec((N_ROW, 1, 32, 128), lambda i: (0, i, 0, 0))],
        out_specs=block,
        compiler_params=pltpu.CompilerParams(vmem_limit_bytes=VMEM_LIMIT),
        cost_estimate=pl.CostEstimate(flops=0, bytes_accessed=2**24, transcendentals=0),
    )(lines.reshape(split_lines), arrived)


def direct_body(
    place_ref, staged, wait, made, flush, both_ref, one_ref, zero_ref, left_ref, image_ref, square_ref
):
    lines_ref, *pieces = staged[:9]
    inverse_ref = staged[9]
    panels = staged[10:14]
    leads = staged[14:16]
    rest_ref, high_ref, low_ref, heads_ref, first_ref, keep_ref, give_ref = made
    row_y, row_z, core, col_place = (place_ref[i] for i in range(1, 5))
    is_zero = col_place == 0
    is_one = col_place == 1
    mine = pl.ds(pl.multiple_of(place_ref[0] * 8, 8), 8)
    wait(0)

    def gather(block, carry):
        rows = pl.ds(block * 8, 8)
        for inner in range(LOC_C):
            for half in range(2):
                lanes = slice(half * 128, half * 128 + 128)
                own = lines_ref[pl.ds(block * 128 + inner * 2 + half, 8, stride=16), :]
                if inner == 0:
                    first_ref[rows, lanes] = own
                    own = jnp.where(is_zero | is_one, 0.0, own)
                both_ref[inner, rows, lanes] = own
        return carry

    lax.fori_loop(0, NBLK, gather, 0)
    flush(4)
    wait(*range(1, 9))
    for side in range(2):
        moved = core if side == 0 else 1 - core
        for j in range(4):
            for i in range(4):
                place_y = (row_y - jnp.where(moved == 0, RING[j], RING[i])) & 3
                place_z = (row_z - jnp.where(moved == 0, RING[i], RING[j])) & 3
                owner = (place_y * 4 + place_z) * 2 + moved
                rows = pl.ds(pl.multiple_of(owner * 8, 8), 8)
                piece = pieces[4 * side + j]
                for s in range(LOC_C):
                    start = i * PIECE + s * 8
                    zero_ref[s, rows, :] = piece[start : start + 8, :]
                    start = start + STRIP
                    one_ref[s, rows, :] = piece[start : start + 8, :]

    def product(s, carry):
        both = split(both_ref[s])
        panel_one = jnp.where(jnp.logical_and(is_one, s == 0), 0.0, one_ref[s])
        for place, panel in enumerate((panel_one, zero_ref[s])):
            high, low = split(panel)
            lanes = slice(place * BLK, place * BLK + BLK)
            high_ref[s, :, lanes] = high
            low_ref[s, :, lanes] = low
            image_ref[place] += dot_split(both, (high, low))
        return carry

    image_ref[...] = jnp.zeros_like(image_ref)
    lax.fori_loop(0, LOC_C, product, 0)
    flush(1, 2)
    first = first_ref[...]
    image_one, image_zero = image_ref[0], image_ref[1]
    rest_one = jnp.where(is_one, first, 0.0) - image_one
    rest_zero = jnp.where(is_zero, first, 0.0) - image_zero
    rest_ref[0] = rest_one
    rest_ref[1] = rest_zero
    flush(0)

    wait(*range(9, 16))
    for side in range(2):
        moved = core if side == 0 else 1 - core
        for chip in range(N_CHIP):
            rows = pl.ds(pl.multiple_of((chip * 2 + moved) * 8, 8), 8)
            for head in range(3):
                for half in range(2):
                    start = (head * 2 + half) * 8
                    lanes = slice(half * 128, half * 128 + 128)
                    heads_ref[head, rows, lanes] = leads[side][chip, start : start + 8, :]
    flush(3)
    for d in range(4):
        kind = (col_place - d) & 3
        for s in range(LOC_C):
            rows = pl.ds(pl.multiple_of((4 * s + kind) * 8, 8), 8)
            for panel in range(2):
                tile = panels[d][panel, s * 8 : s * 8 + 8, :]
                if s == 0:
                    tile = jnp.where(kind < 2, 0.0, tile)
                left_ref[panel, rows, :] = tile
    row = lax.broadcasted_iota(jnp.int32, (BLK, BLK), 0)
    column = lax.broadcasted_iota(jnp.int32, (BLK, BLK), 1)

    def lower(value):
        return jnp.where(row >= column, value, 0.0)

    def phi(value):
        return jnp.where(row > column, value, jnp.where(row == column, 0.5 * value, 0.0))

    def spread(square, part):
        square_ref[...] = square
        square_ref[mine, :] += part
        return square_ref[...]

    def corner(square, factor, inverse):
        inner = phi(dot3t(factor, lower(square)))
        whole = dot3(dot3t(inverse, inner), inverse)
        return whole + whole.T

    def put(place, value):
        for half in range(2):
            tile = value[:, half * 128 : half * 128 + 128].reshape(N_CHIP, 2, RSUB, 128)
            rows = slice((place * 2 + half) * 8, (place * 2 + half) * 8 + 8)
            keep_ref[:, rows, :] = jnp.where(core == 0, tile[:, 0], tile[:, 1])
            give_ref[:, rows, :] = jnp.where(core == 0, tile[:, 1], tile[:, 0])

    left_one = split(left_ref[1].T)
    left_zero = split(left_ref[0].T)
    parts_one = split(image_one)
    parts_zero = split(image_zero)
    parts_rest = split(rest_one)
    inverse_one, inverse_zero = inverse_ref[1], inverse_ref[0]
    cross_factor = heads_ref[1]
    sum_one = dot_split(left_one, parts_rest) - dot_split(left_one, parts_one).T
    corner_one = corner(
        spread(-dot3(sum_one, inverse_one), jnp.where(is_one, first[8:16], 0.0)),
        heads_ref[0],
        inverse_one,
    )
    put(2, corner_one)
    sum_cross = dot_split(left_zero, parts_rest).T - dot_split(left_one, parts_zero)
    mixed = spread(dot3t(inverse_one, sum_cross), image_zero[8:16])
    cross = spread(
        -(mixed + dot3(corner_one, cross_factor)), jnp.where(is_zero, first[8:16], 0.0)
    )
    cross = dot3(cross, inverse_zero)
    put(0, cross)
    put(3, cross.T)
    sum_zero = dot_split(left_zero, split(rest_zero)) - dot_split(left_zero, parts_zero).T
    sum_zero = dot3(sum_zero - dot3t(mixed, cross_factor), inverse_zero)
    corner_zero = corner(
        spread(-(sum_zero + dot3t(cross_factor, cross)), jnp.where(is_zero, first[0:8], 0.0)),
        heads_ref[2],
        inverse_zero,
    )
    put(1, corner_zero)
    flush(5, 6)


def image_body(
    place_ref, staged, wait, made, flush, arrived_ref, both_ref, strips_ref, in_sem
):
    source_ref, rest_ref, high_ref, low_ref, heads_ref, inverse_ref = staged
    chunk_refs = made
    col_place = place_ref[4]
    arriving = [
        pltpu.make_async_copy(source_ref.at[:, col], arrived_ref.at[col], in_sem.at[col])
        for col in range(N_COL)
    ]
    for copy in arriving:
        copy.start()
    wait(None)
    for col in range(N_COL):
        arriving[col].wait()

        def turn(low, carry):
            for half in range(2):
                tiles = mirror_tiles(arrived_ref.at[col], low, half)
                for (high, group), tile in tiles.items():
                    inner = 4 * high + low
                    if group == 0 and col < 2:
                        tile = jnp.zeros_like(tile)
                    if high == 0:
                        tile = jnp.where(jnp.logical_and(col_place == 0, low == 0), 0.0, tile)
                    rows = slice((4 * group + col) * 8, (4 * group + col) * 8 + 8)
                    both_ref[inner, rows, half * 128 : half * 128 + 128] = tile
            return carry

        lax.fori_loop(0, 4, turn, 0, unroll=2)
    wait(1, 2, 3)
    strips_ref[...] = jnp.zeros_like(strips_ref)

    def product(s, carry):
        strips_ref[...] += dot_split(split(both_ref[s]), (high_ref[s], low_ref[s]))
        return carry

    lax.fori_loop(0, LOC_C, product, 0)
    wait(4, 5)
    scaled_one = dot3(rest_ref[0] - strips_ref[:, :BLK], inverse_ref[1])
    rest_zero = rest_ref[1] - strips_ref[:, BLK:]
    strips_ref[:, :BLK] = scaled_one
    strips_ref[:, BLK:] = dot3(rest_zero - dot3(scaled_one, heads_ref[1]), inverse_ref[0])
    for d in range(4):
        kind = (col_place + d) & 3
        for s in range(LOC_C):
            tile = strips_ref[pl.ds(pl.multiple_of((4 * s + kind) * 8, 8), 8), :]
            if s == 0:
                tile = jnp.where(kind < 2, 0.0, tile)
            chunk_refs[d][s * 8 : s * 8 + 8, :] = tile
        flush(d)


def strip_body(place_ref, staged, wait, made, flush):
    across_ref, *out_refs = made
    col_place = place_ref[4]
    wait(*range(4))
    strip = (staged[0][...] + staged[1][...]) + (staged[2][...] + staged[3][...])
    for half in range(2):
        tiles = [
            strip[s * 8 : s * 8 + 8, k * BLK + half * 128 : k * BLK + half * 128 + 128]
            for s in range(LOC_C)
            for k in range(2)
        ]
        for sub, tile in enumerate(swap_groups(tiles)):
            across_ref[half * 16 + sub] = tile
    flush(0)
    wait(4)
    total = jnp.sum(staged[4][...], axis=0)
    for d in range(4):
        target = (col_place + d) & 3
        out_refs[d][:STRIP] = jnp.where(target == 0, strip[:, BLK:], strip[:, :BLK])
        for mat in range(2):
            for half in range(2):
                start = mat * 16 + half * 8
                tile = jnp.where(target == 0, total[start : start + 8], total[start + 32 : start + 40])
                rows = slice(STRIP + mat * 8, STRIP + mat * 8 + 8)
                out_refs[d][rows, half * 128 : half * 128 + 128] = tile
        flush(1 + d)


def finish_body(
    place_ref, staged, wait, made, flush, top_ref, edge_ref, head_ref, edge_sem, out_sem
):
    half_ref, lines_ref, first_ref, across_ref = staged[:4]
    strips = staged[4:8]
    (out_ref,) = made
    edge = half_ref.at[:, pl.ds(0, 8), :]
    reading = pltpu.make_async_copy(edge, edge_ref, edge_sem)
    reading.start()
    col_place = place_ref[4]
    is_zero = col_place == 0
    is_one = col_place == 1
    owner = col_place < 2
    wait(1, 3)
    for half in range(2):
        turned = across_ref[half * 16 : half * 16 + 16].reshape(128, 128).T
        for s in range(LOC_C):
            for k in range(2):
                top_ref[k, s, half] = turned[(s * 2 + k) * 8 : (s * 2 + k) * 8 + 8]
    for s in range(1, LOC_C):
        for half in range(2):
            for block in range(2):
                rows = pl.ds(block * 128 + s * 2 + half, 8, stride=16)
                new = lines_ref[rows, :] + top_ref[1 - block, s, half]
                head_ref[block * 8 : block * 8 + 8, s * 2 + half, :] = 0.5 * new
    reading.wait()
    wait(2, 4, 5, 6, 7)
    for half in range(2):
        lanes = slice(half * 128, half * 128 + 128)
        part_a, part_b = [
            (strips[0][rows, lanes] + strips[1][rows, lanes])
            + (strips[2][rows, lanes] + strips[3][rows, lanes])
            for rows in (slice(STRIP, STRIP + 8), slice(STRIP + 8, STRIP + 16))
        ]
        own = lines_ref[pl.ds(half, 8, stride=16), :]
        head_ref[0:8, half, :] = 0.5 * jnp.where(
            is_zero, part_b, own + jnp.where(is_one, part_b, top_ref[1, 0, half])
        )
        own = lines_ref[pl.ds(128 + half, 8, stride=16), :]
        head_ref[8:16, half, :] = jnp.where(
            is_zero,
            edge_ref[8:16, half, :] + 0.5 * (part_a - own),
            0.5 * jnp.where(is_one, part_a, own + top_ref[0, 0, half]),
        )
        for d in range(4):
            kind = (col_place - d) & 3
            for s in range(LOC_C):
                rows = pl.ds(pl.multiple_of((4 * s + kind) * 8, 8), 8)
                change = 0.5 * (strips[d][s * 8 : s * 8 + 8, lanes] - first_ref[rows, lanes])
                edge_ref[rows, half, :] += jnp.where(owner, change, 0.0)
    writing = [
        pltpu.make_async_copy(head_ref, out_ref.at[pl.ds(0, 16)], out_sem.at[0]),
        pltpu.make_async_copy(
            edge_ref.at[pl.ds(16, ROWS - 16)],
            out_ref.at[pl.ds(16, ROWS - 16), pl.ds(0, 8), :],
            out_sem.at[1],
        ),
    ]
    for copy in writing:
        copy.start()
    for copy in writing:
        copy.wait()


def ring(first, d):
    pairs = []
    for i in range(N_ROW):
        y, z, core = i >> 3, (i >> 1) & 3, i & 1
        if (core == 0) == first:
            z = (z + d) & 3
        else:
            y = (y + d) & 3
        pairs.append((i, (y * 4 + z) * 2 + core))
    return pairs


def around(piece, first):
    return [piece] + [lax.ppermute(piece, "row", ring(first, d)) for d in RING[1:]]


def to_owners(pieces):
    moved = [
        lax.ppermute(pieces[d], "col", [((t - d) % 4, t) for t in range(2)]) for d in range(1, 4)
    ]
    return [pieces[0]] + moved


def on_device(adjoint, lower_panels, diag_inverse):
    row_place = lax.axis_index("row")
    col_place = lax.axis_index("col")
    place = jnp.stack(
        [row_place, row_place >> 3, (row_place >> 1) & 3, row_place & 1, col_place]
    ).astype(jnp.int32)
    lines = adjoint.reshape(LINES, 128)
    panels = lower_panels.reshape(2, STRIP, BLK)
    by_rows = [panels] + [
        lax.ppermute(panels, "col", [(i, (i + d) % 4) for i in range(4)]) for d in range(1, 4)
    ]
    lead = jnp.stack([piece[:, :RSUB] for piece in by_rows])
    lead_one = lax.dynamic_index_in_dim(lead, (col_place - 1) & 3, 0, False)
    lead_zero = lax.dynamic_index_in_dim(lead, col_place, 0, False)
    lead = jnp.stack([lead_one[1], lead_one[0], lead_zero[0]]).reshape(3, RSUB, 2, 128)
    lead = lead.transpose(0, 2, 1, 3).reshape(1, 6 * RSUB, 128)
    across_core = [(i, i ^ 1) for i in range(N_ROW)]
    same_core = [[2 * chip + core for chip in range(N_CHIP)] for core in range(2)]

    def exchange(value):
        return lax.all_to_all(
            value, "row", split_axis=0, concat_axis=0, tiled=True, axis_index_groups=same_core
        )

    ring_one = jnp.concatenate(around(panels.reshape(PIECE, BLK), True), axis=0)
    plane = around(ring_one, False)
    leads = exchange(jnp.broadcast_to(lead, (N_CHIP, 6 * RSUB, 128)))
    later, ring_one = lax.optimization_barrier((place, ring_one))
    high_shape = shape(2, LINES // 2, 128)
    part_shape = shape(4, LINES // 4, 128)
    (outgoing,) = call(
        pack_body,
        [part_shape],
        [high_shape],
        scratch=[
            pltpu.VMEM(high_shape.shape, F32),
            pltpu.VMEM((2, LOC_C, BLK, 128), F32),
            pltpu.VMEM(part_shape.shape, F32),
            pltpu.SemaphoreType.DMA((2,)),
            pltpu.SemaphoreType.DMA((4,)),
        ],
        raw_in=(0,),
        raw_out=(0,),
        size=2**24,
    )(later, lines.reshape(high_shape.shape))
    outgoing, *plane = lax.optimization_barrier((outgoing, *plane))
    arrived = lax.all_to_all(
        outgoing.reshape(N_ROW * N_COL, 32, 128), ("row", "col"), split_axis=0, concat_axis=0, tiled=True
    )
    plane = plane + [lax.ppermute(part, "row", across_core) for part in plane]
    leads = [leads, lax.ppermute(leads, "row", across_core)]

    direct_ins = [lines, *plane, diag_inverse, *by_rows, *leads]
    split_shape = shape(LOC_C, BLK, 2 * BLK, dtype=BF16)
    square_shape = pltpu.VMEM((BLK, BLK), F32)
    pair_shape = pltpu.VMEM((2, BLK, BLK), F32)
    wide_shape = pltpu.VMEM((LOC_C, BLK, BLK), F32)
    rest, high, low, heads, first, corners, given = call(
        direct_body,
        [
            shape(2, BLK, BLK), split_shape, split_shape, shape(3, BLK, BLK), shape(BLK, BLK),
            shape(N_CHIP, 64, 128), shape(N_CHIP, 64, 128),
        ],
        direct_ins,
        scratch=[wide_shape, wide_shape, wide_shape, pair_shape, pair_shape, square_shape],
        flops=2**33,
        size=2**24,
    )(place, *direct_ins)
    corners = exchange(corners + lax.ppermute(given, "row", across_core))
    arrived = arrived.reshape(N_ROW, N_COL, 32, 128)
    image_ins = [arrived, rest, high, low, heads, diag_inverse]
    chunks = call(
        image_body,
        [shape(STRIP, 2 * BLK)] * 4,
        image_ins,
        scratch=[
            pltpu.VMEM((N_COL, N_ROW, 32, 128), F32),
            wide_shape,
            pltpu.VMEM((ROWS, 2 * BLK), F32),
            pltpu.SemaphoreType.DMA((N_COL,)),
        ],
        raw_in=(0,),
        eager=False,
        flops=2**32,
        size=2**24,
    )(place, *image_ins)
    arrived, *chunks = lax.optimization_barrier((arrived, *chunks))
    half = half_sum(lines, arrived).reshape(ROWS, 16, 128)
    strips = [chunks[0]] + [
        lax.ppermute(chunks[d], "col", [(i, (i + d) % 4) for i in range(4)]) for d in range(1, 4)
    ]
    half, later = lax.optimization_barrier((half, place))
    strip_ins = [*strips, corners]
    across, *panels = call(
        strip_body,
        [shape(N_ROW, RSUB, 128)] + [shape(STRIP + 2 * RSUB, BLK)] * 4,
        strip_ins,
        size=2**21,
    )(later, *strip_ins)
    across = lax.all_to_all(across, "row", split_axis=0, concat_axis=0, tiled=True)
    panels = to_owners(panels)
    finish_ins = [half, lines, first, across, *panels]
    (result,) = call(
        finish_body,
        [shape(ROWS, 16, 128)],
        finish_ins,
        scratch=[
            pltpu.VMEM((2, LOC_C, 2, RSUB, 128), F32),
            pltpu.VMEM((ROWS, 8, 128), F32),
            pltpu.VMEM((16, 16, 128), F32),
            pltpu.SemaphoreType.DMA,
            pltpu.SemaphoreType.DMA((2,)),
        ],
        heads={1: 2 * 128},
        raw_in=(0,),
        raw_out=(0,),
        aliases={1: 0},
        size=2**23,
    )(place, *finish_ins)
    return result.reshape(NBLK, 1, RSUB, LOC_C, 1, BLK)


def solution(mesh):
    return jax.shard_map(
        on_device,
        mesh=mesh,
        in_specs=(
            P(None, "row", None, None, "col", None),
            P(None, None, "col", "row", None, None),
            P(),
        ),
        out_specs=P(None, "row", None, None, "col", None),
        check_vma=False,
    )
```

```python
import jax
import jax.numpy as jnp
from jax import lax
from jax.experimental import pallas as pl
from jax.experimental.pallas import tpu as pltpu
from jax.sharding import PartitionSpec as P

BLK = 256
RSUB = 8
LOC_C = 8
N_ROW = 32
N_COL = 4
NBLK = 32
ROWS = NBLK * RSUB
COLS = LOC_C * BLK
LINES = ROWS * COLS // 128
STRIP = LOC_C * RSUB
PIECE = 2 * STRIP
N_CHIP = 16
RING = (0, 1, 3, 2)
F32 = jnp.float32
BF16 = jnp.bfloat16
VMEM_LIMIT = 56 * 1024 * 1024
SMEM = pl.BlockSpec(memory_space=pltpu.SMEM)


def shape(*dims, dtype=F32):
    return jax.ShapeDtypeStruct(dims, dtype)


def call(
    body, outs, ins, scratch=(), heads=None, raw_in=(), raw_out=(), aliases=None, eager=True, flops=0, size=0
):
    count, results = len(ins), len(outs)
    heads = heads or {}
    staged_in = [i for i in range(count) if i not in raw_in]
    staged_out = [i for i in range(results) if i not in raw_out]

    def kernel(*refs):
        refs = list(refs)
        place = refs.pop(0)
        sources, refs = refs[:count], refs[count:]
        targets, refs = refs[:results], refs[results:]
        staged, made = list(sources), list(targets)
        for i in staged_in:
            staged[i] = refs.pop(0)
        for i in staged_out:
            made[i] = refs.pop(0)
        in_sem, out_sem = refs[-2:]
        copies = {
            i: pltpu.make_async_copy(
                sources[i].at[pl.ds(0, heads[i])] if i in heads else sources[i],
                staged[i],
                in_sem.at[i],
            )
            for i in staged_in
        }
        leaving = {
            i: pltpu.make_async_copy(made[i], targets[i], out_sem.at[i]) for i in staged_out
        }

        def begin():
            for copy in copies.values():
                copy.start()

        if eager:
            begin()
        body(
            place,
            staged,
            lambda *which: begin() if which == (None,) else [copies[i].wait() for i in which],
            made,
            lambda *which: [leaving[i].start() for i in which],
            *refs[:-2],
        )
        for copy in leaving.values():
            copy.wait()

    anywhere = pl.BlockSpec(memory_space=pl.ANY)
    return pl.pallas_call(
        kernel,
        out_shape=list(outs),
        in_specs=[SMEM] + [anywhere] * count,
        out_specs=[anywhere] * results,
        scratch_shapes=[
            pltpu.VMEM((heads.get(i, ins[i].shape[0]), *ins[i].shape[1:]), ins[i].dtype)
            for i in staged_in
        ]
        + [pltpu.VMEM(outs[i].shape, outs[i].dtype) for i in staged_out]
        + list(scratch)
        + [pltpu.SemaphoreType.DMA((count,)), pltpu.SemaphoreType.DMA((results,))],
        input_output_aliases=aliases or {},
        compiler_params=pltpu.CompilerParams(vmem_limit_bytes=VMEM_LIMIT),
        cost_estimate=pl.CostEstimate(flops=flops, bytes_accessed=size, transcendentals=0),
    )


def split(value):
    high = value.astype(BF16)
    return high, (value - high.astype(F32)).astype(BF16)


def dot_split(left, right):
    left_high, left_low = left
    right_high, right_low = right

    def one(a, b):
        return jnp.dot(a, b, preferred_element_type=F32)

    return one(left_high, right_high) + (one(left_high, right_low) + one(left_low, right_high))


def dot3(left, right):
    return dot_split(split(left), split(right))


def dot3t(left, right):
    return dot3(left.T, right)


def swap_groups(tiles):
    tiles = list(tiles)
    group = lax.broadcasted_iota(jnp.int32, (8, 128), 1) // 8
    for bit in (1, 2, 4, 8):
        keep = (group & bit) == 0
        for i in range(16):
            if i & bit:
                continue
            a, b = tiles[i], tiles[i | bit]
            tiles[i] = jnp.where(keep, a, pltpu.roll(b, 8 * bit, 1))
            tiles[i | bit] = jnp.where(keep, pltpu.roll(a, 128 - 8 * bit, 1), b)
    return tiles


def pack_body(place_ref, staged, wait, made, flush, lines_ref, turned_ref, packed_ref, in_sem, out_sem):
    (source_ref,), (out_ref,) = staged, made
    arriving = [
        pltpu.make_async_copy(source_ref.at[high], lines_ref.at[high], in_sem.at[high])
        for high in range(2)
    ]
    for copy in arriving:
        copy.start()
    for high in range(2):
        arriving[high].wait()

        def first(group, carry):
            for half in range(2):
                tiles = [
                    lines_ref[high, pl.ds((4 * low + col) * 128 + group * 2 + half, 8, stride=16), :]
                    for col in range(N_COL)
                    for low in range(4)
                ]
                turned = jnp.concatenate(tiles, axis=0).T
                turned_ref[high, group, half * 128 : half * 128 + 128, :] = turned
            return carry

        lax.fori_loop(0, LOC_C, first, 0, unroll=2)
    leaving = []
    for part in range(4):

        def second(index, carry):
            row = part * 8 + index
            tiles = [
                turned_ref[high, group, pl.ds(row * 8, 8), :]
                for high in range(2)
                for group in range(LOC_C)
            ]
            packed_ref[part, pl.ds(index * 128, 128), :] = jnp.concatenate(tiles, axis=0).T
            return carry

        lax.fori_loop(0, 8, second, 0, unroll=4)
        leaving.append(
            pltpu.make_async_copy(packed_ref.at[part], out_ref.at[part], out_sem.at[part])
        )
        leaving[part].start()
    for copy in leaving:
        copy.wait()


def mirror_tiles(piece_ref, low, half):
    tiles = [piece_ref[half * 16 + sub, pl.ds(low * 8, 8), :] for sub in range(16)]
    turned = jnp.concatenate(tiles, axis=0).T
    return {
        (high, group): turned[high * 64 + group * 8 : high * 64 + group * 8 + 8]
        for high in range(2)
        for group in range(LOC_C)
    }


def half_kernel(lines_ref, arrived_ref, out_ref):
    def turn(low, carry):
        for half in range(2):
            for (high, group), tile in mirror_tiles(arrived_ref.at[:, 0], low, half).items():
                rows = pl.ds((4 * high + low) * 2 + half, 8, stride=16)
                out_ref[group, 0, rows, :] = 0.5 * (lines_ref[group, 0, rows, :] + tile)
        return carry

    lax.fori_loop(0, 4, turn, 0, unroll=2)


def half_sum(lines, arrived):
    split_lines = (LOC_C, N_COL, 128, 128)
    block = pl.BlockSpec((LOC_C, 1, 128, 128), lambda i: (0, i, 0, 0))
    return pl.pallas_call(
        half_kernel,
        grid=(N_COL,),
        out_shape=shape(*split_lines),
        in_specs=[block, pl.BlockSpec((N_ROW, 1, 32, 128), lambda i: (0, i, 0, 0))],
        out_specs=block,
        compiler_params=pltpu.CompilerParams(vmem_limit_bytes=VMEM_LIMIT),
        cost_estimate=pl.CostEstimate(flops=0, bytes_accessed=2**24, transcendentals=0),
    )(lines.reshape(split_lines), arrived)


def direct_body(
    place_ref, staged, wait, made, flush, both_ref, one_ref, zero_ref, left_ref, image_ref, square_ref
):
    lines_ref, *pieces = staged[:9]
    inverse_ref = staged[9]
    panels = staged[10:14]
    leads = staged[14:16]
    rest_ref, high_ref, low_ref, heads_ref, first_ref, keep_ref, give_ref = made
    row_y, row_z, core, col_place = (place_ref[i] for i in range(1, 5))
    is_zero = col_place == 0
    is_one = col_place == 1
    mine = pl.ds(pl.multiple_of(place_ref[0] * 8, 8), 8)
    wait(0)

    def gather(block, carry):
        rows = pl.ds(block * 8, 8)
        for inner in range(LOC_C):
            for half in range(2):
                lanes = slice(half * 128, half * 128 + 128)
                own = lines_ref[pl.ds(block * 128 + inner * 2 + half, 8, stride=16), :]
                if inner == 0:
                    first_ref[rows, lanes] = own
                    own = jnp.where(is_zero | is_one, 0.0, own)
                both_ref[inner, rows, lanes] = own
        return carry

    lax.fori_loop(0, NBLK, gather, 0)
    flush(4)
    wait(*range(1, 9))
    for side in range(2):
        moved = core if side == 0 else 1 - core
        for j in range(4):
            for i in range(4):
                place_y = (row_y - jnp.where(moved == 0, RING[j], RING[i])) & 3
                place_z = (row_z - jnp.where(moved == 0, RING[i], RING[j])) & 3
                owner = (place_y * 4 + place_z) * 2 + moved
                rows = pl.ds(pl.multiple_of(owner * 8, 8), 8)
                piece = pieces[4 * side + j]
                for s in range(LOC_C):
                    start = i * PIECE + s * 8
                    zero_ref[s, rows, :] = piece[start : start + 8, :]
                    start = start + STRIP
                    one_ref[s, rows, :] = piece[start : start + 8, :]

    def product(s, carry):
        both = split(both_ref[s])
        panel_one = jnp.where(jnp.logical_and(is_one, s == 0), 0.0, one_ref[s])
        for place, panel in enumerate((panel_one, zero_ref[s])):
            high, low = split(panel)
            lanes = slice(place * BLK, place * BLK + BLK)
            high_ref[s, :, lanes] = high
            low_ref[s, :, lanes] = low
            image_ref[place] += dot_split(both, (high, low))
        return carry

    image_ref[...] = jnp.zeros_like(image_ref)
    lax.fori_loop(0, LOC_C, product, 0)
    flush(1, 2)
    first = first_ref[...]
    image_one, image_zero = image_ref[0], image_ref[1]
    rest_one = jnp.where(is_one, first, 0.0) - image_one
    rest_zero = jnp.where(is_zero, first, 0.0) - image_zero
    rest_ref[0] = rest_one
    rest_ref[1] = rest_zero
    flush(0)

    wait(*range(9, 16))
    for side in range(2):
        moved = core if side == 0 else 1 - core
        for chip in range(N_CHIP):
            rows = pl.ds(pl.multiple_of((chip * 2 + moved) * 8, 8), 8)
            for head in range(3):
                for half in range(2):
                    start = (head * 2 + half) * 8
                    lanes = slice(half * 128, half * 128 + 128)
                    heads_ref[head, rows, lanes] = leads[side][chip, start : start + 8, :]
    flush(3)
    for d in range(4):
        kind = (col_place - d) & 3
        for s in range(LOC_C):
            rows = pl.ds(pl.multiple_of((4 * s + kind) * 8, 8), 8)
            for panel in range(2):
                tile = panels[d][panel, s * 8 : s * 8 + 8, :]
                if s == 0:
                    tile = jnp.where(kind < 2, 0.0, tile)
                left_ref[panel, rows, :] = tile
    row = lax.broadcasted_iota(jnp.int32, (BLK, BLK), 0)
    column = lax.broadcasted_iota(jnp.int32, (BLK, BLK), 1)

    def lower(value):
        return jnp.where(row >= column, value, 0.0)

    def phi(value):
        return jnp.where(row > column, value, jnp.where(row == column, 0.5 * value, 0.0))

    def spread(square, part):
        square_ref[...] = square
        square_ref[mine, :] += part
        return square_ref[...]

    def corner(square, factor, inverse):
        inner = phi(dot3t(factor, lower(square)))
        whole = dot3(dot3t(inverse, inner), inverse)
        return whole + whole.T

    def put(place, value):
        for half in range(2):
            tile = value[:, half * 128 : half * 128 + 128].reshape(N_CHIP, 2, RSUB, 128)
            rows = slice((place * 2 + half) * 8, (place * 2 + half) * 8 + 8)
            keep_ref[:, rows, :] = jnp.where(core == 0, tile[:, 0], tile[:, 1])
            give_ref[:, rows, :] = jnp.where(core == 0, tile[:, 1], tile[:, 0])

    left_one = split(left_ref[1].T)
    left_zero = split(left_ref[0].T)
    parts_one = split(image_one)
    parts_zero = split(image_zero)
    parts_rest = split(rest_one)
    inverse_one, inverse_zero = inverse_ref[1], inverse_ref[0]
    cross_factor = heads_ref[1]
    sum_one = dot_split(left_one, parts_rest) - dot_split(left_one, parts_one).T
    corner_one = corner(
        spread(-dot3(sum_one, inverse_one), jnp.where(is_one, first[8:16], 0.0)),
        heads_ref[0],
        inverse_one,
    )
    put(2, corner_one)
    sum_cross = dot_split(left_zero, parts_rest).T - dot_split(left_one, parts_zero)
    mixed = spread(dot3t(inverse_one, sum_cross), image_zero[8:16])
    cross = spread(
        -(mixed + dot3(corner_one, cross_factor)), jnp.where(is_zero, first[8:16], 0.0)
    )
    cross = dot3(cross, inverse_zero)
    put(0, cross)
    put(3, cross.T)
    sum_zero = dot_split(left_zero, split(rest_zero)) - dot_split(left_zero, parts_zero).T
    sum_zero = dot3(sum_zero - dot3t(mixed, cross_factor), inverse_zero)
    corner_zero = corner(
        spread(-(sum_zero + dot3t(cross_factor, cross)), jnp.where(is_zero, first[0:8], 0.0)),
        heads_ref[2],
        inverse_zero,
    )
    put(1, corner_zero)
    flush(5, 6)


def image_body(
    place_ref, staged, wait, made, flush, arrived_ref, both_ref, strips_ref, in_sem
):
    source_ref, rest_ref, high_ref, low_ref, heads_ref, inverse_ref = staged
    chunk_refs = made
    col_place = place_ref[4]
    arriving = [
        pltpu.make_async_copy(source_ref.at[:, col], arrived_ref.at[col], in_sem.at[col])
        for col in range(N_COL)
    ]
    for copy in arriving:
        copy.start()
    wait(None)
    for col in range(N_COL):
        arriving[col].wait()

        def turn(low, carry):
            for half in range(2):
                tiles = mirror_tiles(arrived_ref.at[col], low, half)
                for (high, group), tile in tiles.items():
                    inner = 4 * high + low
                    if group == 0 and col < 2:
                        tile = jnp.zeros_like(tile)
                    if high == 0:
                        tile = jnp.where(jnp.logical_and(col_place == 0, low == 0), 0.0, tile)
                    rows = slice((4 * group + col) * 8, (4 * group + col) * 8 + 8)
                    both_ref[inner, rows, half * 128 : half * 128 + 128] = tile
            return carry

        lax.fori_loop(0, 4, turn, 0, unroll=2)
    wait(1, 2, 3)
    for part in range(2):
        blocks = range(part * 4, part * 4 + 4)
        pairs = [split(both_ref[s]) for s in blocks]
        left = [pair[0] for pair in pairs] * 2 + [pair[1] for pair in pairs]
        right = [high_ref[s] for s in blocks] + [low_ref[s] for s in blocks]
        right += [high_ref[s] for s in blocks]
        product = jnp.dot(
            jnp.concatenate(left, axis=1),
            jnp.concatenate(right, axis=0),
            preferred_element_type=F32,
        )
        strips_ref[...] = product if part == 0 else strips_ref[...] + product
    wait(4, 5)
    scaled_one = dot3(rest_ref[0] - strips_ref[:, :BLK], inverse_ref[1])
    rest_zero = rest_ref[1] - strips_ref[:, BLK:]
    strips_ref[:, :BLK] = scaled_one
    strips_ref[:, BLK:] = dot3(rest_zero - dot3(scaled_one, heads_ref[1]), inverse_ref[0])
    for d in range(4):
        kind = (col_place + d) & 3
        for s in range(LOC_C):
            tile = strips_ref[pl.ds(pl.multiple_of((4 * s + kind) * 8, 8), 8), :]
            if s == 0:
                tile = jnp.where(kind < 2, 0.0, tile)
            chunk_refs[d][s * 8 : s * 8 + 8, :] = tile
        flush(d)


def total_body(place_ref, staged, wait, made, flush):
    wait(0)
    made[0][...] = jnp.sum(staged[0][...], axis=0)
    flush(0)


def strip_body(place_ref, staged, wait, made, flush):
    across_ref, *out_refs = made
    totals_ref = staged[4]
    col_place = place_ref[4]
    wait(*range(4))
    strip = (staged[0][...] + staged[1][...]) + (staged[2][...] + staged[3][...])
    for half in range(2):
        tiles = [
            strip[s * 8 : s * 8 + 8, k * BLK + half * 128 : k * BLK + half * 128 + 128]
            for s in range(LOC_C)
            for k in range(2)
        ]
        for sub, tile in enumerate(swap_groups(tiles)):
            across_ref[half * 16 + sub] = tile
    flush(0)
    wait(4)
    for d in range(4):
        target = (col_place + d) & 3
        out_refs[d][:STRIP] = jnp.where(target == 0, strip[:, BLK:], strip[:, :BLK])
        for mat in range(2):
            for half in range(2):
                start = mat * 16 + half * 8
                tile = jnp.where(
                    target == 0, totals_ref[start : start + 8], totals_ref[start + 32 : start + 40]
                )
                rows = slice(STRIP + mat * 8, STRIP + mat * 8 + 8)
                out_refs[d][rows, half * 128 : half * 128 + 128] = tile
        flush(1 + d)


def finish_body(
    place_ref, staged, wait, made, flush, top_ref, edge_ref, head_ref, edge_sem, out_sem
):
    half_ref, lines_ref, first_ref, across_ref = staged[:4]
    strips = staged[4:8]
    (out_ref,) = made
    edge = half_ref.at[:, pl.ds(0, 8), :]
    reading = pltpu.make_async_copy(edge, edge_ref, edge_sem)
    reading.start()
    col_place = place_ref[4]
    is_zero = col_place == 0
    is_one = col_place == 1
    owner = col_place < 2
    wait(1, 3)
    for half in range(2):
        turned = across_ref[half * 16 : half * 16 + 16].reshape(128, 128).T
        for s in range(LOC_C):
            for k in range(2):
                top_ref[k, s, half] = turned[(s * 2 + k) * 8 : (s * 2 + k) * 8 + 8]
    for s in range(1, LOC_C):
        for half in range(2):
            for block in range(2):
                rows = pl.ds(block * 128 + s * 2 + half, 8, stride=16)
                new = lines_ref[rows, :] + top_ref[1 - block, s, half]
                head_ref[block * 8 : block * 8 + 8, s * 2 + half, :] = 0.5 * new
    reading.wait()
    wait(2, 4, 5, 6, 7)
    for half in range(2):
        lanes = slice(half * 128, half * 128 + 128)
        part_a, part_b = [
            (strips[0][rows, lanes] + strips[1][rows, lanes])
            + (strips[2][rows, lanes] + strips[3][rows, lanes])
            for rows in (slice(STRIP, STRIP + 8), slice(STRIP + 8, STRIP + 16))
        ]
        own = lines_ref[pl.ds(half, 8, stride=16), :]
        head_ref[0:8, half, :] = 0.5 * jnp.where(
            is_zero, part_b, own + jnp.where(is_one, part_b, top_ref[1, 0, half])
        )
        own = lines_ref[pl.ds(128 + half, 8, stride=16), :]
        head_ref[8:16, half, :] = jnp.where(
            is_zero,
            edge_ref[8:16, half, :] + 0.5 * (part_a - own),
            0.5 * jnp.where(is_one, part_a, own + top_ref[0, 0, half]),
        )
        for d in range(4):
            kind = (col_place - d) & 3
            for s in range(LOC_C):
                rows = pl.ds(pl.multiple_of((4 * s + kind) * 8, 8), 8)
                change = 0.5 * (strips[d][s * 8 : s * 8 + 8, lanes] - first_ref[rows, lanes])
                edge_ref[rows, half, :] += jnp.where(owner, change, 0.0)
    writing = [
        pltpu.make_async_copy(head_ref, out_ref.at[pl.ds(0, 16)], out_sem.at[0]),
        pltpu.make_async_copy(
            edge_ref.at[pl.ds(16, ROWS - 16)],
            out_ref.at[pl.ds(16, ROWS - 16), pl.ds(0, 8), :],
            out_sem.at[1],
        ),
    ]
    for copy in writing:
        copy.start()
    for copy in writing:
        copy.wait()


def ring(first, d):
    pairs = []
    for i in range(N_ROW):
        y, z, core = i >> 3, (i >> 1) & 3, i & 1
        if (core == 0) == first:
            z = (z + d) & 3
        else:
            y = (y + d) & 3
        pairs.append((i, (y * 4 + z) * 2 + core))
    return pairs


def around(piece, first):
    return [piece] + [lax.ppermute(piece, "row", ring(first, d)) for d in RING[1:]]


def to_owners(pieces):
    moved = [
        lax.ppermute(pieces[d], "col", [((t - d) % 4, t) for t in range(2)]) for d in range(1, 4)
    ]
    return [pieces[0]] + moved


def on_device(adjoint, lower_panels, diag_inverse):
    row_place = lax.axis_index("row")
    col_place = lax.axis_index("col")
    place = jnp.stack(
        [row_place, row_place >> 3, (row_place >> 1) & 3, row_place & 1, col_place]
    ).astype(jnp.int32)
    lines = adjoint.reshape(LINES, 128)
    panels = lower_panels.reshape(2, STRIP, BLK)
    by_rows = [panels] + [
        lax.ppermute(panels, "col", [(i, (i + d) % 4) for i in range(4)]) for d in range(1, 4)
    ]
    lead = jnp.stack([piece[:, :RSUB] for piece in by_rows])
    lead_one = lax.dynamic_index_in_dim(lead, (col_place - 1) & 3, 0, False)
    lead_zero = lax.dynamic_index_in_dim(lead, col_place, 0, False)
    lead = jnp.stack([lead_one[1], lead_one[0], lead_zero[0]]).reshape(3, RSUB, 2, 128)
    lead = lead.transpose(0, 2, 1, 3).reshape(1, 6 * RSUB, 128)
    across_core = [(i, i ^ 1) for i in range(N_ROW)]
    same_core = [[2 * chip + core for chip in range(N_CHIP)] for core in range(2)]

    def exchange(value):
        return lax.all_to_all(
            value, "row", split_axis=0, concat_axis=0, tiled=True, axis_index_groups=same_core
        )

    ring_one = jnp.concatenate(around(panels.reshape(PIECE, BLK), True), axis=0)
    plane = around(ring_one, False)
    leads = exchange(jnp.broadcast_to(lead, (N_CHIP, 6 * RSUB, 128)))
    later, ring_one = lax.optimization_barrier((place, ring_one))
    high_shape = shape(2, LINES // 2, 128)
    part_shape = shape(4, LINES // 4, 128)
    (outgoing,) = call(
        pack_body,
        [part_shape],
        [high_shape],
        scratch=[
            pltpu.VMEM(high_shape.shape, F32),
            pltpu.VMEM((2, LOC_C, BLK, 128), F32),
            pltpu.VMEM(part_shape.shape, F32),
            pltpu.SemaphoreType.DMA((2,)),
            pltpu.SemaphoreType.DMA((4,)),
        ],
        raw_in=(0,),
        raw_out=(0,),
        size=2**24,
    )(later, lines.reshape(high_shape.shape))
    outgoing, *plane = lax.optimization_barrier((outgoing, *plane))
    arrived = lax.all_to_all(
        outgoing.reshape(N_ROW * N_COL, 32, 128), ("row", "col"), split_axis=0, concat_axis=0, tiled=True
    )
    plane = plane + [lax.ppermute(part, "row", across_core) for part in plane]
    leads = [leads, lax.ppermute(leads, "row", across_core)]

    direct_ins = [lines, *plane, diag_inverse, *by_rows, *leads]
    split_shape = shape(LOC_C, BLK, 2 * BLK, dtype=BF16)
    square_shape = pltpu.VMEM((BLK, BLK), F32)
    pair_shape = pltpu.VMEM((2, BLK, BLK), F32)
    wide_shape = pltpu.VMEM((LOC_C, BLK, BLK), F32)
    rest, high, low, heads, first, corners, given = call(
        direct_body,
        [
            shape(2, BLK, BLK), split_shape, split_shape, shape(3, BLK, BLK), shape(BLK, BLK),
            shape(N_CHIP, 64, 128), shape(N_CHIP, 64, 128),
        ],
        direct_ins,
        scratch=[wide_shape, wide_shape, wide_shape, pair_shape, pair_shape, square_shape],
        flops=2**33,
        size=2**24,
    )(place, *direct_ins)
    corners = exchange(corners + lax.ppermute(given, "row", across_core))
    arrived = arrived.reshape(N_ROW, N_COL, 32, 128)
    image_ins = [arrived, rest, high, low, heads, diag_inverse]
    chunks = call(
        image_body,
        [shape(STRIP, 2 * BLK)] * 4,
        image_ins,
        scratch=[
            pltpu.VMEM((N_COL, N_ROW, 32, 128), F32),
            wide_shape,
            pltpu.VMEM((ROWS, 2 * BLK), F32),
            pltpu.SemaphoreType.DMA((N_COL,)),
        ],
        raw_in=(0,),
        eager=False,
        flops=2**32,
        size=2**24,
    )(place, *image_ins)
    strips = [chunks[0]] + [
        lax.ppermute(chunks[d], "col", [(i, (i + d) % 4) for i in range(4)]) for d in range(1, 4)
    ]
    corners, *chunks = lax.optimization_barrier((corners, *chunks))
    totals = call(total_body, [shape(64, 128)], [corners], size=2**19)(place, corners)
    strip_ins = [*strips, *totals]
    across, *panels = call(
        strip_body,
        [shape(N_ROW, RSUB, 128)] + [shape(STRIP + 2 * RSUB, BLK)] * 4,
        strip_ins,
        size=2**21,
    )(place, *strip_ins)
    arrived, across = lax.optimization_barrier((arrived, across))
    across = lax.all_to_all(across, "row", split_axis=0, concat_axis=0, tiled=True)
    panels = to_owners(panels)
    half = half_sum(lines, arrived).reshape(ROWS, 16, 128)
    finish_ins = [half, lines, first, across, *panels]
    (result,) = call(
        finish_body,
        [shape(ROWS, 16, 128)],
        finish_ins,
        scratch=[
            pltpu.VMEM((2, LOC_C, 2, RSUB, 128), F32),
            pltpu.VMEM((ROWS, 8, 128), F32),
            pltpu.VMEM((16, 16, 128), F32),
            pltpu.SemaphoreType.DMA,
            pltpu.SemaphoreType.DMA((2,)),
        ],
        heads={1: 2 * 128},
        raw_in=(0,),
        raw_out=(0,),
        aliases={1: 0},
        size=2**23,
    )(place, *finish_ins)
    return result.reshape(NBLK, 1, RSUB, LOC_C, 1, BLK)


def solution(mesh):
    return jax.shard_map(
        on_device,
        mesh=mesh,
        in_specs=(
            P(None, "row", None, None, "col", None),
            P(None, None, "col", "row", None, None),
            P(),
        ),
        out_specs=P(None, "row", None, None, "col", None),
        check_vma=False,
    )
```

```python
import jax
import jax.numpy as jnp
from jax import lax
from jax.experimental import pallas as pl
from jax.experimental.pallas import tpu as pltpu
from jax.sharding import PartitionSpec as P

BLK = 256
RSUB = 8
LOC_C = 8
N_ROW = 32
N_COL = 4
NBLK = 32
ROWS = NBLK * RSUB
COLS = LOC_C * BLK
LINES = ROWS * COLS // 128
STRIP = LOC_C * RSUB
PIECE = 2 * STRIP
N_CHIP = 16
RING = (0, 1, 3, 2)
F32 = jnp.float32
BF16 = jnp.bfloat16
VMEM_LIMIT = 56 * 1024 * 1024
SMEM = pl.BlockSpec(memory_space=pltpu.SMEM)


def shape(*dims, dtype=F32):
    return jax.ShapeDtypeStruct(dims, dtype)


def call(
    body, outs, ins, scratch=(), heads=None, raw_in=(), raw_out=(), aliases=None, eager=True, flops=0, size=0
):
    count, results = len(ins), len(outs)
    heads = heads or {}
    staged_in = [i for i in range(count) if i not in raw_in]
    staged_out = [i for i in range(results) if i not in raw_out]

    def kernel(*refs):
        refs = list(refs)
        place = refs.pop(0)
        sources, refs = refs[:count], refs[count:]
        targets, refs = refs[:results], refs[results:]
        staged, made = list(sources), list(targets)
        for i in staged_in:
            staged[i] = refs.pop(0)
        for i in staged_out:
            made[i] = refs.pop(0)
        in_sem, out_sem = refs[-2:]
        copies = {
            i: pltpu.make_async_copy(
                sources[i].at[pl.ds(0, heads[i])] if i in heads else sources[i],
                staged[i],
                in_sem.at[i],
            )
            for i in staged_in
        }
        leaving = {
            i: pltpu.make_async_copy(made[i], targets[i], out_sem.at[i]) for i in staged_out
        }

        def begin():
            for copy in copies.values():
                copy.start()

        if eager:
            begin()
        body(
            place,
            staged,
            lambda *which: begin() if which == (None,) else [copies[i].wait() for i in which],
            made,
            lambda *which: [leaving[i].start() for i in which],
            *refs[:-2],
        )
        for copy in leaving.values():
            copy.wait()

    anywhere = pl.BlockSpec(memory_space=pl.ANY)
    return pl.pallas_call(
        kernel,
        out_shape=list(outs),
        in_specs=[SMEM] + [anywhere] * count,
        out_specs=[anywhere] * results,
        scratch_shapes=[
            pltpu.VMEM((heads.get(i, ins[i].shape[0]), *ins[i].shape[1:]), ins[i].dtype)
            for i in staged_in
        ]
        + [pltpu.VMEM(outs[i].shape, outs[i].dtype) for i in staged_out]
        + list(scratch)
        + [pltpu.SemaphoreType.DMA((count,)), pltpu.SemaphoreType.DMA((results,))],
        input_output_aliases=aliases or {},
        compiler_params=pltpu.CompilerParams(vmem_limit_bytes=VMEM_LIMIT),
        cost_estimate=pl.CostEstimate(flops=flops, bytes_accessed=size, transcendentals=0),
    )


def split(value):
    high = value.astype(BF16)
    return high, (value - high.astype(F32)).astype(BF16)


def dot_split(left, right):
    left_high, left_low = left
    right_high, right_low = right
    return jnp.dot(
        jnp.concatenate([left_high, left_high, left_low], axis=1),
        jnp.concatenate([right_high, right_low, right_high], axis=0),
        preferred_element_type=F32,
    )


def beside(left, right):
    return tuple(jnp.concatenate(pair, axis=1) for pair in zip(left, right))


def dot3(left, right):
    return dot_split(split(left), split(right))


def dot3t(left, right):
    return dot3(left.T, right)


def swap_groups(tiles):
    tiles = list(tiles)
    group = lax.broadcasted_iota(jnp.int32, (8, 128), 1) // 8
    for bit in (1, 2, 4, 8):
        keep = (group & bit) == 0
        for i in range(16):
            if i & bit:
                continue
            a, b = tiles[i], tiles[i | bit]
            tiles[i] = jnp.where(keep, a, pltpu.roll(b, 8 * bit, 1))
            tiles[i | bit] = jnp.where(keep, pltpu.roll(a, 128 - 8 * bit, 1), b)
    return tiles


def pack_body(
    place_ref, staged, wait, made, flush, lines_ref, turned_ref, packed_ref, in_sem, out_sem
):
    (source_ref,), (out_ref, matrix_ref) = staged, made
    arriving = [
        pltpu.make_async_copy(source_ref.at[high], lines_ref.at[high], in_sem.at[high])
        for high in range(2)
    ]
    for copy in arriving:
        copy.start()
    for high in range(2):
        arriving[high].wait()

        def first(group, carry):
            for half in range(2):
                tiles = []
                for col in range(N_COL):
                    for low in range(4):
                        start = (4 * low + col) * 128 + group * 2 + half
                        tile = lines_ref[high, pl.ds(start, 8, stride=16), :]
                        block = 16 * high + 4 * low + col
                        matrix_ref[group, block * 8 : block * 8 + 8, half * 128 : half * 128 + 128] = tile
                        tiles.append(tile)
                turned = jnp.concatenate(tiles, axis=0).T
                turned_ref[high, group, half * 128 : half * 128 + 128, :] = turned
            return carry

        lax.fori_loop(0, LOC_C, first, 0, unroll=2)
    flush(1)
    leaving = []
    for part in range(4):

        def second(index, carry):
            row = part * 8 + index
            tiles = [
                turned_ref[high, group, pl.ds(row * 8, 8), :]
                for high in range(2)
                for group in range(LOC_C)
            ]
            packed_ref[part, pl.ds(index * 128, 128), :] = jnp.concatenate(tiles, axis=0).T
            return carry

        lax.fori_loop(0, 8, second, 0, unroll=4)
        leaving.append(
            pltpu.make_async_copy(packed_ref.at[part], out_ref.at[part], out_sem.at[part])
        )
        leaving[part].start()
    for copy in leaving:
        copy.wait()


def mirror_tiles(piece_ref, low, half):
    tiles = [piece_ref[half * 16 + sub, pl.ds(low * 8, 8), :] for sub in range(16)]
    turned = jnp.concatenate(tiles, axis=0).T
    return {
        (high, group): turned[high * 64 + group * 8 : high * 64 + group * 8 + 8]
        for high in range(2)
        for group in range(LOC_C)
    }


def half_kernel(lines_ref, arrived_ref, out_ref):
    def turn(low, carry):
        for half in range(2):
            for (high, group), tile in mirror_tiles(arrived_ref.at[:, 0], low, half).items():
                rows = pl.ds((4 * high + low) * 2 + half, 8, stride=16)
                out_ref[group, 0, rows, :] = 0.5 * (lines_ref[group, 0, rows, :] + tile)
        return carry

    lax.fori_loop(0, 4, turn, 0, unroll=2)


def half_sum(lines, arrived):
    split_lines = (LOC_C, N_COL, 128, 128)
    block = pl.BlockSpec((LOC_C, 1, 128, 128), lambda i: (0, i, 0, 0))
    return pl.pallas_call(
        half_kernel,
        grid=(N_COL,),
        out_shape=shape(*split_lines),
        in_specs=[block, pl.BlockSpec((N_ROW, 1, 32, 128), lambda i: (0, i, 0, 0))],
        out_specs=block,
        compiler_params=pltpu.CompilerParams(vmem_limit_bytes=VMEM_LIMIT),
        cost_estimate=pl.CostEstimate(flops=0, bytes_accessed=2**24, transcendentals=0),
    )(lines.reshape(split_lines), arrived)


def direct_body(
    place_ref, staged, wait, made, flush, one_ref, zero_ref, left_ref, image_ref, square_ref, heads_ref
):
    matrix_ref, *pieces = staged[:9]
    inverse_ref = staged[9]
    panels = staged[10:14]
    leads = staged[14:16]
    rest_ref, high_ref, low_ref, keep_ref, give_ref = made
    row_y, row_z, core, col_place = (place_ref[i] for i in range(1, 5))
    is_zero = col_place == 0
    is_one = col_place == 1
    mine = pl.ds(pl.multiple_of(place_ref[0] * 8, 8), 8)
    wait(*range(1, 9))
    for side in range(2):
        moved = core if side == 0 else 1 - core
        for j in range(4):
            for i in range(4):
                place_y = (row_y - jnp.where(moved == 0, RING[j], RING[i])) & 3
                place_z = (row_z - jnp.where(moved == 0, RING[i], RING[j])) & 3
                owner = (place_y * 4 + place_z) * 2 + moved
                rows = pl.ds(pl.multiple_of(owner * 8, 8), 8)
                piece = pieces[4 * side + j]
                for s in range(LOC_C):
                    start = i * PIECE + s * 8
                    zero_ref[s, rows, :] = piece[start : start + 8, :]
                    start = start + STRIP
                    one_ref[s, rows, :] = piece[start : start + 8, :]

    wait(*range(9, 16))
    for side in range(2):
        moved = core if side == 0 else 1 - core
        for chip in range(N_CHIP):
            rows = pl.ds(pl.multiple_of((chip * 2 + moved) * 8, 8), 8)
            for head in range(3):
                for half in range(2):
                    start = (head * 2 + half) * 8
                    lanes = slice(half * 128, half * 128 + 128)
                    heads_ref[head, rows, lanes] = leads[side][chip, start : start + 8, :]
    inverse_one, inverse_zero = split(inverse_ref[1]), split(inverse_ref[0])
    cross_factor = heads_ref[1]
    mixer = split(dot3(dot_split(inverse_one, split(cross_factor)), inverse_ref[0]))

    def product(s, carry):
        hidden = jnp.logical_and(s == 0, is_zero | is_one)
        both = split(jnp.where(hidden, 0.0, matrix_ref[s]))
        panel_one = split(jnp.where(jnp.logical_and(is_one, s == 0), 0.0, one_ref[s]))
        panel_zero = split(zero_ref[s])
        product = dot_split(both, beside(panel_one, panel_zero))
        image_ref[0] += product[:, :BLK]
        image_ref[1] += product[:, BLK:]
        scaled = dot_split(panel_one, beside(inverse_one, mixer))
        scaled_zero = dot_split(panel_zero, inverse_zero) - scaled[:, BLK:]
        for place, panel in enumerate((scaled[:, :BLK], scaled_zero)):
            lanes = slice(place * BLK, place * BLK + BLK)
            high_ref[s, :, lanes], low_ref[s, :, lanes] = split(panel)
        return carry

    wait(0)
    image_ref[...] = jnp.zeros_like(image_ref)
    lax.fori_loop(0, LOC_C, product, 0)
    flush(1, 2)
    first = matrix_ref[0]
    image_one, image_zero = image_ref[0], image_ref[1]
    rest_one = jnp.where(is_one, first, 0.0) - image_one
    rest_zero = jnp.where(is_zero, first, 0.0) - image_zero
    scaled_one = dot_split(split(rest_one), inverse_one)
    rest_ref[0] = scaled_one
    rest_ref[1] = dot_split(split(rest_zero - dot3(scaled_one, cross_factor)), inverse_zero)
    flush(0)

    for d in range(4):
        kind = (col_place - d) & 3
        for s in range(LOC_C):
            rows = pl.ds(pl.multiple_of((4 * s + kind) * 8, 8), 8)
            for panel in range(2):
                tile = panels[d][panel, s * 8 : s * 8 + 8, :]
                if s == 0:
                    tile = jnp.where(kind < 2, 0.0, tile)
                left_ref[panel, rows, :] = tile
    row = lax.broadcasted_iota(jnp.int32, (BLK, BLK), 0)
    column = lax.broadcasted_iota(jnp.int32, (BLK, BLK), 1)

    def lower(value):
        return jnp.where(row >= column, value, 0.0)

    def phi(value):
        return jnp.where(row > column, value, jnp.where(row == column, 0.5 * value, 0.0))

    def spread(square, part):
        square_ref[...] = square
        square_ref[mine, :] += part
        return square_ref[...]

    def corner(square, factor, inverse):
        inner = phi(dot3t(factor, lower(square)))
        whole = dot3(dot3t(inverse, inner), inverse)
        return whole + whole.T

    def put(place, value):
        for half in range(2):
            tile = value[:, half * 128 : half * 128 + 128].reshape(N_CHIP, 2, RSUB, 128)
            rows = slice((place * 2 + half) * 8, (place * 2 + half) * 8 + 8)
            keep_ref[:, rows, :] = jnp.where(core == 0, tile[:, 0], tile[:, 1])
            give_ref[:, rows, :] = jnp.where(core == 0, tile[:, 1], tile[:, 0])

    left_one = split(left_ref[1].T)
    left_zero = split(left_ref[0].T)
    parts_one = split(image_one)
    parts_zero = split(image_zero)
    parts_rest = split(rest_one)
    inverse_one, inverse_zero = inverse_ref[1], inverse_ref[0]
    sum_one = dot_split(left_one, parts_rest) - dot_split(left_one, parts_one).T
    corner_one = corner(
        spread(-dot3(sum_one, inverse_one), jnp.where(is_one, first[8:16], 0.0)),
        heads_ref[0],
        inverse_one,
    )
    put(2, corner_one)
    sum_cross = dot_split(left_zero, parts_rest).T - dot_split(left_one, parts_zero)
    mixed = spread(dot3t(inverse_one, sum_cross), image_zero[8:16])
    cross = spread(
        -(mixed + dot3(corner_one, cross_factor)), jnp.where(is_zero, first[8:16], 0.0)
    )
    cross = dot3(cross, inverse_zero)
    put(0, cross)
    put(3, cross.T)
    sum_zero = dot_split(left_zero, split(rest_zero)) - dot_split(left_zero, parts_zero).T
    sum_zero = dot3(sum_zero - dot3t(mixed, cross_factor), inverse_zero)
    corner_zero = corner(
        spread(-(sum_zero + dot3t(cross_factor, cross)), jnp.where(is_zero, first[0:8], 0.0)),
        heads_ref[2],
        inverse_zero,
    )
    put(1, corner_zero)
    flush(3, 4)


def image_body(
    place_ref, staged, wait, made, flush, arrived_ref, both_ref, strips_ref, in_sem
):
    source_ref, rest_ref, high_ref, low_ref = staged
    chunk_refs = made
    col_place = place_ref[4]
    arriving = [
        pltpu.make_async_copy(source_ref.at[:, col], arrived_ref.at[col], in_sem.at[col])
        for col in range(N_COL)
    ]
    for copy in arriving:
        copy.start()
    wait(None)
    for col in range(N_COL):
        arriving[col].wait()

        def turn(low, carry):
            for half in range(2):
                tiles = mirror_tiles(arrived_ref.at[col], low, half)
                for (high, group), tile in tiles.items():
                    inner = 4 * high + low
                    if group == 0 and col < 2:
                        tile = jnp.zeros_like(tile)
                    if high == 0:
                        tile = jnp.where(jnp.logical_and(col_place == 0, low == 0), 0.0, tile)
                    rows = slice((4 * group + col) * 8, (4 * group + col) * 8 + 8)
                    both_ref[inner, rows, half * 128 : half * 128 + 128] = tile
            return carry

        lax.fori_loop(0, 4, turn, 0, unroll=2)
    wait(1, 2, 3)
    for part in range(2):
        blocks = range(part * 4, part * 4 + 4)
        pairs = [split(both_ref[s]) for s in blocks]
        left = [pair[0] for pair in pairs] * 2 + [pair[1] for pair in pairs]
        right = [high_ref[s] for s in blocks] + [low_ref[s] for s in blocks]
        right += [high_ref[s] for s in blocks]
        product = jnp.dot(
            jnp.concatenate(left, axis=1),
            jnp.concatenate(right, axis=0),
            preferred_element_type=F32,
        )
        for panel in range(2):
            lanes = slice(panel * BLK, panel * BLK + BLK)
            base = rest_ref[panel] if part == 0 else strips_ref[:, lanes]
            strips_ref[:, lanes] = base - product[:, lanes]
    for d in range(4):
        kind = (col_place + d) & 3
        for s in range(LOC_C):
            tile = strips_ref[pl.ds(pl.multiple_of((4 * s + kind) * 8, 8), 8), :]
            if s == 0:
                tile = jnp.where(kind < 2, 0.0, tile)
            chunk_refs[d][s * 8 : s * 8 + 8, :] = tile
        flush(d)


def total_body(place_ref, staged, wait, made, flush):
    wait(0)
    made[0][...] = jnp.sum(staged[0][...], axis=0)
    flush(0)


def strip_body(place_ref, staged, wait, made, flush):
    across_ref, *out_refs = made
    totals_ref = staged[4]
    col_place = place_ref[4]
    wait(*range(4))
    strip = (staged[0][...] + staged[1][...]) + (staged[2][...] + staged[3][...])
    for half in range(2):
        tiles = [
            strip[s * 8 : s * 8 + 8, k * BLK + half * 128 : k * BLK + half * 128 + 128]
            for s in range(LOC_C)
            for k in range(2)
        ]
        for sub, tile in enumerate(swap_groups(tiles)):
            across_ref[half * 16 + sub] = tile
    flush(0)
    wait(4)
    for d in range(4):
        target = (col_place + d) & 3
        out_refs[d][:STRIP] = jnp.where(target == 0, strip[:, BLK:], strip[:, :BLK])
        for mat in range(2):
            for half in range(2):
                start = mat * 16 + half * 8
                tile = jnp.where(
                    target == 0, totals_ref[start : start + 8], totals_ref[start + 32 : start + 40]
                )
                rows = slice(STRIP + mat * 8, STRIP + mat * 8 + 8)
                out_refs[d][rows, half * 128 : half * 128 + 128] = tile
        flush(1 + d)


def finish_body(
    place_ref, staged, wait, made, flush, top_ref, edge_ref, head_ref, edge_sem, out_sem
):
    half_ref, lines_ref, first_ref, across_ref = staged[:4]
    strips = staged[4:8]
    (out_ref,) = made
    edge = half_ref.at[:, pl.ds(0, 8), :]
    reading = pltpu.make_async_copy(edge, edge_ref, edge_sem)
    reading.start()
    col_place = place_ref[4]
    is_zero = col_place == 0
    is_one = col_place == 1
    owner = col_place < 2
    wait(1, 3)
    for half in range(2):
        turned = across_ref[half * 16 : half * 16 + 16].reshape(128, 128).T
        for s in range(LOC_C):
            for k in range(2):
                top_ref[k, s, half] = turned[(s * 2 + k) * 8 : (s * 2 + k) * 8 + 8]
    for s in range(1, LOC_C):
        for half in range(2):
            for block in range(2):
                rows = pl.ds(block * 128 + s * 2 + half, 8, stride=16)
                new = lines_ref[rows, :] + top_ref[1 - block, s, half]
                head_ref[block * 8 : block * 8 + 8, s * 2 + half, :] = 0.5 * new
    reading.wait()
    wait(2, 4, 5, 6, 7)
    for half in range(2):
        lanes = slice(half * 128, half * 128 + 128)
        part_a, part_b = [
            (strips[0][rows, lanes] + strips[1][rows, lanes])
            + (strips[2][rows, lanes] + strips[3][rows, lanes])
            for rows in (slice(STRIP, STRIP + 8), slice(STRIP + 8, STRIP + 16))
        ]
        own = lines_ref[pl.ds(half, 8, stride=16), :]
        head_ref[0:8, half, :] = 0.5 * jnp.where(
            is_zero, part_b, own + jnp.where(is_one, part_b, top_ref[1, 0, half])
        )
        own = lines_ref[pl.ds(128 + half, 8, stride=16), :]
        head_ref[8:16, half, :] = jnp.where(
            is_zero,
            edge_ref[8:16, half, :] + 0.5 * (part_a - own),
            0.5 * jnp.where(is_one, part_a, own + top_ref[0, 0, half]),
        )
        for d in range(4):
            kind = (col_place - d) & 3
            for s in range(LOC_C):
                rows = pl.ds(pl.multiple_of((4 * s + kind) * 8, 8), 8)
                change = 0.5 * (strips[d][s * 8 : s * 8 + 8, lanes] - first_ref[0, rows, lanes])
                edge_ref[rows, half, :] += jnp.where(owner, change, 0.0)
    writing = [
        pltpu.make_async_copy(head_ref, out_ref.at[pl.ds(0, 16)], out_sem.at[0]),
        pltpu.make_async_copy(
            edge_ref.at[pl.ds(16, ROWS - 16)],
            out_ref.at[pl.ds(16, ROWS - 16), pl.ds(0, 8), :],
            out_sem.at[1],
        ),
    ]
    for copy in writing:
        copy.start()
    for copy in writing:
        copy.wait()


def ring(first, d):
    pairs = []
    for i in range(N_ROW):
        y, z, core = i >> 3, (i >> 1) & 3, i & 1
        if (core == 0) == first:
            z = (z + d) & 3
        else:
            y = (y + d) & 3
        pairs.append((i, (y * 4 + z) * 2 + core))
    return pairs


def around(piece, first):
    return [piece] + [lax.ppermute(piece, "row", ring(first, d)) for d in RING[1:]]


def to_owners(pieces):
    moved = [
        lax.ppermute(pieces[d], "col", [((t - d) % 4, t) for t in range(2)]) for d in range(1, 4)
    ]
    return [pieces[0]] + moved


def on_device(adjoint, lower_panels, diag_inverse):
    row_place = lax.axis_index("row")
    col_place = lax.axis_index("col")
    place = jnp.stack(
        [row_place, row_place >> 3, (row_place >> 1) & 3, row_place & 1, col_place]
    ).astype(jnp.int32)
    lines = adjoint.reshape(LINES, 128)
    panels = lower_panels.reshape(2, STRIP, BLK)
    by_rows = [panels] + [
        lax.ppermute(panels, "col", [(i, (i + d) % 4) for i in range(4)]) for d in range(1, 4)
    ]
    lead = jnp.stack([piece[:, :RSUB] for piece in by_rows])
    lead_one = lax.dynamic_index_in_dim(lead, (col_place - 1) & 3, 0, False)
    lead_zero = lax.dynamic_index_in_dim(lead, col_place, 0, False)
    lead = jnp.stack([lead_one[1], lead_one[0], lead_zero[0]]).reshape(3, RSUB, 2, 128)
    lead = lead.transpose(0, 2, 1, 3).reshape(1, 6 * RSUB, 128)
    across_core = [(i, i ^ 1) for i in range(N_ROW)]
    same_core = [[2 * chip + core for chip in range(N_CHIP)] for core in range(2)]

    def exchange(value):
        return lax.all_to_all(
            value, "row", split_axis=0, concat_axis=0, tiled=True, axis_index_groups=same_core
        )

    ring_one = jnp.concatenate(around(panels.reshape(PIECE, BLK), True), axis=0)
    plane = around(ring_one, False)
    leads = exchange(jnp.broadcast_to(lead, (N_CHIP, 6 * RSUB, 128)))
    later, ring_one = lax.optimization_barrier((place, ring_one))
    high_shape = shape(2, LINES // 2, 128)
    part_shape = shape(4, LINES // 4, 128)
    wide = shape(LOC_C, ROWS, BLK)
    outgoing, matrix = call(
        pack_body,
        [part_shape, wide],
        [high_shape],
        scratch=[
            pltpu.VMEM(high_shape.shape, F32),
            pltpu.VMEM((2, LOC_C, BLK, 128), F32),
            pltpu.VMEM(part_shape.shape, F32),
            pltpu.SemaphoreType.DMA((2,)),
            pltpu.SemaphoreType.DMA((4,)),
        ],
        raw_in=(0,),
        raw_out=(0,),
        size=2**24,
    )(later, lines.reshape(high_shape.shape))
    outgoing, *plane = lax.optimization_barrier((outgoing, *plane))
    arrived = lax.all_to_all(
        outgoing.reshape(N_ROW * N_COL, 32, 128), ("row", "col"), split_axis=0, concat_axis=0, tiled=True
    )
    plane = plane + [lax.ppermute(part, "row", across_core) for part in plane]
    leads = [leads, lax.ppermute(leads, "row", across_core)]

    direct_ins = [matrix, *plane, diag_inverse, *by_rows, *leads]
    split_shape = shape(LOC_C, BLK, 2 * BLK, dtype=BF16)
    square_shape = pltpu.VMEM((BLK, BLK), F32)
    pair_shape = pltpu.VMEM((2, BLK, BLK), F32)
    wide_shape = pltpu.VMEM((LOC_C, BLK, BLK), F32)
    rest, high, low, corners, given = call(
        direct_body,
        [
            shape(2, BLK, BLK), split_shape, split_shape,
            shape(N_CHIP, 64, 128), shape(N_CHIP, 64, 128),
        ],
        direct_ins,
        scratch=[wide_shape, wide_shape, pair_shape, pair_shape, square_shape, pltpu.VMEM((3, BLK, BLK), F32)],
        flops=2**33,
        size=2**24,
    )(place, *direct_ins)
    corners = exchange(corners + lax.ppermute(given, "row", across_core))
    arrived = arrived.reshape(N_ROW, N_COL, 32, 128)
    image_ins = [arrived, rest, high, low]
    chunks = call(
        image_body,
        [shape(STRIP, 2 * BLK)] * 4,
        image_ins,
        scratch=[
            pltpu.VMEM((N_COL, N_ROW, 32, 128), F32),
            wide_shape,
            pltpu.VMEM((ROWS, 2 * BLK), F32),
            pltpu.SemaphoreType.DMA((N_COL,)),
        ],
        raw_in=(0,),
        eager=False,
        flops=2**32,
        size=2**24,
    )(place, *image_ins)
    strips = [chunks[0]] + [
        lax.ppermute(chunks[d], "col", [(i, (i + d) % 4) for i in range(4)]) for d in range(1, 4)
    ]
    corners, *chunks = lax.optimization_barrier((corners, *chunks))
    totals = call(total_body, [shape(64, 128)], [corners], size=2**19)(place, corners)
    strip_ins = [*strips, *totals]
    across, *panels = call(
        strip_body,
        [shape(N_ROW, RSUB, 128)] + [shape(STRIP + 2 * RSUB, BLK)] * 4,
        strip_ins,
        size=2**21,
    )(place, *strip_ins)
    arrived, across = lax.optimization_barrier((arrived, across))
    across = lax.all_to_all(across, "row", split_axis=0, concat_axis=0, tiled=True)
    panels = to_owners(panels)
    half = half_sum(lines, arrived).reshape(ROWS, 16, 128)
    finish_ins = [half, lines, matrix, across, *panels]
    (result,) = call(
        finish_body,
        [shape(ROWS, 16, 128)],
        finish_ins,
        scratch=[
            pltpu.VMEM((2, LOC_C, 2, RSUB, 128), F32),
            pltpu.VMEM((ROWS, 8, 128), F32),
            pltpu.VMEM((16, 16, 128), F32),
            pltpu.SemaphoreType.DMA,
            pltpu.SemaphoreType.DMA((2,)),
        ],
        heads={1: 2 * 128, 2: 1},
        raw_in=(0,),
        raw_out=(0,),
        aliases={1: 0},
        size=2**23,
    )(place, *finish_ins)
    return result.reshape(NBLK, 1, RSUB, LOC_C, 1, BLK)


def solution(mesh):
    return jax.shard_map(
        on_device,
        mesh=mesh,
        in_specs=(
            P(None, "row", None, None, "col", None),
            P(None, None, "col", "row", None, None),
            P(),
        ),
        out_specs=P(None, "row", None, None, "col", None),
        check_vma=False,
    )
```

```python
import jax
import jax.numpy as jnp
from jax import lax
from jax.experimental import pallas as pl
from jax.experimental.pallas import tpu as pltpu
from jax.sharding import PartitionSpec as P

BLK = 256
RSUB = 8
LOC_C = 8
N_ROW = 32
N_COL = 4
NBLK = 32
ROWS = NBLK * RSUB
COLS = LOC_C * BLK
LINES = ROWS * COLS // 128
STRIP = LOC_C * RSUB
PIECE = 2 * STRIP
N_CHIP = 16
RING = (0, 1, 3, 2)
F32 = jnp.float32
BF16 = jnp.bfloat16
VMEM_LIMIT = 56 * 1024 * 1024
SMALL_LIMIT = 24 * 1024 * 1024
SMEM = pl.BlockSpec(memory_space=pltpu.SMEM)


def shape(*dims, dtype=F32):
    return jax.ShapeDtypeStruct(dims, dtype)


def call(
    body, outs, ins, scratch=(), heads=None, raw_in=(), raw_out=(), near=(), aliases=None, eager=True,
    flops=0, size=0,
):
    count, results = len(ins), len(outs)
    heads = heads or {}
    staged_in = [i for i in range(count) if i not in raw_in and i not in near]
    staged_out = [i for i in range(results) if i not in raw_out]

    def kernel(*refs):
        refs = list(refs)
        place = refs.pop(0)
        sources, refs = refs[:count], refs[count:]
        targets, refs = refs[:results], refs[results:]
        staged, made = list(sources), list(targets)
        for i in staged_in:
            staged[i] = refs.pop(0)
        for i in staged_out:
            made[i] = refs.pop(0)
        in_sem, out_sem = refs[-2:]
        copies = {
            i: pltpu.make_async_copy(
                sources[i].at[pl.ds(0, heads[i])] if i in heads else sources[i],
                staged[i],
                in_sem.at[i],
            )
            for i in staged_in
        }
        leaving = {
            i: pltpu.make_async_copy(made[i], targets[i], out_sem.at[i]) for i in staged_out
        }

        def begin():
            for copy in copies.values():
                copy.start()

        if eager:
            begin()
        body(
            place,
            staged,
            lambda *which: begin()
            if which == (None,)
            else [copies[i].wait() for i in which if i in copies],
            made,
            lambda *which: [leaving[i].start() for i in which],
            *refs[:-2],
        )
        for copy in leaving.values():
            copy.wait()

    anywhere = pl.BlockSpec(memory_space=pl.ANY)
    nearby = pl.BlockSpec(memory_space=pltpu.VMEM)
    return pl.pallas_call(
        kernel,
        out_shape=list(outs),
        in_specs=[SMEM] + [nearby if i in near else anywhere for i in range(count)],
        out_specs=[anywhere] * results,
        scratch_shapes=[
            pltpu.VMEM((heads.get(i, ins[i].shape[0]), *ins[i].shape[1:]), ins[i].dtype)
            for i in staged_in
        ]
        + [pltpu.VMEM(outs[i].shape, outs[i].dtype) for i in staged_out]
        + list(scratch)
        + [pltpu.SemaphoreType.DMA((count,)), pltpu.SemaphoreType.DMA((results,))],
        input_output_aliases=aliases or {},
        compiler_params=pltpu.CompilerParams(vmem_limit_bytes=SMALL_LIMIT if near else VMEM_LIMIT),
        cost_estimate=pl.CostEstimate(flops=flops, bytes_accessed=size, transcendentals=0),
    )


def split(value):
    high = value.astype(BF16)
    return high, (value - high.astype(F32)).astype(BF16)


def dot_split(left, right):
    left_high, left_low = left
    right_high, right_low = right
    return jnp.dot(
        jnp.concatenate([left_high, left_high, left_low], axis=1),
        jnp.concatenate([right_high, right_low, right_high], axis=0),
        preferred_element_type=F32,
    )


def beside(left, right):
    return tuple(jnp.concatenate(pair, axis=1) for pair in zip(left, right))


def dot3(left, right):
    return dot_split(split(left), split(right))


def dot3t(left, right):
    return dot3(left.T, right)


def swap_groups(tiles):
    tiles = list(tiles)
    group = lax.broadcasted_iota(jnp.int32, (8, 128), 1) // 8
    for bit in (1, 2, 4, 8):
        keep = (group & bit) == 0
        for i in range(16):
            if i & bit:
                continue
            a, b = tiles[i], tiles[i | bit]
            tiles[i] = jnp.where(keep, a, pltpu.roll(b, 8 * bit, 1))
            tiles[i | bit] = jnp.where(keep, pltpu.roll(a, 128 - 8 * bit, 1), b)
    return tiles


def pack_body(
    place_ref, staged, wait, made, flush, lines_ref, turned_ref, packed_ref, in_sem, out_sem
):
    (source_ref,), (out_ref, matrix_ref) = staged, made
    arriving = [
        pltpu.make_async_copy(source_ref.at[high], lines_ref.at[high], in_sem.at[high])
        for high in range(2)
    ]
    for copy in arriving:
        copy.start()
    for high in range(2):
        arriving[high].wait()

        def first(group, carry):
            for half in range(2):
                tiles = []
                for col in range(N_COL):
                    for low in range(4):
                        start = (4 * low + col) * 128 + group * 2 + half
                        tile = lines_ref[high, pl.ds(start, 8, stride=16), :]
                        block = 16 * high + 4 * low + col
                        matrix_ref[group, block * 8 : block * 8 + 8, half * 128 : half * 128 + 128] = tile
                        tiles.append(tile)
                turned = jnp.concatenate(tiles, axis=0).T
                turned_ref[high, group, half * 128 : half * 128 + 128, :] = turned
            return carry

        lax.fori_loop(0, LOC_C, first, 0, unroll=2)
    flush(1)
    leaving = []
    for part in range(4):

        def second(index, carry):
            row = part * 8 + index
            tiles = [
                turned_ref[high, group, pl.ds(row * 8, 8), :]
                for high in range(2)
                for group in range(LOC_C)
            ]
            packed_ref[part, pl.ds(index * 128, 128), :] = jnp.concatenate(tiles, axis=0).T
            return carry

        lax.fori_loop(0, 8, second, 0, unroll=4)
        leaving.append(
            pltpu.make_async_copy(packed_ref.at[part], out_ref.at[part], out_sem.at[part])
        )
        leaving[part].start()
    for copy in leaving:
        copy.wait()


def mirror_tiles(piece_ref, low, half):
    tiles = [piece_ref[half * 16 + sub, pl.ds(low * 8, 8), :] for sub in range(16)]
    turned = jnp.concatenate(tiles, axis=0).T
    return {
        (high, group): turned[high * 64 + group * 8 : high * 64 + group * 8 + 8]
        for high in range(2)
        for group in range(LOC_C)
    }


def half_kernel(lines_ref, arrived_ref, out_ref):
    def turn(low, carry):
        for half in range(2):
            for (high, group), tile in mirror_tiles(arrived_ref.at[:, 0], low, half).items():
                rows = pl.ds((4 * high + low) * 2 + half, 8, stride=16)
                out_ref[group, 0, rows, :] = 0.5 * (lines_ref[group, 0, rows, :] + tile)
        return carry

    lax.fori_loop(0, 4, turn, 0, unroll=2)


def half_sum(lines, arrived):
    split_lines = (LOC_C, N_COL, 128, 128)
    block = pl.BlockSpec((LOC_C, 1, 128, 128), lambda i: (0, i, 0, 0))
    return pl.pallas_call(
        half_kernel,
        grid=(N_COL,),
        out_shape=shape(*split_lines),
        in_specs=[block, pl.BlockSpec((N_ROW, 1, 32, 128), lambda i: (0, i, 0, 0))],
        out_specs=block,
        compiler_params=pltpu.CompilerParams(vmem_limit_bytes=VMEM_LIMIT),
        cost_estimate=pl.CostEstimate(flops=0, bytes_accessed=2**24, transcendentals=0),
    )(lines.reshape(split_lines), arrived)


def direct_body(
    place_ref, staged, wait, made, flush, one_ref, zero_ref, left_ref, image_ref, square_ref, heads_ref
):
    matrix_ref, *pieces = staged[:9]
    inverse_ref = staged[9]
    panels = staged[10:14]
    leads = staged[14:16]
    rest_ref, high_ref, low_ref, keep_ref, give_ref = made
    row_y, row_z, core, col_place = (place_ref[i] for i in range(1, 5))
    is_zero = col_place == 0
    is_one = col_place == 1
    mine = pl.ds(pl.multiple_of(place_ref[0] * 8, 8), 8)
    wait(*range(1, 9))
    for side in range(2):
        moved = core if side == 0 else 1 - core
        for j in range(4):
            for i in range(4):
                place_y = (row_y - jnp.where(moved == 0, RING[j], RING[i])) & 3
                place_z = (row_z - jnp.where(moved == 0, RING[i], RING[j])) & 3
                owner = (place_y * 4 + place_z) * 2 + moved
                rows = pl.ds(pl.multiple_of(owner * 8, 8), 8)
                piece = pieces[4 * side + j]
                for s in range(LOC_C):
                    start = i * PIECE + s * 8
                    zero_ref[s, rows, :] = piece[start : start + 8, :]
                    start = start + STRIP
                    one_ref[s, rows, :] = piece[start : start + 8, :]

    wait(*range(9, 16))
    for side in range(2):
        moved = core if side == 0 else 1 - core
        for chip in range(N_CHIP):
            rows = pl.ds(pl.multiple_of((chip * 2 + moved) * 8, 8), 8)
            for head in range(3):
                for half in range(2):
                    start = (head * 2 + half) * 8
                    lanes = slice(half * 128, half * 128 + 128)
                    heads_ref[head, rows, lanes] = leads[side][chip, start : start + 8, :]
    inverse_one, inverse_zero = split(inverse_ref[1]), split(inverse_ref[0])
    cross_factor = heads_ref[1]
    mixer = split(dot3(dot_split(inverse_one, split(cross_factor)), inverse_ref[0]))

    def product(s, carry):
        hidden = jnp.logical_and(s == 0, is_zero | is_one)
        both = split(jnp.where(hidden, 0.0, matrix_ref[s]))
        panel_one = split(jnp.where(jnp.logical_and(is_one, s == 0), 0.0, one_ref[s]))
        panel_zero = split(zero_ref[s])
        product = dot_split(both, beside(panel_one, panel_zero))
        image_ref[0] += product[:, :BLK]
        image_ref[1] += product[:, BLK:]
        scaled = dot_split(panel_one, beside(inverse_one, mixer))
        scaled_zero = dot_split(panel_zero, inverse_zero) - scaled[:, BLK:]
        for place, panel in enumerate((scaled[:, :BLK], scaled_zero)):
            lanes = slice(place * BLK, place * BLK + BLK)
            high_ref[s, :, lanes], low_ref[s, :, lanes] = split(panel)
        return carry

    wait(0)
    image_ref[...] = jnp.zeros_like(image_ref)
    lax.fori_loop(0, LOC_C, product, 0)
    flush(1, 2)
    first = matrix_ref[0]
    image_one, image_zero = image_ref[0], image_ref[1]
    rest_one = jnp.where(is_one, first, 0.0) - image_one
    rest_zero = jnp.where(is_zero, first, 0.0) - image_zero
    scaled_one = dot_split(split(rest_one), inverse_one)
    rest_ref[0] = scaled_one
    rest_ref[1] = dot_split(split(rest_zero - dot3(scaled_one, cross_factor)), inverse_zero)
    flush(0)

    for d in range(4):
        kind = (col_place - d) & 3
        for s in range(LOC_C):
            rows = pl.ds(pl.multiple_of((4 * s + kind) * 8, 8), 8)
            for panel in range(2):
                tile = panels[d][panel, s * 8 : s * 8 + 8, :]
                if s == 0:
                    tile = jnp.where(kind < 2, 0.0, tile)
                left_ref[panel, rows, :] = tile
    row = lax.broadcasted_iota(jnp.int32, (BLK, BLK), 0)
    column = lax.broadcasted_iota(jnp.int32, (BLK, BLK), 1)

    def lower(value):
        return jnp.where(row >= column, value, 0.0)

    def phi(value):
        return jnp.where(row > column, value, jnp.where(row == column, 0.5 * value, 0.0))

    def spread(square, part):
        square_ref[...] = square
        square_ref[mine, :] += part
        return square_ref[...]

    def corner(square, factor, inverse):
        inner = phi(dot3t(factor, lower(square)))
        whole = dot3(dot3t(inverse, inner), inverse)
        return whole + whole.T

    def put(place, value):
        for half in range(2):
            tile = value[:, half * 128 : half * 128 + 128].reshape(N_CHIP, 2, RSUB, 128)
            rows = slice((place * 2 + half) * 8, (place * 2 + half) * 8 + 8)
            keep_ref[:, rows, :] = jnp.where(core == 0, tile[:, 0], tile[:, 1])
            give_ref[:, rows, :] = jnp.where(core == 0, tile[:, 1], tile[:, 0])

    left_one = split(left_ref[1].T)
    left_zero = split(left_ref[0].T)
    parts_one = split(image_one)
    parts_zero = split(image_zero)
    parts_rest = split(rest_one)
    inverse_one, inverse_zero = inverse_ref[1], inverse_ref[0]
    sum_one = dot_split(left_one, parts_rest) - dot_split(left_one, parts_one).T
    corner_one = corner(
        spread(-dot3(sum_one, inverse_one), jnp.where(is_one, first[8:16], 0.0)),
        heads_ref[0],
        inverse_one,
    )
    put(2, corner_one)
    sum_cross = dot_split(left_zero, parts_rest).T - dot_split(left_one, parts_zero)
    mixed = spread(dot3t(inverse_one, sum_cross), image_zero[8:16])
    cross = spread(
        -(mixed + dot3(corner_one, cross_factor)), jnp.where(is_zero, first[8:16], 0.0)
    )
    cross = dot3(cross, inverse_zero)
    put(0, cross)
    put(3, cross.T)
    sum_zero = dot_split(left_zero, split(rest_zero)) - dot_split(left_zero, parts_zero).T
    sum_zero = dot3(sum_zero - dot3t(mixed, cross_factor), inverse_zero)
    corner_zero = corner(
        spread(-(sum_zero + dot3t(cross_factor, cross)), jnp.where(is_zero, first[0:8], 0.0)),
        heads_ref[2],
        inverse_zero,
    )
    put(1, corner_zero)
    flush(3, 4)


def image_body(
    place_ref, staged, wait, made, flush, arrived_ref, both_ref, strips_ref, in_sem
):
    source_ref, rest_ref, high_ref, low_ref = staged
    chunk_refs = made
    col_place = place_ref[4]
    arriving = [
        pltpu.make_async_copy(source_ref.at[:, col], arrived_ref.at[col], in_sem.at[col])
        for col in range(N_COL)
    ]
    for copy in arriving:
        copy.start()
    wait(None)
    for col in range(N_COL):
        arriving[col].wait()

        def turn(low, carry):
            for half in range(2):
                tiles = mirror_tiles(arrived_ref.at[col], low, half)
                for (high, group), tile in tiles.items():
                    inner = 4 * high + low
                    if group == 0 and col < 2:
                        tile = jnp.zeros_like(tile)
                    if high == 0:
                        tile = jnp.where(jnp.logical_and(col_place == 0, low == 0), 0.0, tile)
                    rows = slice((4 * group + col) * 8, (4 * group + col) * 8 + 8)
                    both_ref[inner, rows, half * 128 : half * 128 + 128] = tile
            return carry

        lax.fori_loop(0, 4, turn, 0, unroll=2)
    wait(1, 2, 3)
    for part in range(2):
        blocks = range(part * 4, part * 4 + 4)
        pairs = [split(both_ref[s]) for s in blocks]
        left = [pair[0] for pair in pairs] * 2 + [pair[1] for pair in pairs]
        right = [high_ref[s] for s in blocks] + [low_ref[s] for s in blocks]
        right += [high_ref[s] for s in blocks]
        product = jnp.dot(
            jnp.concatenate(left, axis=1),
            jnp.concatenate(right, axis=0),
            preferred_element_type=F32,
        )
        for panel in range(2):
            lanes = slice(panel * BLK, panel * BLK + BLK)
            base = rest_ref[panel] if part == 0 else strips_ref[:, lanes]
            strips_ref[:, lanes] = base - product[:, lanes]
    for d in range(4):
        kind = (col_place + d) & 3
        for s in range(LOC_C):
            tile = strips_ref[pl.ds(pl.multiple_of((4 * s + kind) * 8, 8), 8), :]
            if s == 0:
                tile = jnp.where(kind < 2, 0.0, tile)
            chunk_refs[d][s * 8 : s * 8 + 8, :] = tile
        flush(d)


def total_body(place_ref, staged, wait, made, flush):
    wait(0)
    made[0][...] = jnp.sum(staged[0][...], axis=0)
    flush(0)


def strip_body(place_ref, staged, wait, made, flush):
    across_ref, *out_refs = made
    totals_ref = staged[4]
    col_place = place_ref[4]
    wait(*range(4))
    strip = (staged[0][...] + staged[1][...]) + (staged[2][...] + staged[3][...])
    for half in range(2):
        tiles = [
            strip[s * 8 : s * 8 + 8, k * BLK + half * 128 : k * BLK + half * 128 + 128]
            for s in range(LOC_C)
            for k in range(2)
        ]
        for sub, tile in enumerate(swap_groups(tiles)):
            across_ref[half * 16 + sub] = tile
    flush(0)
    wait(4)
    for d in range(4):
        target = (col_place + d) & 3
        out_refs[d][:STRIP] = jnp.where(target == 0, strip[:, BLK:], strip[:, :BLK])
        for mat in range(2):
            for half in range(2):
                start = mat * 16 + half * 8
                tile = jnp.where(
                    target == 0, totals_ref[start : start + 8], totals_ref[start + 32 : start + 40]
                )
                rows = slice(STRIP + mat * 8, STRIP + mat * 8 + 8)
                out_refs[d][rows, half * 128 : half * 128 + 128] = tile
        flush(1 + d)


def finish_body(
    place_ref, staged, wait, made, flush, top_ref, edge_ref, head_ref, edge_sem, out_sem
):
    half_ref, lines_ref, first_ref, across_ref = staged[:4]
    strips = staged[4:8]
    (out_ref,) = made
    edge = half_ref.at[:, pl.ds(0, 8), :]
    reading = pltpu.make_async_copy(edge, edge_ref, edge_sem)
    reading.start()
    col_place = place_ref[4]
    is_zero = col_place == 0
    is_one = col_place == 1
    owner = col_place < 2
    wait(1, 3)
    for half in range(2):
        turned = across_ref[half * 16 : half * 16 + 16].reshape(128, 128).T
        for s in range(LOC_C):
            for k in range(2):
                top_ref[k, s, half] = turned[(s * 2 + k) * 8 : (s * 2 + k) * 8 + 8]
    for s in range(1, LOC_C):
        for half in range(2):
            for block in range(2):
                rows = pl.ds(block * 128 + s * 2 + half, 8, stride=16)
                new = lines_ref[rows, :] + top_ref[1 - block, s, half]
                head_ref[block * 8 : block * 8 + 8, s * 2 + half, :] = 0.5 * new
    reading.wait()
    wait(2, 4, 5, 6, 7)
    for half in range(2):
        lanes = slice(half * 128, half * 128 + 128)
        part_a, part_b = [
            (strips[0][rows, lanes] + strips[1][rows, lanes])
            + (strips[2][rows, lanes] + strips[3][rows, lanes])
            for rows in (slice(STRIP, STRIP + 8), slice(STRIP + 8, STRIP + 16))
        ]
        own = lines_ref[pl.ds(half, 8, stride=16), :]
        head_ref[0:8, half, :] = 0.5 * jnp.where(
            is_zero, part_b, own + jnp.where(is_one, part_b, top_ref[1, 0, half])
        )
        own = lines_ref[pl.ds(128 + half, 8, stride=16), :]
        head_ref[8:16, half, :] = jnp.where(
            is_zero,
            edge_ref[8:16, half, :] + 0.5 * (part_a - own),
            0.5 * jnp.where(is_one, part_a, own + top_ref[0, 0, half]),
        )
        for d in range(4):
            kind = (col_place - d) & 3
            for s in range(LOC_C):
                rows = pl.ds(pl.multiple_of((4 * s + kind) * 8, 8), 8)
                change = 0.5 * (strips[d][s * 8 : s * 8 + 8, lanes] - first_ref[rows, lanes])
                edge_ref[rows, half, :] += jnp.where(owner, change, 0.0)
    writing = [
        pltpu.make_async_copy(head_ref, out_ref.at[pl.ds(0, 16)], out_sem.at[0]),
        pltpu.make_async_copy(
            edge_ref.at[pl.ds(16, ROWS - 16)],
            out_ref.at[pl.ds(16, ROWS - 16), pl.ds(0, 8), :],
            out_sem.at[1],
        ),
    ]
    for copy in writing:
        copy.start()
    for copy in writing:
        copy.wait()


def ring(first, d):
    pairs = []
    for i in range(N_ROW):
        y, z, core = i >> 3, (i >> 1) & 3, i & 1
        if (core == 0) == first:
            z = (z + d) & 3
        else:
            y = (y + d) & 3
        pairs.append((i, (y * 4 + z) * 2 + core))
    return pairs


def around(piece, first):
    return [piece] + [lax.ppermute(piece, "row", ring(first, d)) for d in RING[1:]]


def to_owners(pieces):
    moved = [
        lax.ppermute(pieces[d], "col", [((t - d) % 4, t) for t in range(2)]) for d in range(1, 4)
    ]
    return [pieces[0]] + moved


def on_device(adjoint, lower_panels, diag_inverse):
    row_place = lax.axis_index("row")
    col_place = lax.axis_index("col")
    place = jnp.stack(
        [row_place, row_place >> 3, (row_place >> 1) & 3, row_place & 1, col_place]
    ).astype(jnp.int32)
    lines = adjoint.reshape(LINES, 128)
    panels = lower_panels.reshape(2, STRIP, BLK)
    by_rows = [panels] + [
        lax.ppermute(panels, "col", [(i, (i + d) % 4) for i in range(4)]) for d in range(1, 4)
    ]
    lead = jnp.stack([piece[:, :RSUB] for piece in by_rows])
    lead_one = lax.dynamic_index_in_dim(lead, (col_place - 1) & 3, 0, False)
    lead_zero = lax.dynamic_index_in_dim(lead, col_place, 0, False)
    lead = jnp.stack([lead_one[1], lead_one[0], lead_zero[0]]).reshape(3, RSUB, 2, 128)
    lead = lead.transpose(0, 2, 1, 3).reshape(1, 6 * RSUB, 128)
    across_core = [(i, i ^ 1) for i in range(N_ROW)]
    same_core = [[2 * chip + core for chip in range(N_CHIP)] for core in range(2)]

    def exchange(value):
        return lax.all_to_all(
            value, "row", split_axis=0, concat_axis=0, tiled=True, axis_index_groups=same_core
        )

    ring_one = jnp.concatenate(around(panels.reshape(PIECE, BLK), True), axis=0)
    plane = around(ring_one, False)
    leads = exchange(jnp.broadcast_to(lead, (N_CHIP, 6 * RSUB, 128)))
    later, ring_one = lax.optimization_barrier((place, ring_one))
    high_shape = shape(2, LINES // 2, 128)
    part_shape = shape(4, LINES // 4, 128)
    wide = shape(LOC_C, ROWS, BLK)
    outgoing, matrix = call(
        pack_body,
        [part_shape, wide],
        [high_shape],
        scratch=[
            pltpu.VMEM(high_shape.shape, F32),
            pltpu.VMEM((2, LOC_C, BLK, 128), F32),
            pltpu.VMEM(part_shape.shape, F32),
            pltpu.SemaphoreType.DMA((2,)),
            pltpu.SemaphoreType.DMA((4,)),
        ],
        raw_in=(0,),
        raw_out=(0,),
        size=2**24,
    )(later, lines.reshape(high_shape.shape))
    outgoing, *plane = lax.optimization_barrier((outgoing, *plane))
    arrived = lax.all_to_all(
        outgoing.reshape(N_ROW * N_COL, 32, 128), ("row", "col"), split_axis=0, concat_axis=0, tiled=True
    )
    plane = plane + [lax.ppermute(part, "row", across_core) for part in plane]
    leads = [leads, lax.ppermute(leads, "row", across_core)]

    direct_ins = [matrix, *plane, diag_inverse, *by_rows, *leads]
    split_shape = shape(LOC_C, BLK, 2 * BLK, dtype=BF16)
    square_shape = pltpu.VMEM((BLK, BLK), F32)
    pair_shape = pltpu.VMEM((2, BLK, BLK), F32)
    wide_shape = pltpu.VMEM((LOC_C, BLK, BLK), F32)
    rest, high, low, corners, given = call(
        direct_body,
        [
            shape(2, BLK, BLK), split_shape, split_shape,
            shape(N_CHIP, 64, 128), shape(N_CHIP, 64, 128),
        ],
        direct_ins,
        scratch=[wide_shape, wide_shape, pair_shape, pair_shape, square_shape, pltpu.VMEM((3, BLK, BLK), F32)],
        flops=2**33,
        size=2**24,
    )(place, *direct_ins)
    corners = exchange(corners + lax.ppermute(given, "row", across_core))
    arrived = arrived.reshape(N_ROW, N_COL, 32, 128)
    image_ins = [arrived, rest, high, low]
    chunks = call(
        image_body,
        [shape(STRIP, 2 * BLK)] * 4,
        image_ins,
        scratch=[
            pltpu.VMEM((N_COL, N_ROW, 32, 128), F32),
            wide_shape,
            pltpu.VMEM((ROWS, 2 * BLK), F32),
            pltpu.SemaphoreType.DMA((N_COL,)),
        ],
        raw_in=(0,),
        eager=False,
        flops=2**32,
        size=2**24,
    )(place, *image_ins)
    strips = [chunks[0]] + [
        lax.ppermute(chunks[d], "col", [(i, (i + d) % 4) for i in range(4)]) for d in range(1, 4)
    ]
    corners, *chunks = lax.optimization_barrier((corners, *chunks))
    totals = call(total_body, [shape(64, 128)], [corners], near=(0,), size=2**19)(place, corners)
    strip_ins = [*strips, *totals]
    across, *panels = call(
        strip_body,
        [shape(N_ROW, RSUB, 128)] + [shape(STRIP + 2 * RSUB, BLK)] * 4,
        strip_ins,
        near=(1, 2, 3),
        size=2**21,
    )(place, *strip_ins)
    arrived, across = lax.optimization_barrier((arrived, across))
    across = lax.all_to_all(across, "row", split_axis=0, concat_axis=0, tiled=True)
    panels = to_owners(panels)
    half = half_sum(lines, arrived).reshape(ROWS, 16, 128)
    finish_ins = [half, lines, matrix[0], across, *panels]
    (result,) = call(
        finish_body,
        [shape(ROWS, 16, 128)],
        finish_ins,
        scratch=[
            pltpu.VMEM((2, LOC_C, 2, RSUB, 128), F32),
            pltpu.VMEM((ROWS, 8, 128), F32),
            pltpu.VMEM((16, 16, 128), F32),
            pltpu.SemaphoreType.DMA,
            pltpu.SemaphoreType.DMA((2,)),
        ],
        heads={1: 2 * 128},
        near=(3, 5, 6, 7),
        raw_in=(0,),
        raw_out=(0,),
        aliases={1: 0},
        size=2**23,
    )(place, *finish_ins)
    return result.reshape(NBLK, 1, RSUB, LOC_C, 1, BLK)


def solution(mesh):
    return jax.shard_map(
        on_device,
        mesh=mesh,
        in_specs=(
            P(None, "row", None, None, "col", None),
            P(None, None, "col", "row", None, None),
            P(),
        ),
        out_specs=P(None, "row", None, None, "col", None),
        check_vma=False,
    )
```

```python
import jax
import jax.numpy as jnp
from jax import lax
from jax.experimental import pallas as pl
from jax.experimental.pallas import tpu as pltpu
from jax.sharding import PartitionSpec as P

BLK = 256
RSUB = 8
LOC_C = 8
N_ROW = 32
N_COL = 4
NBLK = 32
ROWS = NBLK * RSUB
COLS = LOC_C * BLK
LINES = ROWS * COLS // 128
STRIP = LOC_C * RSUB
PIECE = 2 * STRIP
N_CHIP = 16
RING = (0, 1, 3, 2)
F32 = jnp.float32
BF16 = jnp.bfloat16
VMEM_LIMIT = 56 * 1024 * 1024
SMALL_LIMIT = 24 * 1024 * 1024
SMEM = pl.BlockSpec(memory_space=pltpu.SMEM)


def shape(*dims, dtype=F32):
    return jax.ShapeDtypeStruct(dims, dtype)


def call(
    body, outs, ins, scratch=(), heads=None, raw_in=(), raw_out=(), near=(), aliases=None, eager=True,
    flops=0, size=0,
):
    count, results = len(ins), len(outs)
    heads = heads or {}
    staged_in = [i for i in range(count) if i not in raw_in and i not in near]
    staged_out = [i for i in range(results) if i not in raw_out]

    def kernel(*refs):
        refs = list(refs)
        place = refs.pop(0)
        sources, refs = refs[:count], refs[count:]
        targets, refs = refs[:results], refs[results:]
        staged, made = list(sources), list(targets)
        for i in staged_in:
            staged[i] = refs.pop(0)
        for i in staged_out:
            made[i] = refs.pop(0)
        in_sem, out_sem = refs[-2:]
        copies = {
            i: pltpu.make_async_copy(
                sources[i].at[pl.ds(0, heads[i])] if i in heads else sources[i],
                staged[i],
                in_sem.at[i],
            )
            for i in staged_in
        }
        leaving = {
            i: pltpu.make_async_copy(made[i], targets[i], out_sem.at[i]) for i in staged_out
        }

        def begin():
            for copy in copies.values():
                copy.start()

        if eager:
            begin()
        body(
            place,
            staged,
            lambda *which: begin()
            if which == (None,)
            else [copies[i].wait() for i in which if i in copies],
            made,
            lambda *which: [leaving[i].start() for i in which],
            *refs[:-2],
        )
        for copy in leaving.values():
            copy.wait()

    anywhere = pl.BlockSpec(memory_space=pl.ANY)
    nearby = pl.BlockSpec(memory_space=pltpu.VMEM)
    return pl.pallas_call(
        kernel,
        out_shape=list(outs),
        in_specs=[SMEM] + [nearby if i in near else anywhere for i in range(count)],
        out_specs=[anywhere] * results,
        scratch_shapes=[
            pltpu.VMEM((heads.get(i, ins[i].shape[0]), *ins[i].shape[1:]), ins[i].dtype)
            for i in staged_in
        ]
        + [pltpu.VMEM(outs[i].shape, outs[i].dtype) for i in staged_out]
        + list(scratch)
        + [pltpu.SemaphoreType.DMA((count,)), pltpu.SemaphoreType.DMA((results,))],
        input_output_aliases=aliases or {},
        compiler_params=pltpu.CompilerParams(vmem_limit_bytes=SMALL_LIMIT if near else VMEM_LIMIT),
        cost_estimate=pl.CostEstimate(flops=flops, bytes_accessed=size, transcendentals=0),
    )


def split(value):
    high = value.astype(BF16)
    return high, (value - high.astype(F32)).astype(BF16)


def dot_split(left, right):
    left_high, left_low = left
    right_high, right_low = right
    return jnp.dot(
        jnp.concatenate([left_high, left_high, left_low], axis=1),
        jnp.concatenate([right_high, right_low, right_high], axis=0),
        preferred_element_type=F32,
    )


def beside(left, right):
    return tuple(jnp.concatenate(pair, axis=1) for pair in zip(left, right))


def dot3(left, right):
    return dot_split(split(left), split(right))


def dot3t(left, right):
    return dot3(left.T, right)


def swap_groups(tiles):
    tiles = list(tiles)
    group = lax.broadcasted_iota(jnp.int32, (8, 128), 1) // 8
    for bit in (1, 2, 4, 8):
        keep = (group & bit) == 0
        for i in range(16):
            if i & bit:
                continue
            a, b = tiles[i], tiles[i | bit]
            tiles[i] = jnp.where(keep, a, pltpu.roll(b, 8 * bit, 1))
            tiles[i | bit] = jnp.where(keep, pltpu.roll(a, 128 - 8 * bit, 1), b)
    return tiles


def pack_body(
    place_ref, staged, wait, made, flush, lines_ref, turned_ref, packed_ref, in_sem, out_sem
):
    (source_ref,), (out_ref, matrix_ref) = staged, made
    arriving = [
        pltpu.make_async_copy(source_ref.at[high], lines_ref.at[high], in_sem.at[high])
        for high in range(2)
    ]
    for copy in arriving:
        copy.start()
    for high in range(2):
        arriving[high].wait()

        def first(group, carry):
            for half in range(2):
                tiles = []
                for col in range(N_COL):
                    for low in range(4):
                        start = (4 * low + col) * 128 + group * 2 + half
                        tile = lines_ref[high, pl.ds(start, 8, stride=16), :]
                        block = 16 * high + 4 * low + col
                        matrix_ref[group, block * 8 : block * 8 + 8, half * 128 : half * 128 + 128] = tile
                        tiles.append(tile)
                turned = jnp.concatenate(tiles, axis=0).T
                turned_ref[high, group, half * 128 : half * 128 + 128, :] = turned
            return carry

        lax.fori_loop(0, LOC_C, first, 0, unroll=2)
    flush(1)
    leaving = []
    for part in range(4):

        def second(index, carry):
            row = part * 8 + index
            tiles = [
                turned_ref[high, group, pl.ds(row * 8, 8), :]
                for high in range(2)
                for group in range(LOC_C)
            ]
            packed_ref[part, pl.ds(index * 128, 128), :] = jnp.concatenate(tiles, axis=0).T
            return carry

        lax.fori_loop(0, 8, second, 0, unroll=4)
        leaving.append(
            pltpu.make_async_copy(packed_ref.at[part], out_ref.at[part], out_sem.at[part])
        )
        leaving[part].start()
    for copy in leaving:
        copy.wait()


def mirror_tiles(piece_ref, low, half):
    tiles = [piece_ref[half * 16 + sub, pl.ds(low * 8, 8), :] for sub in range(16)]
    turned = jnp.concatenate(tiles, axis=0).T
    return {
        (high, group): turned[high * 64 + group * 8 : high * 64 + group * 8 + 8]
        for high in range(2)
        for group in range(LOC_C)
    }


def half_kernel(lines_ref, arrived_ref, out_ref):
    def turn(low, carry):
        for half in range(2):
            for (high, group), tile in mirror_tiles(arrived_ref.at[:, 0], low, half).items():
                rows = pl.ds((4 * high + low) * 2 + half, 8, stride=16)
                out_ref[group, 0, rows, :] = 0.5 * (lines_ref[group, 0, rows, :] + tile)
        return carry

    lax.fori_loop(0, 4, turn, 0, unroll=2)


def half_sum(lines, arrived):
    split_lines = (LOC_C, N_COL, 128, 128)
    block = pl.BlockSpec((LOC_C, 1, 128, 128), lambda i: (0, i, 0, 0))
    return pl.pallas_call(
        half_kernel,
        grid=(N_COL,),
        out_shape=shape(*split_lines),
        in_specs=[block, pl.BlockSpec((N_ROW, 1, 32, 128), lambda i: (0, i, 0, 0))],
        out_specs=block,
        compiler_params=pltpu.CompilerParams(vmem_limit_bytes=VMEM_LIMIT),
        cost_estimate=pl.CostEstimate(flops=0, bytes_accessed=2**24, transcendentals=0),
    )(lines.reshape(split_lines), arrived)


def direct_body(
    place_ref, staged, wait, made, flush, one_ref, zero_ref, left_ref, image_ref, square_ref, heads_ref
):
    matrix_ref, *pieces = staged[:9]
    inverse_ref = staged[9]
    panels = staged[10:14]
    leads = staged[14:16]
    rest_ref, high_ref, low_ref, keep_ref, give_ref = made
    row_y, row_z, core, col_place = (place_ref[i] for i in range(1, 5))
    is_zero = col_place == 0
    is_one = col_place == 1
    mine = pl.ds(pl.multiple_of(place_ref[0] * 8, 8), 8)
    wait(*range(1, 9))
    for side in range(2):
        moved = core if side == 0 else 1 - core
        for j in range(4):
            for i in range(4):
                place_y = (row_y - jnp.where(moved == 0, RING[j], RING[i])) & 3
                place_z = (row_z - jnp.where(moved == 0, RING[i], RING[j])) & 3
                owner = (place_y * 4 + place_z) * 2 + moved
                rows = pl.ds(pl.multiple_of(owner * 8, 8), 8)
                piece = pieces[4 * side + j]
                for s in range(LOC_C):
                    start = i * PIECE + s * 8
                    zero_ref[s, rows, :] = piece[start : start + 8, :]
                    start = start + STRIP
                    one_ref[s, rows, :] = piece[start : start + 8, :]

    wait(*range(9, 16))
    for side in range(2):
        moved = core if side == 0 else 1 - core
        for chip in range(N_CHIP):
            rows = pl.ds(pl.multiple_of((chip * 2 + moved) * 8, 8), 8)
            for head in range(3):
                for half in range(2):
                    start = (head * 2 + half) * 8
                    lanes = slice(half * 128, half * 128 + 128)
                    heads_ref[head, rows, lanes] = leads[side][chip, start : start + 8, :]
    inverse_one, inverse_zero = split(inverse_ref[1]), split(inverse_ref[0])
    cross_factor = heads_ref[1]
    mixer = split(dot3(dot_split(inverse_one, split(cross_factor)), inverse_ref[0]))

    def product(s, carry):
        hidden = jnp.logical_and(s == 0, is_zero | is_one)
        both = split(jnp.where(hidden, 0.0, matrix_ref[s]))
        panel_one = split(jnp.where(jnp.logical_and(is_one, s == 0), 0.0, one_ref[s]))
        panel_zero = split(zero_ref[s])
        product = dot_split(both, beside(panel_one, panel_zero))
        image_ref[0] += product[:, :BLK]
        image_ref[1] += product[:, BLK:]
        scaled = dot_split(panel_one, beside(inverse_one, mixer))
        scaled_zero = dot_split(panel_zero, inverse_zero) - scaled[:, BLK:]
        for place, panel in enumerate((scaled[:, :BLK], scaled_zero)):
            lanes = slice(place * BLK, place * BLK + BLK)
            high_ref[s, :, lanes], low_ref[s, :, lanes] = split(panel)
        return carry

    wait(0)
    image_ref[...] = jnp.zeros_like(image_ref)
    lax.fori_loop(0, LOC_C, product, 0)
    flush(1, 2)
    first = matrix_ref[0]
    image_one, image_zero = image_ref[0], image_ref[1]
    rest_one = jnp.where(is_one, first, 0.0) - image_one
    rest_zero = jnp.where(is_zero, first, 0.0) - image_zero
    scaled_one = dot_split(split(rest_one), inverse_one)
    rest_ref[0] = scaled_one
    rest_ref[1] = dot_split(split(rest_zero - dot3(scaled_one, cross_factor)), inverse_zero)
    flush(0)

    for d in range(4):
        kind = (col_place - d) & 3
        for s in range(LOC_C):
            rows = pl.ds(pl.multiple_of((4 * s + kind) * 8, 8), 8)
            for panel in range(2):
                tile = panels[d][panel, s * 8 : s * 8 + 8, :]
                if s == 0:
                    tile = jnp.where(kind < 2, 0.0, tile)
                left_ref[panel, rows, :] = tile
    row = lax.broadcasted_iota(jnp.int32, (BLK, BLK), 0)
    column = lax.broadcasted_iota(jnp.int32, (BLK, BLK), 1)

    def lower(value):
        return jnp.where(row >= column, value, 0.0)

    def phi(value):
        return jnp.where(row > column, value, jnp.where(row == column, 0.5 * value, 0.0))

    def spread(square, part):
        square_ref[...] = square
        square_ref[mine, :] += part
        return square_ref[...]

    def corner(square, factor, inverse):
        inner = phi(dot3t(factor, lower(square)))
        whole = dot3(dot3t(inverse, inner), inverse)
        return whole + whole.T

    def put(place, value):
        for half in range(2):
            tile = value[:, half * 128 : half * 128 + 128].reshape(N_CHIP, 2, RSUB, 128)
            rows = slice((place * 2 + half) * 8, (place * 2 + half) * 8 + 8)
            keep_ref[:, rows, :] = jnp.where(core == 0, tile[:, 0], tile[:, 1])
            give_ref[:, rows, :] = jnp.where(core == 0, tile[:, 1], tile[:, 0])

    left_one = split(left_ref[1].T)
    left_zero = split(left_ref[0].T)
    parts_one = split(image_one)
    parts_zero = split(image_zero)
    parts_rest = split(rest_one)
    inverse_one, inverse_zero = inverse_ref[1], inverse_ref[0]
    sum_one = dot_split(left_one, parts_rest) - dot_split(left_one, parts_one).T
    corner_one = corner(
        spread(-dot3(sum_one, inverse_one), jnp.where(is_one, first[8:16], 0.0)),
        heads_ref[0],
        inverse_one,
    )
    put(2, corner_one)
    sum_cross = dot_split(left_zero, parts_rest).T - dot_split(left_one, parts_zero)
    mixed = spread(dot3t(inverse_one, sum_cross), image_zero[8:16])
    cross = spread(
        -(mixed + dot3(corner_one, cross_factor)), jnp.where(is_zero, first[8:16], 0.0)
    )
    cross = dot3(cross, inverse_zero)
    put(0, cross)
    put(3, cross.T)
    sum_zero = dot_split(left_zero, split(rest_zero)) - dot_split(left_zero, parts_zero).T
    sum_zero = dot3(sum_zero - dot3t(mixed, cross_factor), inverse_zero)
    corner_zero = corner(
        spread(-(sum_zero + dot3t(cross_factor, cross)), jnp.where(is_zero, first[0:8], 0.0)),
        heads_ref[2],
        inverse_zero,
    )
    put(1, corner_zero)
    flush(3, 4)


def image_body(
    place_ref, staged, wait, made, flush, arrived_ref, both_ref, strips_ref, in_sem
):
    source_ref, rest_ref, high_ref, low_ref = staged
    chunk_refs = made
    col_place = place_ref[4]
    arriving = [
        pltpu.make_async_copy(source_ref.at[:, col], arrived_ref.at[col], in_sem.at[col])
        for col in range(N_COL)
    ]
    for copy in arriving:
        copy.start()
    wait(None)
    for col in range(N_COL):
        arriving[col].wait()

        def turn(low, carry):
            for half in range(2):
                tiles = mirror_tiles(arrived_ref.at[col], low, half)
                for (high, group), tile in tiles.items():
                    inner = 4 * high + low
                    if group == 0 and col < 2:
                        tile = jnp.zeros_like(tile)
                    if high == 0:
                        tile = jnp.where(jnp.logical_and(col_place == 0, low == 0), 0.0, tile)
                    rows = slice((4 * group + col) * 8, (4 * group + col) * 8 + 8)
                    both_ref[inner, rows, half * 128 : half * 128 + 128] = tile
            return carry

        lax.fori_loop(0, 4, turn, 0, unroll=2)
    wait(1, 2, 3)
    for part in range(2):
        blocks = range(part * 4, part * 4 + 4)
        pairs = [split(both_ref[s]) for s in blocks]
        left = [pair[0] for pair in pairs] * 2 + [pair[1] for pair in pairs]
        right = [high_ref[s] for s in blocks] + [low_ref[s] for s in blocks]
        right += [high_ref[s] for s in blocks]
        product = jnp.dot(
            jnp.concatenate(left, axis=1),
            jnp.concatenate(right, axis=0),
            preferred_element_type=F32,
        )
        for panel in range(2):
            lanes = slice(panel * BLK, panel * BLK + BLK)
            base = rest_ref[panel] if part == 0 else strips_ref[:, lanes]
            strips_ref[:, lanes] = base - product[:, lanes]
    for d in range(4):
        kind = (col_place + d) & 3
        for s in range(LOC_C):
            tile = strips_ref[pl.ds(pl.multiple_of((4 * s + kind) * 8, 8), 8), :]
            if s == 0:
                tile = jnp.where(kind < 2, 0.0, tile)
            chunk_refs[d][s * 8 : s * 8 + 8, :] = tile
        flush(d)


def total_body(place_ref, staged, wait, made, flush):
    wait(0)
    made[0][...] = jnp.sum(staged[0][...], axis=0)
    flush(0)


def strip_body(place_ref, staged, wait, made, flush):
    across_ref, *out_refs = made
    totals_ref = staged[4]
    col_place = place_ref[4]
    wait(*range(4))
    strip = (staged[0][...] + staged[1][...]) + (staged[2][...] + staged[3][...])
    for half in range(2):
        tiles = [
            strip[s * 8 : s * 8 + 8, k * BLK + half * 128 : k * BLK + half * 128 + 128]
            for s in range(LOC_C)
            for k in range(2)
        ]
        for sub, tile in enumerate(swap_groups(tiles)):
            across_ref[half * 16 + sub] = tile
    flush(0)
    wait(4)
    for d in range(4):
        target = (col_place + d) & 3
        out_refs[d][:STRIP] = jnp.where(target == 0, strip[:, BLK:], strip[:, :BLK])
        for mat in range(2):
            for half in range(2):
                start = mat * 16 + half * 8
                tile = jnp.where(
                    target == 0, totals_ref[start : start + 8], totals_ref[start + 32 : start + 40]
                )
                rows = slice(STRIP + mat * 8, STRIP + mat * 8 + 8)
                out_refs[d][rows, half * 128 : half * 128 + 128] = tile
        flush(1 + d)


def finish_body(
    place_ref, staged, wait, made, flush, top_ref, edge_ref, head_ref, edge_sem, out_sem
):
    half_ref, lines_ref, first_ref, across_ref = staged[:4]
    strips = staged[4:8]
    (out_ref,) = made
    edge = half_ref.at[:, pl.ds(0, 8), :]
    reading = pltpu.make_async_copy(edge, edge_ref, edge_sem)
    reading.start()
    col_place = place_ref[4]
    is_zero = col_place == 0
    is_one = col_place == 1
    owner = col_place < 2
    wait(1, 3)
    for half in range(2):
        turned = across_ref[half * 16 : half * 16 + 16].reshape(128, 128).T
        for s in range(LOC_C):
            for k in range(2):
                top_ref[k, s, half] = turned[(s * 2 + k) * 8 : (s * 2 + k) * 8 + 8]
    for s in range(1, LOC_C):
        for half in range(2):
            for block in range(2):
                rows = pl.ds(block * 128 + s * 2 + half, 8, stride=16)
                new = lines_ref[rows, :] + top_ref[1 - block, s, half]
                head_ref[block * 8 : block * 8 + 8, s * 2 + half, :] = 0.5 * new
    reading.wait()
    wait(2, 4, 5, 6, 7)
    for half in range(2):
        lanes = slice(half * 128, half * 128 + 128)
        part_a, part_b = [
            (strips[0][rows, lanes] + strips[1][rows, lanes])
            + (strips[2][rows, lanes] + strips[3][rows, lanes])
            for rows in (slice(STRIP, STRIP + 8), slice(STRIP + 8, STRIP + 16))
        ]
        own = lines_ref[pl.ds(half, 8, stride=16), :]
        head_ref[0:8, half, :] = 0.5 * jnp.where(
            is_zero, part_b, own + jnp.where(is_one, part_b, top_ref[1, 0, half])
        )
        own = lines_ref[pl.ds(128 + half, 8, stride=16), :]
        head_ref[8:16, half, :] = jnp.where(
            is_zero,
            edge_ref[8:16, half, :] + 0.5 * (part_a - own),
            0.5 * jnp.where(is_one, part_a, own + top_ref[0, 0, half]),
        )
        for d in range(4):
            kind = (col_place - d) & 3
            for s in range(LOC_C):
                rows = pl.ds(pl.multiple_of((4 * s + kind) * 8, 8), 8)
                change = 0.5 * (strips[d][s * 8 : s * 8 + 8, lanes] - first_ref[rows, lanes])
                edge_ref[rows, half, :] += jnp.where(owner, change, 0.0)
    writing = [
        pltpu.make_async_copy(head_ref, out_ref.at[pl.ds(0, 16)], out_sem.at[0]),
        pltpu.make_async_copy(
            edge_ref.at[pl.ds(16, ROWS - 16)],
            out_ref.at[pl.ds(16, ROWS - 16), pl.ds(0, 8), :],
            out_sem.at[1],
        ),
    ]
    for copy in writing:
        copy.start()
    for copy in writing:
        copy.wait()


def ring(first, d):
    pairs = []
    for i in range(N_ROW):
        y, z, core = i >> 3, (i >> 1) & 3, i & 1
        if (core == 0) == first:
            z = (z + d) & 3
        else:
            y = (y + d) & 3
        pairs.append((i, (y * 4 + z) * 2 + core))
    return pairs


def around(piece, first):
    return [piece] + [lax.ppermute(piece, "row", ring(first, d)) for d in RING[1:]]


def to_owners(pieces):
    moved = [
        lax.ppermute(pieces[d], "col", [((t - d) % 4, t) for t in range(2)]) for d in range(1, 4)
    ]
    return [pieces[0]] + moved


def on_device(adjoint, lower_panels, diag_inverse):
    row_place = lax.axis_index("row")
    col_place = lax.axis_index("col")
    place = jnp.stack(
        [row_place, row_place >> 3, (row_place >> 1) & 3, row_place & 1, col_place]
    ).astype(jnp.int32)
    lines = adjoint.reshape(LINES, 128)
    panels = lower_panels.reshape(2, STRIP, BLK)
    by_rows = [panels] + [
        lax.ppermute(panels, "col", [(i, (i + d) % 4) for i in range(4)]) for d in range(1, 4)
    ]
    lead = jnp.stack([piece[:, :RSUB] for piece in by_rows])
    lead_one = lax.dynamic_index_in_dim(lead, (col_place - 1) & 3, 0, False)
    lead_zero = lax.dynamic_index_in_dim(lead, col_place, 0, False)
    lead = jnp.stack([lead_one[1], lead_one[0], lead_zero[0]]).reshape(3, RSUB, 2, 128)
    lead = lead.transpose(0, 2, 1, 3).reshape(1, 6 * RSUB, 128)
    across_core = [(i, i ^ 1) for i in range(N_ROW)]
    same_core = [[2 * chip + core for chip in range(N_CHIP)] for core in range(2)]

    def exchange(value):
        return lax.all_to_all(
            value, "row", split_axis=0, concat_axis=0, tiled=True, axis_index_groups=same_core
        )

    ring_one = jnp.concatenate(around(panels.reshape(PIECE, BLK), True), axis=0)
    plane = around(ring_one, False)
    leads = exchange(jnp.broadcast_to(lead, (N_CHIP, 6 * RSUB, 128)))
    later, ring_one = lax.optimization_barrier((place, ring_one))
    high_shape = shape(2, LINES // 2, 128)
    part_shape = shape(4, LINES // 4, 128)
    wide = shape(LOC_C, ROWS, BLK)
    outgoing, matrix = call(
        pack_body,
        [part_shape, wide],
        [high_shape],
        scratch=[
            pltpu.VMEM(high_shape.shape, F32),
            pltpu.VMEM((2, LOC_C, BLK, 128), F32),
            pltpu.VMEM(part_shape.shape, F32),
            pltpu.SemaphoreType.DMA((2,)),
            pltpu.SemaphoreType.DMA((4,)),
        ],
        raw_in=(0,),
        raw_out=(0,),
        size=2**24,
    )(later, lines.reshape(high_shape.shape))
    outgoing, *plane = lax.optimization_barrier((outgoing, *plane))
    arrived = lax.all_to_all(
        outgoing.reshape(N_ROW * N_COL, 32, 128), ("row", "col"), split_axis=0, concat_axis=0, tiled=True
    )
    plane = plane + [lax.ppermute(part, "row", across_core) for part in plane]
    leads = [leads, lax.ppermute(leads, "row", across_core)]

    direct_ins = [matrix, *plane, diag_inverse, *by_rows, *leads]
    split_shape = shape(LOC_C, BLK, 2 * BLK, dtype=BF16)
    square_shape = pltpu.VMEM((BLK, BLK), F32)
    pair_shape = pltpu.VMEM((2, BLK, BLK), F32)
    wide_shape = pltpu.VMEM((LOC_C, BLK, BLK), F32)
    rest, high, low, corners, given = call(
        direct_body,
        [
            shape(2, BLK, BLK), split_shape, split_shape,
            shape(N_CHIP, 64, 128), shape(N_CHIP, 64, 128),
        ],
        direct_ins,
        scratch=[wide_shape, wide_shape, pair_shape, pair_shape, square_shape, pltpu.VMEM((3, BLK, BLK), F32)],
        flops=2**33,
        size=2**24,
    )(place, *direct_ins)
    corners = exchange(corners + lax.ppermute(given, "row", across_core))
    arrived = arrived.reshape(N_ROW, N_COL, 32, 128)
    image_ins = [arrived, rest, high, low]
    chunks = call(
        image_body,
        [shape(STRIP, 2 * BLK)] * 4,
        image_ins,
        scratch=[
            pltpu.VMEM((N_COL, N_ROW, 32, 128), F32),
            wide_shape,
            pltpu.VMEM((ROWS, 2 * BLK), F32),
            pltpu.SemaphoreType.DMA((N_COL,)),
        ],
        raw_in=(0,),
        eager=False,
        flops=2**32,
        size=2**24,
    )(place, *image_ins)
    strips = [chunks[0]] + [
        lax.ppermute(chunks[d], "col", [(i, (i + d) % 4) for i in range(4)]) for d in range(1, 4)
    ]
    corners, first, *chunks = lax.optimization_barrier((corners, matrix[0], *chunks))
    totals = call(total_body, [shape(64, 128)], [corners], near=(0,), size=2**19)(place, corners)
    strip_ins = [*strips, *totals]
    across, *panels = call(
        strip_body,
        [shape(N_ROW, RSUB, 128)] + [shape(STRIP + 2 * RSUB, BLK)] * 4,
        strip_ins,
        near=(1, 2, 3),
        size=2**21,
    )(place, *strip_ins)
    arrived, across = lax.optimization_barrier((arrived, across))
    across = lax.all_to_all(across, "row", split_axis=0, concat_axis=0, tiled=True)
    panels = to_owners(panels)
    half = half_sum(lines, arrived).reshape(ROWS, 16, 128)
    finish_ins = [half, lines, first, across, *panels]
    (result,) = call(
        finish_body,
        [shape(ROWS, 16, 128)],
        finish_ins,
        scratch=[
            pltpu.VMEM((2, LOC_C, 2, RSUB, 128), F32),
            pltpu.VMEM((ROWS, 8, 128), F32),
            pltpu.VMEM((16, 16, 128), F32),
            pltpu.SemaphoreType.DMA,
            pltpu.SemaphoreType.DMA((2,)),
        ],
        heads={1: 2 * 128},
        near=(3, 5, 6, 7),
        raw_in=(0,),
        raw_out=(0,),
        aliases={1: 0},
        size=2**23,
    )(place, *finish_ins)
    return result.reshape(NBLK, 1, RSUB, LOC_C, 1, BLK)


def solution(mesh):
    return jax.shard_map(
        on_device,
        mesh=mesh,
        in_specs=(
            P(None, "row", None, None, "col", None),
            P(None, None, "col", "row", None, None),
            P(),
        ),
        out_specs=P(None, "row", None, None, "col", None),
        check_vma=False,
    )
```

```python
import jax
import jax.numpy as jnp
from jax import lax
from jax.experimental import pallas as pl
from jax.experimental.pallas import tpu as pltpu
from jax.sharding import PartitionSpec as P

BLK = 256
RSUB = 8
LOC_C = 8
N_ROW = 32
N_COL = 4
NBLK = 32
ROWS = NBLK * RSUB
COLS = LOC_C * BLK
LINES = ROWS * COLS // 128
STRIP = LOC_C * RSUB
PIECE = 2 * STRIP
N_CHIP = 16
RING = (0, 1, 3, 2)
F32 = jnp.float32
BF16 = jnp.bfloat16
VMEM_LIMIT = 56 * 1024 * 1024
SMALL_LIMIT = 24 * 1024 * 1024
SMEM = pl.BlockSpec(memory_space=pltpu.SMEM)


def shape(*dims, dtype=F32):
    return jax.ShapeDtypeStruct(dims, dtype)


def call(
    body, outs, ins, scratch=(), heads=None, raw_in=(), raw_out=(), near=(), limit=0, aliases=None, eager=True,
    flops=0, size=0,
):
    count, results = len(ins), len(outs)
    heads = heads or {}
    staged_in = [i for i in range(count) if i not in raw_in and i not in near]
    staged_out = [i for i in range(results) if i not in raw_out]

    def kernel(*refs):
        refs = list(refs)
        place = refs.pop(0)
        sources, refs = refs[:count], refs[count:]
        targets, refs = refs[:results], refs[results:]
        staged, made = list(sources), list(targets)
        for i in staged_in:
            staged[i] = refs.pop(0)
        for i in staged_out:
            made[i] = refs.pop(0)
        in_sem, out_sem = refs[-2:]
        copies = {
            i: pltpu.make_async_copy(
                sources[i].at[pl.ds(0, heads[i])] if i in heads else sources[i],
                staged[i],
                in_sem.at[i],
            )
            for i in staged_in
        }
        leaving = {
            i: pltpu.make_async_copy(made[i], targets[i], out_sem.at[i]) for i in staged_out
        }

        def begin():
            for copy in copies.values():
                copy.start()

        if eager:
            begin()
        body(
            place,
            staged,
            lambda *which: begin()
            if which == (None,)
            else [copies[i].wait() for i in which if i in copies],
            made,
            lambda *which: [leaving[i].start() for i in which],
            *refs[:-2],
        )
        for copy in leaving.values():
            copy.wait()

    anywhere = pl.BlockSpec(memory_space=pl.ANY)
    nearby = pl.BlockSpec(memory_space=pltpu.VMEM)
    return pl.pallas_call(
        kernel,
        out_shape=list(outs),
        in_specs=[SMEM] + [nearby if i in near else anywhere for i in range(count)],
        out_specs=[anywhere] * results,
        scratch_shapes=[
            pltpu.VMEM((heads.get(i, ins[i].shape[0]), *ins[i].shape[1:]), ins[i].dtype)
            for i in staged_in
        ]
        + [pltpu.VMEM(outs[i].shape, outs[i].dtype) for i in staged_out]
        + list(scratch)
        + [pltpu.SemaphoreType.DMA((count,)), pltpu.SemaphoreType.DMA((results,))],
        input_output_aliases=aliases or {},
        compiler_params=pltpu.CompilerParams(vmem_limit_bytes=limit or (SMALL_LIMIT if near else VMEM_LIMIT)),
        cost_estimate=pl.CostEstimate(flops=flops, bytes_accessed=size, transcendentals=0),
    )


def split(value):
    high = value.astype(BF16)
    return high, (value - high.astype(F32)).astype(BF16)


def dot_split(left, right):
    left_high, left_low = left
    right_high, right_low = right
    return jnp.dot(
        jnp.concatenate([left_high, left_high, left_low], axis=1),
        jnp.concatenate([right_high, right_low, right_high], axis=0),
        preferred_element_type=F32,
    )


def beside(left, right):
    return tuple(jnp.concatenate(pair, axis=1) for pair in zip(left, right))


def dot3(left, right):
    return dot_split(split(left), split(right))


def dot3t(left, right):
    return dot3(left.T, right)


def swap_groups(tiles):
    tiles = list(tiles)
    group = lax.broadcasted_iota(jnp.int32, (8, 128), 1) // 8
    for bit in (1, 2, 4, 8):
        keep = (group & bit) == 0
        for i in range(16):
            if i & bit:
                continue
            a, b = tiles[i], tiles[i | bit]
            tiles[i] = jnp.where(keep, a, pltpu.roll(b, 8 * bit, 1))
            tiles[i | bit] = jnp.where(keep, pltpu.roll(a, 128 - 8 * bit, 1), b)
    return tiles


def pack_body(
    place_ref, staged, wait, made, flush, lines_ref, turned_ref, packed_ref, in_sem, out_sem
):
    (source_ref,), (out_ref, matrix_ref) = staged, made
    arriving = [
        pltpu.make_async_copy(source_ref.at[high], lines_ref.at[high], in_sem.at[high])
        for high in range(2)
    ]
    for copy in arriving:
        copy.start()
    for high in range(2):
        arriving[high].wait()

        def first(group, carry):
            for half in range(2):
                tiles = []
                for col in range(N_COL):
                    for low in range(4):
                        start = (4 * low + col) * 128 + group * 2 + half
                        tile = lines_ref[high, pl.ds(start, 8, stride=16), :]
                        block = 16 * high + 4 * low + col
                        matrix_ref[group, block * 8 : block * 8 + 8, half * 128 : half * 128 + 128] = tile
                        tiles.append(tile)
                turned = jnp.concatenate(tiles, axis=0).T
                turned_ref[high, group, half * 128 : half * 128 + 128, :] = turned
            return carry

        lax.fori_loop(0, LOC_C, first, 0, unroll=2)
    flush(1)
    leaving = []
    for part in range(4):

        def second(index, carry):
            row = part * 8 + index
            tiles = [
                turned_ref[high, group, pl.ds(row * 8, 8), :]
                for high in range(2)
                for group in range(LOC_C)
            ]
            packed_ref[part, pl.ds(index * 128, 128), :] = jnp.concatenate(tiles, axis=0).T
            return carry

        lax.fori_loop(0, 8, second, 0, unroll=4)
        leaving.append(
            pltpu.make_async_copy(packed_ref.at[part], out_ref.at[part], out_sem.at[part])
        )
        leaving[part].start()
    for copy in leaving:
        copy.wait()


def mirror_tiles(piece_ref, low, half):
    tiles = [piece_ref[half * 16 + sub, pl.ds(low * 8, 8), :] for sub in range(16)]
    turned = jnp.concatenate(tiles, axis=0).T
    return {
        (high, group): turned[high * 64 + group * 8 : high * 64 + group * 8 + 8]
        for high in range(2)
        for group in range(LOC_C)
    }


def half_kernel(lines_ref, arrived_ref, out_ref):
    def turn(low, carry):
        for half in range(2):
            for (high, group), tile in mirror_tiles(arrived_ref.at[:, 0], low, half).items():
                rows = pl.ds((4 * high + low) * 2 + half, 8, stride=16)
                out_ref[group, 0, rows, :] = 0.5 * (lines_ref[group, 0, rows, :] + tile)
        return carry

    lax.fori_loop(0, 4, turn, 0, unroll=2)


def half_sum(lines, arrived):
    split_lines = (LOC_C, N_COL, 128, 128)
    block = pl.BlockSpec((LOC_C, 1, 128, 128), lambda i: (0, i, 0, 0))
    return pl.pallas_call(
        half_kernel,
        grid=(N_COL,),
        out_shape=shape(*split_lines),
        in_specs=[block, pl.BlockSpec((N_ROW, 1, 32, 128), lambda i: (0, i, 0, 0))],
        out_specs=block,
        compiler_params=pltpu.CompilerParams(vmem_limit_bytes=VMEM_LIMIT),
        cost_estimate=pl.CostEstimate(flops=0, bytes_accessed=2**24, transcendentals=0),
    )(lines.reshape(split_lines), arrived)


def direct_body(
    place_ref, staged, wait, made, flush, one_ref, zero_ref, left_ref, image_ref, square_ref, heads_ref
):
    matrix_ref, *pieces = staged[:9]
    inverse_ref = staged[9]
    panels = staged[10:14]
    leads = staged[14:16]
    rest_ref, high_ref, low_ref, keep_ref, give_ref = made
    row_y, row_z, core, col_place = (place_ref[i] for i in range(1, 5))
    is_zero = col_place == 0
    is_one = col_place == 1
    mine = pl.ds(pl.multiple_of(place_ref[0] * 8, 8), 8)
    wait(*range(1, 9))
    for side in range(2):
        moved = core if side == 0 else 1 - core
        for j in range(4):
            for i in range(4):
                place_y = (row_y - jnp.where(moved == 0, RING[j], RING[i])) & 3
                place_z = (row_z - jnp.where(moved == 0, RING[i], RING[j])) & 3
                owner = (place_y * 4 + place_z) * 2 + moved
                rows = pl.ds(pl.multiple_of(owner * 8, 8), 8)
                piece = pieces[4 * side + j]
                for s in range(LOC_C):
                    start = i * PIECE + s * 8
                    zero_ref[s, rows, :] = piece[start : start + 8, :]
                    start = start + STRIP
                    one_ref[s, rows, :] = piece[start : start + 8, :]

    wait(*range(9, 16))
    for side in range(2):
        moved = core if side == 0 else 1 - core
        for chip in range(N_CHIP):
            rows = pl.ds(pl.multiple_of((chip * 2 + moved) * 8, 8), 8)
            for head in range(3):
                for half in range(2):
                    start = (head * 2 + half) * 8
                    lanes = slice(half * 128, half * 128 + 128)
                    heads_ref[head, rows, lanes] = leads[side][chip, start : start + 8, :]
    inverse_one, inverse_zero = split(inverse_ref[1]), split(inverse_ref[0])
    cross_factor = heads_ref[1]
    mixer = split(dot3(dot_split(inverse_one, split(cross_factor)), inverse_ref[0]))

    def product(s, carry):
        hidden = jnp.logical_and(s == 0, is_zero | is_one)
        both = split(jnp.where(hidden, 0.0, matrix_ref[s]))
        panel_one = split(jnp.where(jnp.logical_and(is_one, s == 0), 0.0, one_ref[s]))
        panel_zero = split(zero_ref[s])
        product = dot_split(both, beside(panel_one, panel_zero))
        image_ref[0] += product[:, :BLK]
        image_ref[1] += product[:, BLK:]
        scaled = dot_split(panel_one, beside(inverse_one, mixer))
        scaled_zero = dot_split(panel_zero, inverse_zero) - scaled[:, BLK:]
        for place, panel in enumerate((scaled[:, :BLK], scaled_zero)):
            lanes = slice(place * BLK, place * BLK + BLK)
            high_ref[s, :, lanes], low_ref[s, :, lanes] = split(panel)
        return carry

    wait(0)
    image_ref[...] = jnp.zeros_like(image_ref)
    lax.fori_loop(0, LOC_C, product, 0)
    flush(1, 2)
    first = matrix_ref[0]
    image_one, image_zero = image_ref[0], image_ref[1]
    rest_one = jnp.where(is_one, first, 0.0) - image_one
    rest_zero = jnp.where(is_zero, first, 0.0) - image_zero
    scaled_one = dot_split(split(rest_one), inverse_one)
    rest_ref[0] = scaled_one
    rest_ref[1] = dot_split(split(rest_zero - dot3(scaled_one, cross_factor)), inverse_zero)
    flush(0)

    for d in range(4):
        kind = (col_place - d) & 3
        for s in range(LOC_C):
            rows = pl.ds(pl.multiple_of((4 * s + kind) * 8, 8), 8)
            for panel in range(2):
                tile = panels[d][panel, s * 8 : s * 8 + 8, :]
                if s == 0:
                    tile = jnp.where(kind < 2, 0.0, tile)
                left_ref[panel, rows, :] = tile
    row = lax.broadcasted_iota(jnp.int32, (BLK, BLK), 0)
    column = lax.broadcasted_iota(jnp.int32, (BLK, BLK), 1)

    def lower(value):
        return jnp.where(row >= column, value, 0.0)

    def phi(value):
        return jnp.where(row > column, value, jnp.where(row == column, 0.5 * value, 0.0))

    def spread(square, part):
        square_ref[...] = square
        square_ref[mine, :] += part
        return square_ref[...]

    def corner(square, factor, inverse):
        inner = phi(dot3t(factor, lower(square)))
        whole = dot3(dot3t(inverse, inner), inverse)
        return whole + whole.T

    def put(place, value):
        for half in range(2):
            tile = value[:, half * 128 : half * 128 + 128].reshape(N_CHIP, 2, RSUB, 128)
            rows = slice((place * 2 + half) * 8, (place * 2 + half) * 8 + 8)
            keep_ref[:, rows, :] = jnp.where(core == 0, tile[:, 0], tile[:, 1])
            give_ref[:, rows, :] = jnp.where(core == 0, tile[:, 1], tile[:, 0])

    left_one = split(left_ref[1].T)
    left_zero = split(left_ref[0].T)
    parts_one = split(image_one)
    parts_zero = split(image_zero)
    parts_rest = split(rest_one)
    inverse_one, inverse_zero = inverse_ref[1], inverse_ref[0]
    sum_one = dot_split(left_one, parts_rest) - dot_split(left_one, parts_one).T
    corner_one = corner(
        spread(-dot3(sum_one, inverse_one), jnp.where(is_one, first[8:16], 0.0)),
        heads_ref[0],
        inverse_one,
    )
    put(2, corner_one)
    sum_cross = dot_split(left_zero, parts_rest).T - dot_split(left_one, parts_zero)
    mixed = spread(dot3t(inverse_one, sum_cross), image_zero[8:16])
    cross = spread(
        -(mixed + dot3(corner_one, cross_factor)), jnp.where(is_zero, first[8:16], 0.0)
    )
    cross = dot3(cross, inverse_zero)
    put(0, cross)
    put(3, cross.T)
    sum_zero = dot_split(left_zero, split(rest_zero)) - dot_split(left_zero, parts_zero).T
    sum_zero = dot3(sum_zero - dot3t(mixed, cross_factor), inverse_zero)
    corner_zero = corner(
        spread(-(sum_zero + dot3t(cross_factor, cross)), jnp.where(is_zero, first[0:8], 0.0)),
        heads_ref[2],
        inverse_zero,
    )
    put(1, corner_zero)
    flush(3, 4)


def image_body(
    place_ref, staged, wait, made, flush, arrived_ref, both_ref, strips_ref, in_sem
):
    source_ref, rest_ref, high_ref, low_ref = staged
    chunk_refs = made
    col_place = place_ref[4]
    arriving = [
        pltpu.make_async_copy(source_ref.at[:, col], arrived_ref.at[col], in_sem.at[col])
        for col in range(N_COL)
    ]
    for copy in arriving:
        copy.start()
    wait(None)
    for col in range(N_COL):
        arriving[col].wait()

        def turn(low, carry):
            for half in range(2):
                tiles = mirror_tiles(arrived_ref.at[col], low, half)
                for (high, group), tile in tiles.items():
                    inner = 4 * high + low
                    if group == 0 and col < 2:
                        tile = jnp.zeros_like(tile)
                    if high == 0:
                        tile = jnp.where(jnp.logical_and(col_place == 0, low == 0), 0.0, tile)
                    rows = slice((4 * group + col) * 8, (4 * group + col) * 8 + 8)
                    both_ref[inner, rows, half * 128 : half * 128 + 128] = tile
            return carry

        lax.fori_loop(0, 4, turn, 0, unroll=2)
    wait(1, 2, 3)
    for part in range(2):
        blocks = range(part * 4, part * 4 + 4)
        pairs = [split(both_ref[s]) for s in blocks]
        left = [pair[0] for pair in pairs] * 2 + [pair[1] for pair in pairs]
        right = [high_ref[s] for s in blocks] + [low_ref[s] for s in blocks]
        right += [high_ref[s] for s in blocks]
        product = jnp.dot(
            jnp.concatenate(left, axis=1),
            jnp.concatenate(right, axis=0),
            preferred_element_type=F32,
        )
        for panel in range(2):
            lanes = slice(panel * BLK, panel * BLK + BLK)
            base = rest_ref[panel] if part == 0 else strips_ref[:, lanes]
            strips_ref[:, lanes] = base - product[:, lanes]
    for d in range(4):
        kind = (col_place + d) & 3
        for s in range(LOC_C):
            tile = strips_ref[pl.ds(pl.multiple_of((4 * s + kind) * 8, 8), 8), :]
            if s == 0:
                tile = jnp.where(kind < 2, 0.0, tile)
            chunk_refs[d][s * 8 : s * 8 + 8, :] = tile
        flush(d)


def total_body(place_ref, staged, wait, made, flush):
    wait(0)
    made[0][...] = jnp.sum(staged[0][...], axis=0)
    flush(0)


def strip_body(place_ref, staged, wait, made, flush):
    across_ref, *out_refs = made
    totals_ref = staged[4]
    col_place = place_ref[4]
    wait(*range(4))
    strip = (staged[0][...] + staged[1][...]) + (staged[2][...] + staged[3][...])
    for half in range(2):
        tiles = [
            strip[s * 8 : s * 8 + 8, k * BLK + half * 128 : k * BLK + half * 128 + 128]
            for s in range(LOC_C)
            for k in range(2)
        ]
        for sub, tile in enumerate(swap_groups(tiles)):
            across_ref[half * 16 + sub] = tile
    flush(0)
    wait(4)
    for d in range(4):
        target = (col_place + d) & 3
        out_refs[d][:STRIP] = jnp.where(target == 0, strip[:, BLK:], strip[:, :BLK])
        for mat in range(2):
            for half in range(2):
                start = mat * 16 + half * 8
                tile = jnp.where(
                    target == 0, totals_ref[start : start + 8], totals_ref[start + 32 : start + 40]
                )
                rows = slice(STRIP + mat * 8, STRIP + mat * 8 + 8)
                out_refs[d][rows, half * 128 : half * 128 + 128] = tile
        flush(1 + d)


def finish_body(
    place_ref, staged, wait, made, flush, top_ref, edge_ref, head_ref, edge_sem, out_sem
):
    half_ref, lines_ref, first_ref, across_ref = staged[:4]
    strips = staged[4:8]
    (out_ref,) = made
    edge = half_ref.at[:, pl.ds(0, 8), :]
    reading = pltpu.make_async_copy(edge, edge_ref, edge_sem)
    reading.start()
    col_place = place_ref[4]
    is_zero = col_place == 0
    is_one = col_place == 1
    owner = col_place < 2
    wait(1, 3)
    for half in range(2):
        turned = across_ref[half * 16 : half * 16 + 16].reshape(128, 128).T
        for s in range(LOC_C):
            for k in range(2):
                top_ref[k, s, half] = turned[(s * 2 + k) * 8 : (s * 2 + k) * 8 + 8]
    for s in range(1, LOC_C):
        for half in range(2):
            for block in range(2):
                rows = pl.ds(block * 128 + s * 2 + half, 8, stride=16)
                new = lines_ref[rows, :] + top_ref[1 - block, s, half]
                head_ref[block * 8 : block * 8 + 8, s * 2 + half, :] = 0.5 * new
    reading.wait()
    wait(2, 4, 5, 6, 7)
    for half in range(2):
        lanes = slice(half * 128, half * 128 + 128)
        part_a, part_b = [
            (strips[0][rows, lanes] + strips[1][rows, lanes])
            + (strips[2][rows, lanes] + strips[3][rows, lanes])
            for rows in (slice(STRIP, STRIP + 8), slice(STRIP + 8, STRIP + 16))
        ]
        own = lines_ref[pl.ds(half, 8, stride=16), :]
        head_ref[0:8, half, :] = 0.5 * jnp.where(
            is_zero, part_b, own + jnp.where(is_one, part_b, top_ref[1, 0, half])
        )
        own = lines_ref[pl.ds(128 + half, 8, stride=16), :]
        head_ref[8:16, half, :] = jnp.where(
            is_zero,
            edge_ref[8:16, half, :] + 0.5 * (part_a - own),
            0.5 * jnp.where(is_one, part_a, own + top_ref[0, 0, half]),
        )
        for d in range(4):
            kind = (col_place - d) & 3
            for s in range(LOC_C):
                rows = pl.ds(pl.multiple_of((4 * s + kind) * 8, 8), 8)
                change = 0.5 * (strips[d][s * 8 : s * 8 + 8, lanes] - first_ref[rows, lanes])
                edge_ref[rows, half, :] += jnp.where(owner, change, 0.0)
    writing = [
        pltpu.make_async_copy(head_ref, out_ref.at[pl.ds(0, 16)], out_sem.at[0]),
        pltpu.make_async_copy(
            edge_ref.at[pl.ds(16, ROWS - 16)],
            out_ref.at[pl.ds(16, ROWS - 16), pl.ds(0, 8), :],
            out_sem.at[1],
        ),
    ]
    for copy in writing:
        copy.start()
    for copy in writing:
        copy.wait()


def ring(first, d):
    pairs = []
    for i in range(N_ROW):
        y, z, core = i >> 3, (i >> 1) & 3, i & 1
        if (core == 0) == first:
            z = (z + d) & 3
        else:
            y = (y + d) & 3
        pairs.append((i, (y * 4 + z) * 2 + core))
    return pairs


def around(piece, first):
    return [piece] + [lax.ppermute(piece, "row", ring(first, d)) for d in RING[1:]]


def to_owners(pieces):
    moved = [
        lax.ppermute(pieces[d], "col", [((t - d) % 4, t) for t in range(2)]) for d in range(1, 4)
    ]
    return [pieces[0]] + moved


def on_device(adjoint, lower_panels, diag_inverse):
    row_place = lax.axis_index("row")
    col_place = lax.axis_index("col")
    place = jnp.stack(
        [row_place, row_place >> 3, (row_place >> 1) & 3, row_place & 1, col_place]
    ).astype(jnp.int32)
    lines = adjoint.reshape(LINES, 128)
    panels = lower_panels.reshape(2, STRIP, BLK)
    by_rows = [panels] + [
        lax.ppermute(panels, "col", [(i, (i + d) % 4) for i in range(4)]) for d in range(1, 4)
    ]
    lead = jnp.stack([piece[:, :RSUB] for piece in by_rows])
    lead_one = lax.dynamic_index_in_dim(lead, (col_place - 1) & 3, 0, False)
    lead_zero = lax.dynamic_index_in_dim(lead, col_place, 0, False)
    lead = jnp.stack([lead_one[1], lead_one[0], lead_zero[0]]).reshape(3, RSUB, 2, 128)
    lead = lead.transpose(0, 2, 1, 3).reshape(1, 6 * RSUB, 128)
    across_core = [(i, i ^ 1) for i in range(N_ROW)]
    same_core = [[2 * chip + core for chip in range(N_CHIP)] for core in range(2)]

    def exchange(value):
        return lax.all_to_all(
            value, "row", split_axis=0, concat_axis=0, tiled=True, axis_index_groups=same_core
        )

    ring_one = jnp.concatenate(around(panels.reshape(PIECE, BLK), True), axis=0)
    plane = around(ring_one, False)
    leads = exchange(jnp.broadcast_to(lead, (N_CHIP, 6 * RSUB, 128)))
    later, ring_one = lax.optimization_barrier((place, ring_one))
    high_shape = shape(2, LINES // 2, 128)
    part_shape = shape(4, LINES // 4, 128)
    wide = shape(LOC_C, ROWS, BLK)
    outgoing, matrix = call(
        pack_body,
        [part_shape, wide],
        [high_shape],
        scratch=[
            pltpu.VMEM(high_shape.shape, F32),
            pltpu.VMEM((2, LOC_C, BLK, 128), F32),
            pltpu.VMEM(part_shape.shape, F32),
            pltpu.SemaphoreType.DMA((2,)),
            pltpu.SemaphoreType.DMA((4,)),
        ],
        raw_in=(0,),
        raw_out=(0,),
        size=2**24,
    )(later, lines.reshape(high_shape.shape))
    outgoing, *plane = lax.optimization_barrier((outgoing, *plane))
    arrived = lax.all_to_all(
        outgoing.reshape(N_ROW * N_COL, 32, 128), ("row", "col"), split_axis=0, concat_axis=0, tiled=True
    )
    plane = plane + [lax.ppermute(part, "row", across_core) for part in plane]
    leads = [leads, lax.ppermute(leads, "row", across_core)]

    direct_ins = [matrix, *plane, diag_inverse, *by_rows, *leads]
    split_shape = shape(LOC_C, BLK, 2 * BLK, dtype=BF16)
    square_shape = pltpu.VMEM((BLK, BLK), F32)
    pair_shape = pltpu.VMEM((2, BLK, BLK), F32)
    wide_shape = pltpu.VMEM((LOC_C, BLK, BLK), F32)
    rest, high, low, corners, given = call(
        direct_body,
        [
            shape(2, BLK, BLK), split_shape, split_shape,
            shape(N_CHIP, 64, 128), shape(N_CHIP, 64, 128),
        ],
        direct_ins,
        near=(*range(1, 9), 11, 12, 13, 14, 15),
        limit=50 * 2**20,
        scratch=[wide_shape, wide_shape, pair_shape, pair_shape, square_shape, pltpu.VMEM((3, BLK, BLK), F32)],
        flops=2**33,
        size=2**24,
    )(place, *direct_ins)
    corners = exchange(corners + lax.ppermute(given, "row", across_core))
    arrived = arrived.reshape(N_ROW, N_COL, 32, 128)
    image_ins = [arrived, rest, high, low]
    chunks = call(
        image_body,
        [shape(STRIP, 2 * BLK)] * 4,
        image_ins,
        scratch=[
            pltpu.VMEM((N_COL, N_ROW, 32, 128), F32),
            wide_shape,
            pltpu.VMEM((ROWS, 2 * BLK), F32),
            pltpu.SemaphoreType.DMA((N_COL,)),
        ],
        raw_in=(0,),
        eager=False,
        flops=2**32,
        size=2**24,
    )(place, *image_ins)
    strips = [chunks[0]] + [
        lax.ppermute(chunks[d], "col", [(i, (i + d) % 4) for i in range(4)]) for d in range(1, 4)
    ]
    corners, first, *chunks = lax.optimization_barrier((corners, matrix[0], *chunks))
    totals = call(total_body, [shape(64, 128)], [corners], near=(0,), size=2**19)(place, corners)
    strip_ins = [*strips, *totals]
    across, *panels = call(
        strip_body,
        [shape(N_ROW, RSUB, 128)] + [shape(STRIP + 2 * RSUB, BLK)] * 4,
        strip_ins,
        near=(0, 1, 2, 3, 4),
        size=2**21,
    )(place, *strip_ins)
    arrived, across = lax.optimization_barrier((arrived, across))
    across = lax.all_to_all(across, "row", split_axis=0, concat_axis=0, tiled=True)
    panels = to_owners(panels)
    half = half_sum(lines, arrived).reshape(ROWS, 16, 128)
    finish_ins = [half, lines, first, across, *panels]
    (result,) = call(
        finish_body,
        [shape(ROWS, 16, 128)],
        finish_ins,
        scratch=[
            pltpu.VMEM((2, LOC_C, 2, RSUB, 128), F32),
            pltpu.VMEM((ROWS, 8, 128), F32),
            pltpu.VMEM((16, 16, 128), F32),
            pltpu.SemaphoreType.DMA,
            pltpu.SemaphoreType.DMA((2,)),
        ],
        heads={1: 2 * 128},
        near=(3, 5, 6, 7),
        raw_in=(0,),
        raw_out=(0,),
        aliases={1: 0},
        size=2**23,
    )(place, *finish_ins)
    return result.reshape(NBLK, 1, RSUB, LOC_C, 1, BLK)


def solution(mesh):
    return jax.shard_map(
        on_device,
        mesh=mesh,
        in_specs=(
            P(None, "row", None, None, "col", None),
            P(None, None, "col", "row", None, None),
            P(),
        ),
        out_specs=P(None, "row", None, None, "col", None),
        check_vma=False,
    )
```

```python
import jax
import jax.numpy as jnp
from jax import lax
from jax.experimental import pallas as pl
from jax.experimental.pallas import tpu as pltpu
from jax.sharding import PartitionSpec as P

BLK = 256
RSUB = 8
LOC_C = 8
N_ROW = 32
N_COL = 4
NBLK = 32
ROWS = NBLK * RSUB
COLS = LOC_C * BLK
LINES = ROWS * COLS // 128
STRIP = LOC_C * RSUB
PIECE = 2 * STRIP
N_CHIP = 16
RING = (0, 1, 3, 2)
F32 = jnp.float32
BF16 = jnp.bfloat16
VMEM_LIMIT = 56 * 1024 * 1024
SMALL_LIMIT = 24 * 1024 * 1024
SMEM = pl.BlockSpec(memory_space=pltpu.SMEM)


def shape(*dims, dtype=F32):
    return jax.ShapeDtypeStruct(dims, dtype)


def call(
    body, outs, ins, scratch=(), heads=None, raw_in=(), raw_out=(), near=(), limit=0, aliases=None, eager=True,
    flops=0, size=0,
):
    count, results = len(ins), len(outs)
    heads = heads or {}
    staged_in = [i for i in range(count) if i not in raw_in and i not in near]
    staged_out = [i for i in range(results) if i not in raw_out]

    def kernel(*refs):
        refs = list(refs)
        place = refs.pop(0)
        sources, refs = refs[:count], refs[count:]
        targets, refs = refs[:results], refs[results:]
        staged, made = list(sources), list(targets)
        for i in staged_in:
            staged[i] = refs.pop(0)
        for i in staged_out:
            made[i] = refs.pop(0)
        in_sem, out_sem = refs[-2:]
        copies = {
            i: pltpu.make_async_copy(
                sources[i].at[pl.ds(0, heads[i])] if i in heads else sources[i],
                staged[i],
                in_sem.at[i],
            )
            for i in staged_in
        }
        leaving = {
            i: pltpu.make_async_copy(made[i], targets[i], out_sem.at[i]) for i in staged_out
        }

        def begin():
            for copy in copies.values():
                copy.start()

        if eager:
            begin()
        body(
            place,
            staged,
            lambda *which: begin()
            if which == (None,)
            else [copies[i].wait() for i in which if i in copies],
            made,
            lambda *which: [leaving[i].start() for i in which],
            *refs[:-2],
        )
        for copy in leaving.values():
            copy.wait()

    anywhere = pl.BlockSpec(memory_space=pl.ANY)
    nearby = pl.BlockSpec(memory_space=pltpu.VMEM)
    return pl.pallas_call(
        kernel,
        out_shape=list(outs),
        in_specs=[SMEM] + [nearby if i in near else anywhere for i in range(count)],
        out_specs=[anywhere] * results,
        scratch_shapes=[
            pltpu.VMEM((heads.get(i, ins[i].shape[0]), *ins[i].shape[1:]), ins[i].dtype)
            for i in staged_in
        ]
        + [pltpu.VMEM(outs[i].shape, outs[i].dtype) for i in staged_out]
        + list(scratch)
        + [pltpu.SemaphoreType.DMA((count,)), pltpu.SemaphoreType.DMA((results,))],
        input_output_aliases=aliases or {},
        compiler_params=pltpu.CompilerParams(vmem_limit_bytes=limit or (SMALL_LIMIT if near else VMEM_LIMIT)),
        cost_estimate=pl.CostEstimate(flops=flops, bytes_accessed=size, transcendentals=0),
    )


def split(value):
    high = value.astype(BF16)
    return high, (value - high.astype(F32)).astype(BF16)


def dot_split(left, right):
    left_high, left_low = left
    right_high, right_low = right
    return jnp.dot(
        jnp.concatenate([left_high, left_high, left_low], axis=1),
        jnp.concatenate([right_high, right_low, right_high], axis=0),
        preferred_element_type=F32,
    )


def beside(left, right):
    return tuple(jnp.concatenate(pair, axis=1) for pair in zip(left, right))


def dot3(left, right):
    return dot_split(split(left), split(right))


def dot3t(left, right):
    return dot3(left.T, right)


def swap_groups(tiles):
    tiles = list(tiles)
    group = lax.broadcasted_iota(jnp.int32, (8, 128), 1) // 8
    for bit in (1, 2, 4, 8):
        keep = (group & bit) == 0
        for i in range(16):
            if i & bit:
                continue
            a, b = tiles[i], tiles[i | bit]
            tiles[i] = jnp.where(keep, a, pltpu.roll(b, 8 * bit, 1))
            tiles[i | bit] = jnp.where(keep, pltpu.roll(a, 128 - 8 * bit, 1), b)
    return tiles


def pack_body(
    place_ref, staged, wait, made, flush, lines_ref, turned_ref, packed_ref, in_sem, out_sem
):
    (source_ref,), (out_ref, matrix_ref) = staged, made
    arriving = [
        pltpu.make_async_copy(source_ref.at[high], lines_ref.at[high], in_sem.at[high])
        for high in range(2)
    ]
    for copy in arriving:
        copy.start()
    for high in range(2):
        arriving[high].wait()

        def first(group, carry):
            for half in range(2):
                tiles = []
                for col in range(N_COL):
                    for low in range(4):
                        start = (4 * low + col) * 128 + group * 2 + half
                        tile = lines_ref[high, pl.ds(start, 8, stride=16), :]
                        block = 16 * high + 4 * low + col
                        matrix_ref[group, block * 8 : block * 8 + 8, half * 128 : half * 128 + 128] = tile
                        tiles.append(tile)
                turned = jnp.concatenate(tiles, axis=0).T
                turned_ref[high, group, half * 128 : half * 128 + 128, :] = turned
            return carry

        lax.fori_loop(0, LOC_C, first, 0, unroll=2)
    flush(1)
    leaving = []
    for part in range(4):

        def second(index, carry):
            row = part * 8 + index
            tiles = [
                turned_ref[high, group, pl.ds(row * 8, 8), :]
                for high in range(2)
                for group in range(LOC_C)
            ]
            packed_ref[part, pl.ds(index * 128, 128), :] = jnp.concatenate(tiles, axis=0).T
            return carry

        lax.fori_loop(0, 8, second, 0, unroll=4)
        leaving.append(
            pltpu.make_async_copy(packed_ref.at[part], out_ref.at[part], out_sem.at[part])
        )
        leaving[part].start()
    for copy in leaving:
        copy.wait()


def mirror_tiles(piece_ref, low, half):
    tiles = [piece_ref[half * 16 + sub, pl.ds(low * 8, 8), :] for sub in range(16)]
    turned = jnp.concatenate(tiles, axis=0).T
    return {
        (high, group): turned[high * 64 + group * 8 : high * 64 + group * 8 + 8]
        for high in range(2)
        for group in range(LOC_C)
    }


def half_kernel(lines_ref, arrived_ref, out_ref):
    def turn(low, carry):
        for half in range(2):
            for (high, group), tile in mirror_tiles(arrived_ref.at[:, 0], low, half).items():
                rows = pl.ds((4 * high + low) * 2 + half, 8, stride=16)
                out_ref[group, 0, rows, :] = 0.5 * (lines_ref[group, 0, rows, :] + tile)
        return carry

    lax.fori_loop(0, 4, turn, 0, unroll=2)


def half_sum(lines, arrived):
    split_lines = (LOC_C, N_COL, 128, 128)
    block = pl.BlockSpec((LOC_C, 1, 128, 128), lambda i: (0, i, 0, 0))
    return pl.pallas_call(
        half_kernel,
        grid=(N_COL,),
        out_shape=shape(*split_lines),
        in_specs=[block, pl.BlockSpec((N_ROW, 1, 32, 128), lambda i: (0, i, 0, 0))],
        out_specs=block,
        compiler_params=pltpu.CompilerParams(vmem_limit_bytes=VMEM_LIMIT),
        cost_estimate=pl.CostEstimate(flops=0, bytes_accessed=2**24, transcendentals=0),
    )(lines.reshape(split_lines), arrived)


def direct_body(
    place_ref, staged, wait, made, flush, one_ref, zero_ref, left_ref, image_ref, square_ref, heads_ref
):
    matrix_ref, *pieces = staged[:9]
    inverse_ref = staged[9]
    panels = staged[10:14]
    leads = staged[14:16]
    rest_ref, high_ref, low_ref, keep_ref, give_ref = made
    row_y, row_z, core, col_place = (place_ref[i] for i in range(1, 5))
    is_zero = col_place == 0
    is_one = col_place == 1
    mine = pl.ds(pl.multiple_of(place_ref[0] * 8, 8), 8)
    wait(*range(1, 9))
    for side in range(2):
        moved = core if side == 0 else 1 - core
        for j in range(4):
            for i in range(4):
                place_y = (row_y - jnp.where(moved == 0, RING[j], RING[i])) & 3
                place_z = (row_z - jnp.where(moved == 0, RING[i], RING[j])) & 3
                owner = (place_y * 4 + place_z) * 2 + moved
                rows = pl.ds(pl.multiple_of(owner * 8, 8), 8)
                piece = pieces[4 * side + j]
                for s in range(LOC_C):
                    start = i * PIECE + s * 8
                    zero_ref[s, rows, :] = piece[start : start + 8, :]
                    start = start + STRIP
                    one_ref[s, rows, :] = piece[start : start + 8, :]

    wait(*range(9, 16))
    for side in range(2):
        moved = core if side == 0 else 1 - core
        for chip in range(N_CHIP):
            rows = pl.ds(pl.multiple_of((chip * 2 + moved) * 8, 8), 8)
            for head in range(3):
                for half in range(2):
                    start = (head * 2 + half) * 8
                    lanes = slice(half * 128, half * 128 + 128)
                    heads_ref[head, rows, lanes] = leads[side][chip, start : start + 8, :]
    inverse_one, inverse_zero = split(inverse_ref[1]), split(inverse_ref[0])
    cross_factor = heads_ref[1]
    mixer = split(dot3(dot_split(inverse_one, split(cross_factor)), inverse_ref[0]))

    def product(s, carry):
        hidden = jnp.logical_and(s == 0, is_zero | is_one)
        both = split(jnp.where(hidden, 0.0, matrix_ref[s]))
        panel_one = split(jnp.where(jnp.logical_and(is_one, s == 0), 0.0, one_ref[s]))
        panel_zero = split(zero_ref[s])
        product = dot_split(both, beside(panel_one, panel_zero))
        image_ref[0] += product[:, :BLK]
        image_ref[1] += product[:, BLK:]
        scaled = dot_split(panel_one, beside(inverse_one, mixer))
        scaled_zero = dot_split(panel_zero, inverse_zero) - scaled[:, BLK:]
        for place, panel in enumerate((scaled[:, :BLK], scaled_zero)):
            lanes = slice(place * BLK, place * BLK + BLK)
            high_ref[s, :, lanes], low_ref[s, :, lanes] = split(panel)
        return carry

    wait(0)
    image_ref[...] = jnp.zeros_like(image_ref)
    lax.fori_loop(0, LOC_C, product, 0)
    flush(1, 2)
    first = matrix_ref[0]
    image_one, image_zero = image_ref[0], image_ref[1]
    rest_one = jnp.where(is_one, first, 0.0) - image_one
    rest_zero = jnp.where(is_zero, first, 0.0) - image_zero
    scaled_one = dot_split(split(rest_one), inverse_one)
    rest_ref[0] = scaled_one
    rest_ref[1] = dot_split(split(rest_zero - dot3(scaled_one, cross_factor)), inverse_zero)
    flush(0)

    for d in range(4):
        kind = (col_place - d) & 3
        for s in range(LOC_C):
            rows = pl.ds(pl.multiple_of((4 * s + kind) * 8, 8), 8)
            for panel in range(2):
                tile = panels[d][panel, s * 8 : s * 8 + 8, :]
                if s == 0:
                    tile = jnp.where(kind < 2, 0.0, tile)
                left_ref[panel, rows, :] = tile
    row = lax.broadcasted_iota(jnp.int32, (BLK, BLK), 0)
    column = lax.broadcasted_iota(jnp.int32, (BLK, BLK), 1)

    def lower(value):
        return jnp.where(row >= column, value, 0.0)

    def phi(value):
        return jnp.where(row > column, value, jnp.where(row == column, 0.5 * value, 0.0))

    def spread(square, part):
        square_ref[...] = square
        square_ref[mine, :] += part
        return square_ref[...]

    def corner(square, factor, inverse):
        inner = phi(dot3t(factor, lower(square)))
        whole = dot3(dot3t(inverse, inner), inverse)
        return whole + whole.T

    def put(place, value):
        for half in range(2):
            tile = value[:, half * 128 : half * 128 + 128].reshape(N_CHIP, 2, RSUB, 128)
            rows = slice((place * 2 + half) * 8, (place * 2 + half) * 8 + 8)
            keep_ref[:, rows, :] = jnp.where(core == 0, tile[:, 0], tile[:, 1])
            give_ref[:, rows, :] = jnp.where(core == 0, tile[:, 1], tile[:, 0])

    left_one = split(left_ref[1].T)
    left_zero = split(left_ref[0].T)
    parts_one = split(image_one)
    parts_zero = split(image_zero)
    parts_rest = split(rest_one)
    inverse_one, inverse_zero = inverse_ref[1], inverse_ref[0]
    sum_one = dot_split(left_one, parts_rest) - dot_split(left_one, parts_one).T
    corner_one = corner(
        spread(-dot3(sum_one, inverse_one), jnp.where(is_one, first[8:16], 0.0)),
        heads_ref[0],
        inverse_one,
    )
    put(2, corner_one)
    sum_cross = dot_split(left_zero, parts_rest).T - dot_split(left_one, parts_zero)
    mixed = spread(dot3t(inverse_one, sum_cross), image_zero[8:16])
    cross = spread(
        -(mixed + dot3(corner_one, cross_factor)), jnp.where(is_zero, first[8:16], 0.0)
    )
    cross = dot3(cross, inverse_zero)
    put(0, cross)
    put(3, cross.T)
    sum_zero = dot_split(left_zero, split(rest_zero)) - dot_split(left_zero, parts_zero).T
    sum_zero = dot3(sum_zero - dot3t(mixed, cross_factor), inverse_zero)
    corner_zero = corner(
        spread(-(sum_zero + dot3t(cross_factor, cross)), jnp.where(is_zero, first[0:8], 0.0)),
        heads_ref[2],
        inverse_zero,
    )
    put(1, corner_zero)
    flush(3, 4)


def image_body(
    place_ref, staged, wait, made, flush, both_ref, strips_ref
):
    source_ref, rest_ref, high_ref, low_ref = staged
    chunk_refs = made
    col_place = place_ref[4]
    for col in range(N_COL):

        def turn(low, carry):
            for half in range(2):
                tiles = mirror_tiles(source_ref.at[:, col], low, half)
                for (high, group), tile in tiles.items():
                    inner = 4 * high + low
                    if group == 0 and col < 2:
                        tile = jnp.zeros_like(tile)
                    if high == 0:
                        tile = jnp.where(jnp.logical_and(col_place == 0, low == 0), 0.0, tile)
                    rows = slice((4 * group + col) * 8, (4 * group + col) * 8 + 8)
                    both_ref[inner, rows, half * 128 : half * 128 + 128] = tile
            return carry

        lax.fori_loop(0, 4, turn, 0, unroll=2)
    wait(1, 2, 3)
    for part in range(2):
        blocks = range(part * 4, part * 4 + 4)
        pairs = [split(both_ref[s]) for s in blocks]
        left = [pair[0] for pair in pairs] * 2 + [pair[1] for pair in pairs]
        right = [high_ref[s] for s in blocks] + [low_ref[s] for s in blocks]
        right += [high_ref[s] for s in blocks]
        product = jnp.dot(
            jnp.concatenate(left, axis=1),
            jnp.concatenate(right, axis=0),
            preferred_element_type=F32,
        )
        for panel in range(2):
            lanes = slice(panel * BLK, panel * BLK + BLK)
            base = rest_ref[panel] if part == 0 else strips_ref[:, lanes]
            strips_ref[:, lanes] = base - product[:, lanes]
    for d in range(4):
        kind = (col_place + d) & 3
        for s in range(LOC_C):
            tile = strips_ref[pl.ds(pl.multiple_of((4 * s + kind) * 8, 8), 8), :]
            if s == 0:
                tile = jnp.where(kind < 2, 0.0, tile)
            chunk_refs[d][s * 8 : s * 8 + 8, :] = tile
        flush(d)


def total_body(place_ref, staged, wait, made, flush):
    wait(0)
    made[0][...] = jnp.sum(staged[0][...], axis=0)
    flush(0)


def strip_body(place_ref, staged, wait, made, flush):
    across_ref, *out_refs = made
    totals_ref = staged[4]
    col_place = place_ref[4]
    wait(*range(4))
    strip = (staged[0][...] + staged[1][...]) + (staged[2][...] + staged[3][...])
    for half in range(2):
        tiles = [
            strip[s * 8 : s * 8 + 8, k * BLK + half * 128 : k * BLK + half * 128 + 128]
            for s in range(LOC_C)
            for k in range(2)
        ]
        for sub, tile in enumerate(swap_groups(tiles)):
            across_ref[half * 16 + sub] = tile
    flush(0)
    wait(4)
    for d in range(4):
        target = (col_place + d) & 3
        out_refs[d][:STRIP] = jnp.where(target == 0, strip[:, BLK:], strip[:, :BLK])
        for mat in range(2):
            for half in range(2):
                start = mat * 16 + half * 8
                tile = jnp.where(
                    target == 0, totals_ref[start : start + 8], totals_ref[start + 32 : start + 40]
                )
                rows = slice(STRIP + mat * 8, STRIP + mat * 8 + 8)
                out_refs[d][rows, half * 128 : half * 128 + 128] = tile
        flush(1 + d)


def finish_body(
    place_ref, staged, wait, made, flush, top_ref, edge_ref, head_ref, edge_sem, out_sem
):
    half_ref, lines_ref, first_ref, across_ref = staged[:4]
    strips = staged[4:8]
    (out_ref,) = made
    edge = half_ref.at[:, pl.ds(0, 8), :]
    reading = pltpu.make_async_copy(edge, edge_ref, edge_sem)
    reading.start()
    col_place = place_ref[4]
    is_zero = col_place == 0
    is_one = col_place == 1
    owner = col_place < 2
    wait(1, 3)
    for half in range(2):
        turned = across_ref[half * 16 : half * 16 + 16].reshape(128, 128).T
        for s in range(LOC_C):
            for k in range(2):
                top_ref[k, s, half] = turned[(s * 2 + k) * 8 : (s * 2 + k) * 8 + 8]
    for s in range(1, LOC_C):
        for half in range(2):
            for block in range(2):
                rows = pl.ds(block * 128 + s * 2 + half, 8, stride=16)
                new = lines_ref[rows, :] + top_ref[1 - block, s, half]
                head_ref[block * 8 : block * 8 + 8, s * 2 + half, :] = 0.5 * new
    reading.wait()
    wait(2, 4, 5, 6, 7)
    for half in range(2):
        lanes = slice(half * 128, half * 128 + 128)
        part_a, part_b = [
            (strips[0][rows, lanes] + strips[1][rows, lanes])
            + (strips[2][rows, lanes] + strips[3][rows, lanes])
            for rows in (slice(STRIP, STRIP + 8), slice(STRIP + 8, STRIP + 16))
        ]
        own = lines_ref[pl.ds(half, 8, stride=16), :]
        head_ref[0:8, half, :] = 0.5 * jnp.where(
            is_zero, part_b, own + jnp.where(is_one, part_b, top_ref[1, 0, half])
        )
        own = lines_ref[pl.ds(128 + half, 8, stride=16), :]
        head_ref[8:16, half, :] = jnp.where(
            is_zero,
            edge_ref[8:16, half, :] + 0.5 * (part_a - own),
            0.5 * jnp.where(is_one, part_a, own + top_ref[0, 0, half]),
        )
        for d in range(4):
            kind = (col_place - d) & 3
            for s in range(LOC_C):
                rows = pl.ds(pl.multiple_of((4 * s + kind) * 8, 8), 8)
                change = 0.5 * (strips[d][s * 8 : s * 8 + 8, lanes] - first_ref[rows, lanes])
                edge_ref[rows, half, :] += jnp.where(owner, change, 0.0)
    writing = [
        pltpu.make_async_copy(head_ref, out_ref.at[pl.ds(0, 16)], out_sem.at[0]),
        pltpu.make_async_copy(
            edge_ref.at[pl.ds(16, ROWS - 16)],
            out_ref.at[pl.ds(16, ROWS - 16), pl.ds(0, 8), :],
            out_sem.at[1],
        ),
    ]
    for copy in writing:
        copy.start()
    for copy in writing:
        copy.wait()


def ring(first, d):
    pairs = []
    for i in range(N_ROW):
        y, z, core = i >> 3, (i >> 1) & 3, i & 1
        if (core == 0) == first:
            z = (z + d) & 3
        else:
            y = (y + d) & 3
        pairs.append((i, (y * 4 + z) * 2 + core))
    return pairs


def around(piece, first):
    return [piece] + [lax.ppermute(piece, "row", ring(first, d)) for d in RING[1:]]


def to_owners(pieces):
    moved = [
        lax.ppermute(pieces[d], "col", [((t - d) % 4, t) for t in range(2)]) for d in range(1, 4)
    ]
    return [pieces[0]] + moved


def on_device(adjoint, lower_panels, diag_inverse):
    row_place = lax.axis_index("row")
    col_place = lax.axis_index("col")
    place = jnp.stack(
        [row_place, row_place >> 3, (row_place >> 1) & 3, row_place & 1, col_place]
    ).astype(jnp.int32)
    lines = adjoint.reshape(LINES, 128)
    panels = lower_panels.reshape(2, STRIP, BLK)
    by_rows = [panels] + [
        lax.ppermute(panels, "col", [(i, (i + d) % 4) for i in range(4)]) for d in range(1, 4)
    ]
    lead = jnp.stack([piece[:, :RSUB] for piece in by_rows])
    lead_one = lax.dynamic_index_in_dim(lead, (col_place - 1) & 3, 0, False)
    lead_zero = lax.dynamic_index_in_dim(lead, col_place, 0, False)
    lead = jnp.stack([lead_one[1], lead_one[0], lead_zero[0]]).reshape(3, RSUB, 2, 128)
    lead = lead.transpose(0, 2, 1, 3).reshape(1, 6 * RSUB, 128)
    across_core = [(i, i ^ 1) for i in range(N_ROW)]
    same_core = [[2 * chip + core for chip in range(N_CHIP)] for core in range(2)]

    def exchange(value):
        return lax.all_to_all(
            value, "row", split_axis=0, concat_axis=0, tiled=True, axis_index_groups=same_core
        )

    ring_one = jnp.concatenate(around(panels.reshape(PIECE, BLK), True), axis=0)
    plane = around(ring_one, False)
    leads = exchange(jnp.broadcast_to(lead, (N_CHIP, 6 * RSUB, 128)))
    later, ring_one = lax.optimization_barrier((place, ring_one))
    high_shape = shape(2, LINES // 2, 128)
    part_shape = shape(4, LINES // 4, 128)
    wide = shape(LOC_C, ROWS, BLK)
    outgoing, matrix = call(
        pack_body,
        [part_shape, wide],
        [high_shape],
        scratch=[
            pltpu.VMEM(high_shape.shape, F32),
            pltpu.VMEM((2, LOC_C, BLK, 128), F32),
            pltpu.VMEM(part_shape.shape, F32),
            pltpu.SemaphoreType.DMA((2,)),
            pltpu.SemaphoreType.DMA((4,)),
        ],
        raw_in=(0,),
        raw_out=(0,),
        size=2**24,
    )(later, lines.reshape(high_shape.shape))
    outgoing, *plane = lax.optimization_barrier((outgoing, *plane))
    arrived = lax.all_to_all(
        outgoing.reshape(N_ROW * N_COL, 32, 128), ("row", "col"), split_axis=0, concat_axis=0, tiled=True
    )
    plane = plane + [lax.ppermute(part, "row", across_core) for part in plane]
    leads = [leads, lax.ppermute(leads, "row", across_core)]

    direct_ins = [matrix, *plane, diag_inverse, *by_rows, *leads]
    split_shape = shape(LOC_C, BLK, 2 * BLK, dtype=BF16)
    square_shape = pltpu.VMEM((BLK, BLK), F32)
    pair_shape = pltpu.VMEM((2, BLK, BLK), F32)
    wide_shape = pltpu.VMEM((LOC_C, BLK, BLK), F32)
    rest, high, low, corners, given = call(
        direct_body,
        [
            shape(2, BLK, BLK), split_shape, split_shape,
            shape(N_CHIP, 64, 128), shape(N_CHIP, 64, 128),
        ],
        direct_ins,
        near=(*range(1, 9), 11, 12, 13, 14, 15),
        limit=50 * 2**20,
        scratch=[wide_shape, wide_shape, pair_shape, pair_shape, square_shape, pltpu.VMEM((3, BLK, BLK), F32)],
        flops=2**33,
        size=2**24,
    )(place, *direct_ins)
    corners = exchange(corners + lax.ppermute(given, "row", across_core))
    arrived = arrived.reshape(N_ROW, N_COL, 32, 128)
    image_ins = [arrived, rest, high, low]
    chunks = call(
        image_body,
        [shape(STRIP, 2 * BLK)] * 4,
        image_ins,
        scratch=[
            wide_shape,
            pltpu.VMEM((ROWS, 2 * BLK), F32),
        ],
        near=(0,),
        limit=VMEM_LIMIT,
        flops=2**32,
        size=2**24,
    )(place, *image_ins)
    strips = [chunks[0]] + [
        lax.ppermute(chunks[d], "col", [(i, (i + d) % 4) for i in range(4)]) for d in range(1, 4)
    ]
    corners, first, *chunks = lax.optimization_barrier((corners, matrix[0], *chunks))
    totals = call(total_body, [shape(64, 128)], [corners], near=(0,), size=2**19)(place, corners)
    strip_ins = [*strips, *totals]
    across, *panels = call(
        strip_body,
        [shape(N_ROW, RSUB, 128)] + [shape(STRIP + 2 * RSUB, BLK)] * 4,
        strip_ins,
        near=(0, 1, 2, 3, 4),
        size=2**21,
    )(place, *strip_ins)
    arrived, across = lax.optimization_barrier((arrived, across))
    across = lax.all_to_all(across, "row", split_axis=0, concat_axis=0, tiled=True)
    panels = to_owners(panels)
    half = half_sum(lines, arrived).reshape(ROWS, 16, 128)
    finish_ins = [half, lines, first, across, *panels]
    (result,) = call(
        finish_body,
        [shape(ROWS, 16, 128)],
        finish_ins,
        scratch=[
            pltpu.VMEM((2, LOC_C, 2, RSUB, 128), F32),
            pltpu.VMEM((ROWS, 8, 128), F32),
            pltpu.VMEM((16, 16, 128), F32),
            pltpu.SemaphoreType.DMA,
            pltpu.SemaphoreType.DMA((2,)),
        ],
        heads={1: 2 * 128},
        near=(3, 5, 6, 7),
        raw_in=(0,),
        raw_out=(0,),
        aliases={1: 0},
        size=2**23,
    )(place, *finish_ins)
    return result.reshape(NBLK, 1, RSUB, LOC_C, 1, BLK)


def solution(mesh):
    return jax.shard_map(
        on_device,
        mesh=mesh,
        in_specs=(
            P(None, "row", None, None, "col", None),
            P(None, None, "col", "row", None, None),
            P(),
        ),
        out_specs=P(None, "row", None, None, "col", None),
        check_vma=False,
    )
```
